32 devices in a mesh: sub: 8 (over z, x), blk: 4 (over y, core).
Axes of the slice: x: 2, y: 2, z: 4, core: 2. Of those that a mesh axis runs over, the one named last changes fastest.
Arguments:
- right_side: float32 [32, 1024, 512], P('sub', 'blk'), may hold values from -8 to 8
- trans_x: float32 [32, 1024, 512], P('sub', 'blk'), may hold values from 0.01 to 10
- trans_y: float32 [32, 1024, 512], P('sub', 'blk'), may hold values from 0.01 to 10
- trans_z: float32 [32, 1024, 512], P('sub', 'blk'), may hold values from 0.01 to 10
- storage: float32 [32, 1024, 512], P('sub', 'blk'), may hold values from 0.05 to 1
- pair_perm: int32 [8, 4, 1024], P('sub', 'blk'), may hold values from 0 to 1023, each once within a row
- pair_type: int32 [8, 4, 1024], P('sub', 'blk'), may hold values from 0 to 3
- pair_count: int32 [8, 4], P('sub', 'blk'), may hold values from 256 to 1024
- proj: float32 [4, 128, 128], replicated, may hold values from -1 to 2, as said below
Outputs:
- solution_field: float32 [32, 1024, 512], P('sub', 'blk')
- residual: float32 [32, 1024, 512], P('sub', 'blk')
The draws below stay inside these ranges and needn't reach their ends.
Inputs may be any that keep to these rules, and one draw needn't show every extreme that they name: `pair_perm`: each subdomain's list is a permutation of its face blocks. `proj`: projection matrices of order one.
All inputs are finite; a program needn't handle non-finite values.
Results may differ from the reference program's by a relative error of at most 0.00013.
Values sent between devices are 32-bit elements; how exact they have to be, the bound alone decides.
No kernel may reach another device: no remote copies, remote signals or barrier semaphores. Data moves between devices by JAX's collectives and lax.ppermute only.
A program may use at most 128 MiB of HBM per device.

```python
import math
import jax
import jax.numpy as jnp
from jax import lax

CX = 4
CY = 256
CZ = 512
FB = 128
NPROJ = 4
ITERS = 2
NFB = 1024
NX = 32
NY = 1024
NZ = 512
N_SUB = 8
N_BLK = 4


def draw_proj(key, part):
    key = jax.random.fold_in(key, 7)
    noise = jax.random.normal(key, (NPROJ, FB, FB), jnp.float32)
    noise = jnp.clip(noise, -5.0, 5.0)
    return jnp.eye(FB, dtype=jnp.float32)[None] + 0.4 / FB ** 0.5 * noise


def plant(entries, own_key, low, top_value):
    longest = entries.shape.index(max(entries.shape))
    spots = []
    for shift in (0, 1):
        where = [jax.random.randint(jax.random.fold_in(own_key, axis), (), 0, length) for axis, length in enumerate(entries.shape)]
        where[longest] = (where[longest] + shift) % entries.shape[longest]
        spots.append(tuple(where))
    return entries.at[spots[0]].set(low).at[spots[1]].set(top_value)


def block_levels(rng, extent, pieces, smallest, top_value):
    def one(position, blocks):
        steps = jax.random.uniform(jax.random.fold_in(jax.random.fold_in(rng, 6), position), (blocks,), jnp.float32, smallest / len(pieces), top_value / len(pieces))
        return jnp.repeat(jnp.exp(steps), extent[position] // blocks).reshape((-1,) + (1,) * (len(extent) - position - 1))

    loudness = one(*pieces[0])
    for cut in pieces[1:]:
        loudness = loudness * one(*cut)
    return loudness


def bell_draw(key, dims, scale, most, shards=(), held_as=jnp.bfloat16):
    entries = jax.random.normal(key, dims, jnp.float32) * scale
    if len(shards) > 0:
        entries = block_levels(key, dims, shards, -0.22, 0.18) * entries
    return jnp.clip(entries, min=-most, max=most).astype(held_as)


def setup_inputs(seed: int = 0) -> dict:
    keys = jax.random.split(jax.random.key(seed), 10)
    return {
        "right_side": bell_draw(keys[0], (NX, NY, NZ), 1.0, 8.0, ((0, 8), (1, 4)), jnp.float32),
        "trans_x": jnp.clip(jnp.exp(math.log(10.0) - 6.9077553 * jax.random.uniform(keys[1], (NX, NY, NZ), jnp.float32) ** block_levels(keys[1], (NX, NY, NZ), ((0, 8), (1, 4)), -0.2, 0.2)), 0.01, 10.0),
        "trans_y": jnp.clip(jnp.exp(math.log(10.0) - 6.9077553 * jax.random.uniform(keys[2], (NX, NY, NZ), jnp.float32) ** block_levels(keys[2], (NX, NY, NZ), ((0, 8), (1, 4)), -0.2, 0.2)), 0.01, 10.0),
        "trans_z": jnp.clip(jnp.exp(math.log(10.0) - 6.9077553 * jax.random.uniform(keys[3], (NX, NY, NZ), jnp.float32) ** block_levels(keys[3], (NX, NY, NZ), ((0, 8), (1, 4)), -0.2, 0.2)), 0.01, 10.0),
        "storage": jnp.clip(jnp.exp(math.log(1.0) - 2.9957323 * jax.random.uniform(keys[4], (NX, NY, NZ), jnp.float32) ** block_levels(keys[4], (NX, NY, NZ), ((0, 8), (1, 4)), -0.2, 0.2)), 0.05, 1.0),
        "pair_perm": jax.vmap(lambda own: jax.random.permutation(own, NFB))(jax.random.split(keys[5], N_SUB * N_BLK)).reshape((N_SUB, N_BLK, NFB)).astype(jnp.int32),
        "pair_type": plant(jax.random.randint(keys[6], (N_SUB, N_BLK, NFB), 0, NPROJ), jax.random.fold_in(keys[6], 1), 0, NPROJ - 1).astype(jnp.int32),
        "pair_count": plant(jax.random.randint(keys[7], (N_SUB, N_BLK), NFB // 4, NFB + 1), jax.random.fold_in(keys[7], 1), NFB // 4, NFB).astype(jnp.int32),
        "proj": draw_proj(jax.random.fold_in(keys[9], 71), 0),
    }


penalty = 4.0


def shift_next(values, axis):
    count = values.shape[axis]
    rest = lax.slice_in_dim(values, 1, count, axis=axis)
    return jnp.concatenate([rest, jnp.zeros_like(lax.slice_in_dim(values, 0, 1, axis=axis))], axis)


def shift_prev(values, axis):
    count = values.shape[axis]
    rest = lax.slice_in_dim(values, 0, count - 1, axis=axis)
    return jnp.concatenate([jnp.zeros_like(lax.slice_in_dim(values, 0, 1, axis=axis)), rest], axis)


def operate(field, coeffs, storage, pair_perm, pair_type, live, proj):
    result = storage * field
    for axis in range(3):
        coeff = coeffs[axis]
        result = result + coeff * (field - shift_next(field, axis)) + shift_prev(coeff, axis) * (field - shift_prev(field, axis))
    view = field.reshape(N_SUB, CX, N_BLK, CY, CZ)
    last = view[:, CX - 1].reshape(N_SUB, N_BLK, NFB, FB)
    first = view[:, 0].reshape(N_SUB, N_BLK, NFB, FB)
    right = jnp.concatenate([first[1:], jnp.zeros_like(first[:1])], 0)
    gathered = jnp.take_along_axis(right, pair_perm[..., None], axis=2)
    projected = jnp.zeros_like(last)
    for kind in range(NPROJ):
        select = (pair_type == kind).astype(jnp.float32)[..., None]
        projected = projected + select * jnp.einsum("sbkc,ac->sbka", gathered, proj[kind], precision=lax.Precision.HIGHEST)
    jump = live[..., None] * (last - projected)
    back = jnp.zeros_like(last)
    for kind in range(NPROJ):
        select = (pair_type == kind).astype(jnp.float32)[..., None]
        back = back + select * jnp.einsum("sbka,ac->sbkc", jump, proj[kind], precision=lax.Precision.HIGHEST)
    back = -penalty * back
    sub_index = jnp.arange(N_SUB, dtype=jnp.int32)[:, None, None]
    blk_index = jnp.arange(N_BLK, dtype=jnp.int32)[None, :, None]
    ordered = jnp.zeros_like(back).at[sub_index, blk_index, pair_perm].set(back)
    received = jnp.concatenate([jnp.zeros_like(ordered[:1]), ordered[:-1]], 0)
    extra = jnp.zeros((N_SUB, CX, N_BLK, CY, CZ), jnp.float32)
    extra = extra.at[:, CX - 1].add((penalty * jump).reshape(N_SUB, N_BLK, CY, CZ))
    extra = extra.at[:, 0].add(received.reshape(N_SUB, N_BLK, CY, CZ))
    return result + extra.reshape(NX, NY, NZ)


def reference(right_side, trans_x, trans_y, trans_z, storage, pair_perm, pair_type, pair_count, proj):
    x_index = jnp.arange(NX, dtype=jnp.int32)[:, None, None]
    y_index = jnp.arange(NY, dtype=jnp.int32)[None, :, None]
    z_index = jnp.arange(NZ, dtype=jnp.int32)[None, None, :]
    tx = trans_x * (x_index % CX != CX - 1).astype(jnp.float32)
    ty = trans_y * (y_index != NY - 1).astype(jnp.float32)
    tz = trans_z * (z_index != NZ - 1).astype(jnp.float32)
    coeffs = (tx, ty, tz)
    live = (jnp.arange(NFB, dtype=jnp.int32)[None, None, :] < pair_count[..., None]).astype(jnp.float32)
    solution_field = jnp.zeros_like(right_side)
    residual, direction = right_side, right_side
    norm_now = jnp.sum(residual * residual)
    for step in range(ITERS):
        image = operate(direction, coeffs, storage, pair_perm, pair_type, live, proj)
        alpha = norm_now / jnp.sum(direction * image)
        solution_field = solution_field + alpha * direction
        residual = residual - alpha * image
        norm_next = jnp.sum(residual * residual)
        direction = residual + (norm_next / norm_now) * direction
        norm_now = norm_next
    return solution_field, residual
```

```python
import jax
import jax.numpy as jnp
from jax import lax
from jax.experimental import pallas as pl
from jax.experimental.pallas import tpu as pltpu
from jax.sharding import PartitionSpec as P

ROWS = 32
FIELDS = 16
SUB = 8
LANES = 128
F32 = jnp.float32
BF16 = jnp.bfloat16
penalty = 4.0


def tile_ids(dim, shape):
    return lax.broadcasted_iota(jnp.int32, shape, dim)


def as_tile(scalars):
    lane = tile_ids(1, (SUB, LANES))
    tile = jnp.zeros((SUB, LANES), F32)
    for place, value in enumerate(scalars):
        tile = jnp.where(lane == place, value, tile)
    return tile


def from_tile(tile, place):
    pick = (tile_ids(1, tile.shape) == place) & (tile_ids(0, tile.shape) == 0)
    return jnp.sum(jnp.where(pick, tile, 0.0))


def at(array, layers, start):
    return [array[layer, pl.ds(start, SUB), :] for layer in range(layers)]


def stencil(values, after, tx, ty, tz, st, carry, below=None, above=None):
    shape = values[0].shape
    row = tile_ids(0, shape)
    last_z = tile_ids(1, shape) == shape[1] - 1
    results, carries = [], []
    flux_x = None if below is None else below[1] * (below[0] - values[0])
    for layer, value in enumerate(values):
        follow = value if after is None else pltpu.roll(after[layer], SUB - 1, 0)
        follow = jnp.where(row == SUB - 1, follow, pltpu.roll(value, SUB - 1, 0))
        flux_y = ty[layer] * (value - follow)
        rolled = pltpu.roll(flux_y, 1, 0)
        carries.append(rolled)
        flux_z = jnp.where(last_z, 0.0, tz[layer] * (value - pltpu.roll(value, shape[1] - 1, 1)))
        result = st[layer] * value + (flux_y - jnp.where(row == 0, carry[layer], rolled))
        result = result + (flux_z - pltpu.roll(flux_z, 1, 1))
        if flux_x is not None:
            result = result - flux_x
        next_x = values[layer + 1] if layer < len(values) - 1 else above
        flux_x = None
        if next_x is not None:
            flux_x = tx[layer] * (value - next_x)
            result = result + flux_x
        results.append(result)
    return results, carries


def at_last_block():
    return lax.axis_index("blk") == lax.axis_size("blk") - 1


def edge_terms(before, first, last, beyond, ty_before, ty_last):
    low = ty_before * (first - before)
    high = jnp.where(at_last_block(), 0.0, ty_last * (last - beyond))
    return low, high


def pack_kernel(b_hbm, ty_hbm, face, sems):
    rows = b_hbm.shape[1]
    copies = [
        pltpu.make_async_copy(b_hbm.at[0], face.at[pl.ds(0, rows), :], sems.at[0]),
        pltpu.make_async_copy(ty_hbm.at[0, pl.ds(rows - SUB, SUB), :], face.at[pl.ds(rows, SUB), :], sems.at[1]),
    ]
    for copy in copies:
        copy.start()
    for copy in copies:
        copy.wait()


def two_parts(array):
    high = array.astype(BF16)
    return high, (array - high.astype(F32)).astype(BF16)


def prepare_pairs(perm, kind, count, proj, rows, groups, picks, puts, codes, proj_t, proj_n):
    kinds, width, _ = proj.shape
    blocks = rows * groups
    lane = tile_ids(1, (1, blocks))
    target = lax.rem(perm, groups) * rows + lax.div(perm, groups)
    shift = kinds.bit_length()
    keys = (target * (1 << shift) + jnp.where(lane < count, kind, kinds)).astype(F32)
    span = LANES // groups
    spread = tile_ids(1, (span, LANES)) - groups * tile_ids(0, (span, LANES))
    lanes = tile_ids(1, (rows, LANES))
    across = []
    for group in range(groups):
        column = jnp.concatenate(
            [
                jnp.sum(jnp.where(spread == group, keys[:, place * LANES : (place + 1) * LANES], 0.0), 1, keepdims=True)
                for place in range(blocks // LANES)
            ],
            axis=0,
        ).astype(jnp.int32)
        column = jnp.broadcast_to(column, (rows, LANES))
        here = pl.ds(group * rows, rows)
        codes[here, :] = column & ((1 << shift) - 1)
        column = column >> shift
        for place in range(blocks // LANES):
            picks[here, pl.ds(place * LANES, LANES)] = jnp.where(column == lanes + place * LANES, 1.0, 0.0).astype(BF16)
        for place in range(rows // LANES):
            turned = jnp.transpose(column[place * LANES : (place + 1) * LANES].astype(F32))
            across.append(turned[0:1, :].astype(jnp.int32))
    across = jnp.concatenate(across, axis=1)
    down = tile_ids(0, (rows, blocks))
    for group in range(groups):
        puts[pl.ds(group * rows, rows), :] = jnp.where(across == down + group * rows, 1.0, 0.0).astype(BF16)
    for kind in range(kinds):
        here = pl.ds(kind * width, width)
        proj_t[here, :] = jnp.concatenate(two_parts(jnp.transpose(proj[kind])), axis=1)
        proj_n[here, :] = jnp.concatenate(two_parts(proj[kind]), axis=1)


def first_kernel(
    count, perm, kind, proj, b_hbm, tx_hbm, ty_hbm, tz_hbm, st_hbm,
    b, tx, ty, tz, st, face_next, s_first, s_mid, s_last, sums, picks, puts, codes, proj_t, proj_n, total, sems,
):
    layers, rows, depth = b.shape
    steps = rows // ROWS
    sources, targets = (b_hbm, tx_hbm, ty_hbm, tz_hbm, st_hbm), (b, tx, ty, tz, st)

    def copy(which, step):
        part = pl.ds(step * ROWS, ROWS)
        return pltpu.make_async_copy(
            sources[which].at[:, part, :], targets[which].at[:, part, :], sems.at[which, step]
        )

    for step in range(steps):
        for which in range(len(sources)):
            copy(which, step).start()
    width = proj.shape[1]
    prepare_pairs(
        perm[0], kind[0], count[0, 0], proj, rows, depth // width, picks, puts, codes, proj_t, proj_n
    )
    total[...] = jnp.zeros_like(total)
    copy(0, 0).wait()

    def chunk(start, after, carry):
        values = at(b, layers, start)
        results, carry = stencil(values, after, *[at(array, layers, start) for array in (tx, ty, tz, st)], carry)
        here = pl.ds(start, SUB)
        squares, products = values[0] * values[0], values[0] * results[0]
        for layer in range(1, layers):
            squares = squares + values[layer] * values[layer]
            products = products + values[layer] * results[layer]
        total[0] += squares
        total[1] += products
        face_next[here, :] = results[0]
        s_first[here, :] = results[0]
        for layer in range(1, layers - 1):
            s_mid[layer - 1, here, :] = results[layer]
        s_last[here, :] = results[layers - 1]
        return carry

    carry = [jnp.zeros((SUB, depth), F32)] * layers
    for step in range(steps):
        for which in range(1, len(sources)):
            copy(which, step).wait()
        if step < steps - 1:
            copy(0, step + 1).wait()
        for start in range(step * ROWS, (step + 1) * ROWS, SUB):
            carry = chunk(start, None if start == rows - SUB else at(b, layers, start + SUB), carry)
    sums[...] = as_tile([jnp.sum(total[0]), jnp.sum(total[1])])


def up_places(layers):
    return 0, layers, 2 * layers, 3 * layers, 3 * layers + 1, 3 * layers + 2


def edge_kernel(
    sums_in, b, ty, right, up, down, s_first_in, s_mid_in, s_last_in, w_last_in, back_in,
    s_first, s_mid, s_last, w_last, back, sums, right_edges, w_up, w_down,
):
    layers, rows, _ = b.shape
    at_b, at_ty, at_w, at_back, at_right, at_right_ty = up_places(layers)
    product = 0.0
    for layer in range(layers):
        first, last = b[layer, 0:1, :], b[layer, rows - 1 :, :]
        low, high = edge_terms(
            up[at_b + layer : at_b + layer + 1, :], first, last, down[layer : layer + 1, :],
            up[at_ty + layer : at_ty + layer + 1, :], ty[layer, rows - 1 :, :],
        )
        pairs = [(s_first_in, s_first)] if layer == 0 else [(s_last_in, s_last), (w_last_in, w_last)]
        if 0 < layer < layers - 1:
            pairs = [(s_mid_in.at[layer - 1], s_mid.at[layer - 1])]
        for source, target in pairs:
            target[0:1, :] = source[0:1, :] + low
            target[rows - 1 :, :] = source[rows - 1 :, :] + high
        product = product + first * low + last * high
        w_up[layer : layer + 1, :] = up[at_w + layer : at_w + layer + 1, :] - low
        w_down[layer : layer + 1, :] = down[layers + layer : layers + layer + 1, :] - high
    sums[...] = sums_in[...] + as_tile([0.0, jnp.sum(product)])
    back[rows : rows + 1, :] = up[at_back : at_back + 1, :]
    back[rows + 1 : rows + 2, :] = down[2 * layers : 2 * layers + 1, :]
    low, high = edge_terms(
        up[at_right : at_right + 1, :], right[0:1, :], right[rows - 1 : rows, :], down[2 * layers + 1 :, :],
        up[at_right_ty : at_right_ty + 1, :], right[rows + SUB - 1 :, :],
    )
    right_edges[0:1, :] = low
    right_edges[1:2, :] = high


def mm(left, right):
    return lax.dot_general(left, right, (((1,), (0,)), ((), ())), preferred_element_type=F32)


def by_kind(codes, array, kinds):
    zero = jnp.zeros_like(array)
    return jnp.concatenate([jnp.where(codes == kind, array, zero) for kind in range(kinds)], axis=1)


def apply_proj(codes, high, low, proj, kinds, width):
    both = mm(by_kind(codes, high, kinds), proj[...])
    return both[:, :width] + both[:, width:] + mm(by_kind(codes, low, kinds), proj[:, :width])


def take_jump(group, faces, last, picks, codes_col, proj_t):
    width = proj_t.shape[1] // 2
    kinds = proj_t.shape[0] // width
    here = pl.ds(group * last.shape[0], last.shape[0])
    codes = codes_col[here, :]
    taken = mm(picks[here, :], faces)
    projected = apply_proj(codes, taken[:, :width].astype(BF16), taken[:, width:].astype(BF16), proj_t, kinds, width)
    return jnp.where(codes < kinds, last - projected, 0.0)


def turn_back(group, jump, codes_col, proj_n):
    width = proj_n.shape[1] // 2
    kinds = proj_n.shape[0] // width
    scale = jnp.where(lax.axis_index("sub") < lax.axis_size("sub") - 1, -penalty, 0.0)
    codes = codes_col[pl.ds(group * jump.shape[0], jump.shape[0]), :]
    return jnp.concatenate(two_parts(scale * apply_proj(codes, *two_parts(jump), proj_n, kinds, width)), axis=1)


def put_back(group, backs, puts, rows):
    width = backs.shape[1] // 2
    placed = mm(puts[pl.ds(group * rows, rows), :], backs)
    return placed[:, :width] + placed[:, width:]


def stack_parts(parts):
    return jnp.concatenate(two_parts(jnp.concatenate(parts, axis=0)), axis=1)


def jump_first_kernel(b, right, s_last, picks, codes, proj_t, w_last, jump_face, sums):
    width = proj_t.shape[1] // 2
    layers, rows, depth = b.shape
    parts = [pl.ds(group * width, width) for group in range(depth // width)]
    faces = stack_parts([right[:rows, part] for part in parts])
    square = jnp.zeros((rows, width), F32)
    for group, part in enumerate(parts):
        jump = take_jump(group, faces, b[layers - 1, :, part], picks, codes, proj_t)
        square = square + jump * jump
        jump_face[:, part] = jump
        w_last[:, part] = s_last[:, part] + penalty * jump
    sums[...] = as_tile([jnp.sum(square)])


def back_first_kernel(jump, right, b, ty, s_first, s_mid, w_last, puts, codes, proj_n, back, up, down):
    back_kernel(jump, puts, codes, proj_n, back)
    layers, rows, _ = b.shape
    at_b, at_ty, at_w, at_back, at_right, at_right_ty = up_places(layers)
    end = pl.ds(rows - 1, 1)
    back[rows:, :] = jnp.zeros((SUB, back.shape[1]), F32)
    for layer in range(layers):
        image = s_first if layer == 0 else w_last if layer == layers - 1 else s_mid.at[layer - 1]
        up[at_b + layer : at_b + layer + 1, :] = b[layer, end, :]
        up[at_ty + layer : at_ty + layer + 1, :] = ty[layer, end, :]
        up[at_w + layer : at_w + layer + 1, :] = image[end, :]
        down[layer : layer + 1, :] = b[layer, 0:1, :]
        down[layers + layer : layers + layer + 1, :] = image[0:1, :]
    up[at_back : at_back + 1, :] = back[end, :]
    up[at_right : at_right + 1, :] = right[end, :]
    up[at_right_ty : at_right_ty + 1, :] = right[rows + SUB - 1 :, :]
    down[2 * layers : 2 * layers + 1, :] = back[0:1, :]
    down[2 * layers + 1 : 2 * layers + 2, :] = right[0:1, :]


def jump_second_kernel(
    near_sums, w_last, jump, right, right_edges, back_before, picks, codes, proj_t, jump_next, sums, field
):
    width = proj_t.shape[1] // 2
    rows, depth = right.shape
    parts = [pl.ds(group * width, width) for group in range(depth // width)]
    near = from_tile(near_sums[...], 2)
    field[...] = right[...] + back_before[:rows, :]
    field[0:1, :] += right_edges[0:1, :]
    field[rows - 1 :, :] += right_edges[1:2, :]
    faces = stack_parts([field[:, part] for part in parts])
    totals = [jnp.zeros((rows, width), F32)] * 3
    for group, part in enumerate(parts):
        later = take_jump(group, faces, w_last[:, part], picks, codes, proj_t)
        jump_next[:, part] = later
        close = jump[:, part] - near * later
        totals = [total + new for total, new in zip(totals, (close * close, close * later, later * later))]
    found = [jnp.sum(total) for total in totals]
    sums[...] = as_tile([0.0] * 6 + [penalty * found[0], 2.0 * penalty * found[1], penalty * found[2]])


def back_kernel(jump_next, puts, codes, proj_n, back):
    width = proj_n.shape[1] // 2
    rows, depth = jump_next.shape
    parts = [pl.ds(group * width, width) for group in range(depth // width)]
    backs = [turn_back(group, jump_next[:, part], codes, proj_n) for group, part in enumerate(parts)]
    backs = jnp.concatenate(backs, axis=0)
    for group, part in enumerate(parts):
        back[:rows, part] = put_back(group, backs, puts, rows)


def stencil_sums(read, own, near, b, plain, tx, ty, tz, st, image, total):
    layers, rows, depth = b.shape
    first, last = own[0], own[-1]
    total[...] = jnp.zeros_like(total)

    def chunk(start, values, after, carry):
        here = pl.ds(start, SUB)
        below = (values[0], tx[first - 1, here, :]) if first > 0 else None
        above = values[-1] if last < layers - 1 else None
        skip = 0 if below is None else 1
        mine = values[skip : skip + len(own)]
        results, carry = stencil(
            mine, None if after is None else after[skip : skip + len(own)],
            *[[array[layer, here, :] for layer in own] for array in (tx, ty, tz, st)], carry, below, above,
        )
        terms = None
        for place, layer in enumerate(own):
            w, s = mine[place], results[place]
            image[place, here, :] = s
            u = b[layer, here, :] - near * w
            q = plain(layer, here) - near * s
            new = [u * u, u * w, w * w, u * q, u * s + w * q, w * s]
            terms = new if terms is None else [old + more for old, more in zip(terms, new)]
        return terms, carry

    def several(start, count, carry, at_end=False):
        values = [read(pl.multiple_of(start + SUB * place, SUB)) for place in range(count)]
        values.append(None if at_end else read(pl.multiple_of(start + SUB * count, SUB)))
        terms = None
        for place in range(count):
            new, carry = chunk(pl.multiple_of(start + SUB * place, SUB), values[place], values[place + 1], carry)
            terms = new if terms is None else [old + more for old, more in zip(terms, new)]
        for place, term in enumerate(terms):
            total[place] += term
        return carry

    group = 2
    carry = lax.fori_loop(
        0, rows // (group * SUB) - 1,
        lambda index, carry: tuple(several(pl.multiple_of(index * group * SUB, SUB), group, list(carry))),
        (jnp.zeros((SUB, depth), F32),) * len(own),
    )
    several(rows - group * SUB, group, list(carry), True)
    return [jnp.sum(total[place]) for place in range(total.shape[0])]


def second_high_kernel(first_sums, jump_sums, b, s_mid, s_last, w_last, tx, ty, tz, st, image, sums, total):
    layers = b.shape[0]
    split = layers // 2
    norm = from_tile(first_sums[...], 0)
    energy = from_tile(first_sums[...], 1) + penalty * from_tile(jump_sums[...], 0)
    safe = energy > 0.01 * norm
    ratio = jnp.full((SUB, LANES), norm, F32) / jnp.full((SUB, LANES), jnp.where(safe, energy, 1.0), F32)
    near = jnp.where(safe, jnp.max(ratio), 0.0)

    def read(start):
        here = pl.ds(start, SUB)
        return [s_mid[layer - 1, here, :] for layer in range(split - 1, layers - 1)] + [w_last[here, :]]

    def plain(layer, here):
        return s_last[here, :] if layer == layers - 1 else s_mid[layer - 1, here, :]

    found = stencil_sums(read, list(range(split, layers)), near, b, plain, tx, ty, tz, st, image, total)
    sums[...] = as_tile([norm, energy, near] + found)


def second_low_kernel(
    high_sums, jump_sums, b, s_first, s_mid, w_last, recv, w_up, w_down, up, tx, ty, tz, st,
    image, edge_high, table, total,
):
    layers, rows, depth = b.shape
    split = layers // 2
    near = from_tile(high_sums[...], 2)

    def read(start):
        here = pl.ds(start, SUB)
        return [s_first[here, :] + recv[here, :]] + [s_mid[layer - 1, here, :] for layer in range(1, split + 1)]

    def plain(layer, here):
        return s_first[here, :] if layer == 0 else s_mid[layer - 1, here, :]

    found = stencil_sums(read, list(range(split)), near, b, plain, tx, ty, tz, st, image, total)

    def row(layer, place):
        here = pl.ds(place, 1)
        if layer == 0:
            return s_first[here, :] + recv[here, :]
        return w_last[here, :] if layer == layers - 1 else s_mid[layer - 1, here, :]

    extra = [0.0] * 3
    for layer in range(layers):
        before, beyond = w_up[layer : layer + 1, :], w_down[layer : layer + 1, :]
        if layer == 0:
            before, beyond = before + recv[rows : rows + 1, :], beyond + recv[rows + 1 : rows + 2, :]
        ends = row(layer, 0), row(layer, rows - 1)
        added = edge_terms(
            before, *ends, beyond, up[layers + layer : layers + layer + 1, :], ty[layer, rows - 1 :, :]
        )
        for side, (place, w, s) in enumerate(zip((0, rows - 1), ends, added)):
            u = b[layer, place : place + 1, :] - near * w
            new = [-near * u * s, u * s - near * w * s, w * s]
            extra = [old + more for old, more in zip(extra, new)]
            if layer < split:
                image[layer, place : place + 1, :] += s
            else:
                spot = side * (layers - split) + layer - split
                edge_high[spot : spot + 1, :] = s
    extra = [jnp.sum(value) for value in extra]
    sums = high_sums[...] + jump_sums[...] + as_tile([0.0] * 3 + found) + as_tile([0.0] * 6 + extra)
    mine = lax.axis_index("sub") * lax.axis_size("blk") + lax.axis_index("blk")
    device = tile_ids(0, table.shape) * (LANES // FIELDS) + lax.div(tile_ids(1, table.shape), FIELDS)
    field = lax.rem(tile_ids(1, table.shape), FIELDS)
    filled = jnp.zeros(table.shape, F32)
    for place in range(9):
        filled = jnp.where((device == mine) & (field == place), jnp.sum(sums[0:1, place : place + 1]), filled)
    table[...] = filled


def final_kernel(
    tables, b, s_first, s_mid, w_last, recv, image_low, image_high, edge_high, jump_next, recv_next, solution_hbm, residual_hbm,
    solution, residual, sems,
):
    layers, rows, depth = b.shape
    split = image_low.shape[0]
    flat = tables[...]
    norm, energy, near, uu, uw, ww, uq, cross, wq = [
        flat if place == 0 else pltpu.roll(flat, LANES - place, 1) for place in range(9)
    ]
    own = lax.rem(tile_ids(1, flat.shape), FIELDS) == 0

    def whole(array):
        array = jnp.sum(jnp.where(own, array, 0.0), axis=0, keepdims=True)
        return jnp.sum(array, axis=1, keepdims=True)

    norm, energy = whole(norm), whole(energy)
    alpha = norm / energy
    away = alpha - near
    norm_next = whole(uu - away * (2.0 * uw - away * ww))
    energy_next = whole(uq - away * (cross - away * wq))
    beta = norm_next / norm
    step_size = norm_next / (energy_next - beta * norm_next / alpha)
    c0 = jnp.broadcast_to(alpha + step_size * beta + step_size, (SUB, depth))
    c1 = jnp.broadcast_to(step_size * alpha, (SUB, depth))
    c2 = jnp.broadcast_to(alpha + step_size * (1.0 + beta), (SUB, depth))

    def copy(which, step):
        part = pl.ds(step * ROWS, ROWS)
        source, target = ((solution, solution_hbm), (residual, residual_hbm))[which]
        return pltpu.make_async_copy(source.at[:, part, :], target.at[:, part, :], sems.at[which, step])

    for step in range(rows // ROWS):

        def one(index, done):
            here = pl.ds(pl.multiple_of(step * ROWS + index * SUB, SUB), SUB)
            for layer in range(layers):
                v = b[layer, here, :]
                s = image_low[layer, here, :] if layer < split else image_high[layer - split, here, :]
                if layer == 0:
                    w = s_first[here, :] + recv[here, :]
                    s = s + recv_next[here, :]
                elif layer < layers - 1:
                    w = s_mid[layer - 1, here, :]
                else:
                    w = w_last[here, :]
                    s = s + penalty * jump_next[here, :]
                solution[layer, here, :] = c0 * v - c1 * w
                residual[layer, here, :] = v - c2 * w + c1 * s
            return done

        lax.fori_loop(0, ROWS // SUB, one, 0, unroll=True)
        for side, last_step in enumerate((0, rows // ROWS - 1)):
            if step == last_step:
                place = side * (rows - 1)
                for layer in range(split, layers):
                    spot = side * (layers - split) + layer - split
                    residual[layer, place : place + 1, :] += c1[0:1, :] * edge_high[spot : spot + 1, :]
        for which in range(2):
            copy(which, step).start()
    for step in range(rows // ROWS):
        for which in range(2):
            copy(which, step).wait()


SMEM = pl.BlockSpec(memory_space=pltpu.SMEM)
VMEM = pl.BlockSpec(memory_space=pltpu.VMEM)
HBM = pl.BlockSpec(memory_space=pltpu.HBM)


def held(*dims, dtype=F32):
    return pltpu.VMEM(dims, dtype)


def near_core(*arrays):
    return [pltpu.with_memory_space_constraint(array, pltpu.VMEM) for array in arrays]


def in_hbm(*arrays):
    return [pltpu.with_memory_space_constraint(array, pltpu.HBM) for array in arrays]


def params(mib):
    return pltpu.CompilerParams(vmem_limit_bytes=mib * 1024 * 1024)


def shifted(array, axis, by):
    size = lax.axis_size(axis)
    return lax.ppermute(array, axis, [(i, i + by) for i in range(size) if 0 <= i + by < size])


def gather_rows(table):
    for axis in ("blk", "sub"):
        size = lax.axis_size(axis)
        reach = 1 if axis == "blk" else size // 2
        while 0 < reach < size:
            table = table + lax.ppermute(table, axis, [(i, i ^ reach) for i in range(size)])
            reach = reach * 2 if axis == "blk" else reach // 2
    return table


def body(right_side, trans_x, trans_y, trans_z, storage, pair_perm, pair_type, pair_count, proj):
    layers, rows, depth = right_side.shape
    blocks, width, kinds = pair_perm.shape[2], proj.shape[1], proj.shape[0]
    subs, blks = lax.axis_size("sub"), lax.axis_size("blk")
    steps = rows // ROWS
    cells = layers * rows * depth
    cost = lambda flops, size: pl.CostEstimate(flops=int(flops), bytes_accessed=int(size), transcendentals=0)

    (face,) = pl.pallas_call(
        pack_kernel,
        in_specs=[HBM, HBM],
        out_specs=[VMEM],
        out_shape=[held(rows + SUB, depth)],
        scratch_shapes=[pltpu.SemaphoreType.DMA((2,))],
        compiler_params=params(2),
        cost_estimate=cost(0, 4 * rows * depth),
        name="pack",
    )(*in_hbm(right_side, trans_y))
    face_right = shifted(face, "sub", -1)

    b, tx, ty, tz, st, face_next, s_first, s_mid, s_last, first_sums, picks, puts, codes, proj_t, proj_n = pl.pallas_call(
        first_kernel,
        in_specs=[SMEM] + [VMEM] * 3 + [HBM] * 5,
        out_specs=[VMEM] * 15,
        out_shape=[held(layers, rows, depth)] * 5
        + [
            held(rows, depth), held(rows, depth), held(layers - 2, rows, depth), held(rows, depth), held(SUB, LANES),
            held(blocks, blocks, dtype=BF16), held(blocks, blocks, dtype=BF16), held(blocks, width, dtype=jnp.int32),
            held(kinds * width, 2 * width, dtype=BF16), held(kinds * width, 2 * width, dtype=BF16),
        ],
        scratch_shapes=[pltpu.VMEM((2, SUB, depth), F32), pltpu.SemaphoreType.DMA((5, steps))],
        compiler_params=params(16),
        cost_estimate=cost(20 * cells, 24 * cells),
        name="stencil_first",
    )(
        pair_count, pair_perm, pair_type, proj,
        *in_hbm(right_side, trans_x, trans_y, trans_z, storage),
    )
    face_right_next = shifted(face_next, "sub", -1)

    mortar_cost = cost(4 * blocks * blocks * width + 6 * kinds * blocks * width * width, 14 * rows * depth)
    w_last, jump, jump_sums = pl.pallas_call(
        jump_first_kernel,
        in_specs=[VMEM] * 6,
        out_specs=[VMEM] * 3,
        out_shape=[held(rows, depth), held(rows, depth), held(SUB, LANES)],
        compiler_params=params(16),
        cost_estimate=mortar_cost,
        name="jump_first",
    )(*near_core(b, face_right, s_last, picks, codes, proj_t))
    back, up_out, down_out = pl.pallas_call(
        back_first_kernel,
        in_specs=[VMEM] * 10,
        out_specs=[VMEM] * 3,
        out_shape=[held(rows + SUB, depth), held(3 * layers + 3, depth), held(2 * layers + 2, depth)],
        compiler_params=params(16),
        cost_estimate=mortar_cost,
        name="back_first",
    )(*near_core(jump, face_right, b, ty, s_first, s_mid, w_last, puts, codes, proj_n))
    up = shifted(up_out, "blk", 1)
    down = shifted(down_out, "blk", -1)
    s_first, s_mid, s_last, w_last, back, first_sums, right_edges, w_up, w_down = pl.pallas_call(
        edge_kernel,
        in_specs=[VMEM] * 11,
        out_specs=[VMEM] * 9,
        out_shape=[held(rows, depth), held(layers - 2, rows, depth), held(rows, depth), held(rows, depth)]
        + [held(rows + SUB, depth), held(SUB, LANES), held(2, depth), held(layers, depth), held(layers, depth)],
        input_output_aliases={6: 0, 7: 1, 8: 2, 9: 3, 10: 4},
        compiler_params=params(2),
        cost_estimate=cost(32 * depth, 64 * depth),
        name="edges_first",
    )(*near_core(first_sums, b, ty, face_right, up, down, s_first, s_mid, s_last, w_last, back))
    recv = shifted(back, "sub", 1)

    split = layers // 2
    image_high, high_sums = pl.pallas_call(
        second_high_kernel,
        in_specs=[VMEM] * 10,
        out_specs=[VMEM] * 2,
        out_shape=[held(layers - split, rows, depth), held(SUB, LANES)],
        scratch_shapes=[pltpu.VMEM((6, SUB, depth), F32)],
        compiler_params=params(8),
        cost_estimate=cost(20 * cells, 15 * cells),
        name="stencil_second_high",
    )(*near_core(first_sums, jump_sums, b, s_mid, s_last, w_last, tx, ty, tz, st))

    jump_next, second_sums = pl.pallas_call(
        jump_second_kernel,
        in_specs=[VMEM] * 9,
        out_specs=[VMEM] * 2,
        out_shape=[held(rows, depth), held(SUB, LANES)],
        scratch_shapes=[pltpu.VMEM((rows, depth), F32)],
        compiler_params=params(16),
        cost_estimate=mortar_cost,
        name="jump_second",
    )(*near_core(high_sums, w_last, jump, face_right_next, right_edges, back, picks, codes, proj_t))

    count = subs * blks
    image_low, edge_high, table = pl.pallas_call(
        second_low_kernel,
        in_specs=[VMEM] * 14,
        out_specs=[VMEM] * 3,
        out_shape=[held(split, rows, depth), held(2 * (layers - split), depth), held(-(-count * FIELDS // LANES), LANES)],
        scratch_shapes=[pltpu.VMEM((6, SUB, depth), F32)],
        compiler_params=params(8),
        cost_estimate=cost(20 * cells, 15 * cells),
        name="stencil_second_low",
    )(
        *near_core(
            high_sums, second_sums, b, s_first, s_mid, w_last, recv, w_up, w_down, up, tx, ty, tz, st,
        )
    )
    tables = gather_rows(table)

    (back_next,) = pl.pallas_call(
        back_kernel,
        in_specs=[VMEM] * 4,
        out_specs=[VMEM],
        out_shape=[held(rows, depth)],
        compiler_params=params(16),
        cost_estimate=mortar_cost,
        name="back_second",
    )(*near_core(jump_next, puts, codes, proj_n))
    recv_next = shifted(back_next, "sub", 1)

    return pl.pallas_call(
        final_kernel,
        in_specs=[VMEM] * 11,
        out_specs=[HBM] * 2,
        out_shape=[jax.ShapeDtypeStruct((layers, rows, depth), F32)] * 2,
        scratch_shapes=[pltpu.VMEM((layers, rows, depth), F32)] * 2 + [pltpu.SemaphoreType.DMA((2, steps))],
        compiler_params=params(8),
        cost_estimate=cost(8 * cells, 22 * cells),
        name="final_update",
    )(*near_core(tables, b, s_first, s_mid, w_last, recv, image_low, image_high, edge_high, jump_next, recv_next))


def solution(mesh):
    cells = P("sub", "blk", None)
    in_specs = (cells,) * 7 + (P("sub", "blk"), P())
    return jax.shard_map(body, mesh=mesh, in_specs=in_specs, out_specs=(cells, cells), check_vma=False)
```

```python
import jax
import jax.numpy as jnp
from jax import lax
from jax.experimental import pallas as pl
from jax.experimental.pallas import tpu as pltpu
from jax.sharding import PartitionSpec as P

ROWS = 32
FIELDS = 16
SUB = 8
LANES = 128
F32 = jnp.float32
BF16 = jnp.bfloat16
penalty = 4.0


def tile_ids(dim, shape):
    return lax.broadcasted_iota(jnp.int32, shape, dim)


def as_tile(scalars):
    lane = tile_ids(1, (SUB, LANES))
    tile = jnp.zeros((SUB, LANES), F32)
    for place, value in enumerate(scalars):
        tile = jnp.where(lane == place, value, tile)
    return tile


def from_tile(tile, place):
    pick = (tile_ids(1, tile.shape) == place) & (tile_ids(0, tile.shape) == 0)
    return jnp.sum(jnp.where(pick, tile, 0.0))


def at(array, layers, start):
    return [array[layer, pl.ds(start, SUB), :] for layer in range(layers)]


def stencil(values, after, tx, ty, tz, st, carry, below=None, above=None):
    shape = values[0].shape
    row = tile_ids(0, shape)
    last_z = tile_ids(1, shape) == shape[1] - 1
    results, carries = [], []
    flux_x = None if below is None else below[1] * (below[0] - values[0])
    for layer, value in enumerate(values):
        follow = value if after is None else pltpu.roll(after[layer], SUB - 1, 0)
        follow = jnp.where(row == SUB - 1, follow, pltpu.roll(value, SUB - 1, 0))
        flux_y = ty[layer] * (value - follow)
        rolled = pltpu.roll(flux_y, 1, 0)
        carries.append(rolled)
        flux_z = jnp.where(last_z, 0.0, tz[layer] * (value - pltpu.roll(value, shape[1] - 1, 1)))
        result = st[layer] * value + (flux_y - jnp.where(row == 0, carry[layer], rolled))
        result = result + (flux_z - pltpu.roll(flux_z, 1, 1))
        if flux_x is not None:
            result = result - flux_x
        next_x = values[layer + 1] if layer < len(values) - 1 else above
        flux_x = None
        if next_x is not None:
            flux_x = tx[layer] * (value - next_x)
            result = result + flux_x
        results.append(result)
    return results, carries


def at_last_block():
    return lax.axis_index("blk") == lax.axis_size("blk") - 1


def edge_terms(before, first, last, beyond, ty_before, ty_last):
    low = ty_before * (first - before)
    high = jnp.where(at_last_block(), 0.0, ty_last * (last - beyond))
    return low, high


def pack_kernel(b_hbm, ty_hbm, face, sems):
    rows = b_hbm.shape[1]
    copies = [
        pltpu.make_async_copy(b_hbm.at[0], face.at[pl.ds(0, rows), :], sems.at[0]),
        pltpu.make_async_copy(ty_hbm.at[0, pl.ds(rows - SUB, SUB), :], face.at[pl.ds(rows, SUB), :], sems.at[1]),
    ]
    for copy in copies:
        copy.start()
    for copy in copies:
        copy.wait()


def two_parts(array):
    high = array.astype(BF16)
    return high, (array - high.astype(F32)).astype(BF16)


def prepare_pairs(perm, kind, count, proj, rows, groups, picks, puts, codes, proj_t, proj_n):
    kinds, width, _ = proj.shape
    blocks = rows * groups
    lane = tile_ids(1, (1, blocks))
    target = lax.rem(perm, groups) * rows + lax.div(perm, groups)
    shift = kinds.bit_length()
    keys = (target * (1 << shift) + jnp.where(lane < count, kind, kinds)).astype(F32)
    span = LANES // groups
    spread = tile_ids(1, (span, LANES)) - groups * tile_ids(0, (span, LANES))
    lanes = tile_ids(1, (rows, LANES))
    across = []
    for group in range(groups):
        column = jnp.concatenate(
            [
                jnp.sum(jnp.where(spread == group, keys[:, place * LANES : (place + 1) * LANES], 0.0), 1, keepdims=True)
                for place in range(blocks // LANES)
            ],
            axis=0,
        ).astype(jnp.int32)
        column = jnp.broadcast_to(column, (rows, LANES))
        here = pl.ds(group * rows, rows)
        codes[here, :] = column & ((1 << shift) - 1)
        column = column >> shift
        for place in range(blocks // LANES):
            picks[here, pl.ds(place * LANES, LANES)] = jnp.where(column == lanes + place * LANES, 1.0, 0.0).astype(BF16)
        for place in range(rows // LANES):
            turned = jnp.transpose(column[place * LANES : (place + 1) * LANES].astype(F32))
            across.append(turned[0:1, :].astype(jnp.int32))
    across = jnp.concatenate(across, axis=1)
    down = tile_ids(0, (rows, blocks))
    for group in range(groups):
        puts[pl.ds(group * rows, rows), :] = jnp.where(across == down + group * rows, 1.0, 0.0).astype(BF16)
    for kind in range(kinds):
        here = pl.ds(kind * width, width)
        proj_t[here, :] = jnp.concatenate(two_parts(jnp.transpose(proj[kind])), axis=1)
        proj_n[here, :] = jnp.concatenate(two_parts(proj[kind]), axis=1)


def first_kernel(
    count, perm, kind, proj, b_hbm, tx_hbm, ty_hbm, tz_hbm, st_hbm,
    b, tx, ty, tz, st, face_next, s_first, s_mid, s_last, sums, picks, puts, codes, proj_t, proj_n, total, sems,
):
    layers, rows, depth = b.shape
    steps = rows // ROWS
    sources, targets = (b_hbm, tx_hbm, ty_hbm, tz_hbm, st_hbm), (b, tx, ty, tz, st)

    def copy(which, step):
        part = pl.ds(step * ROWS, ROWS)
        return pltpu.make_async_copy(
            sources[which].at[:, part, :], targets[which].at[:, part, :], sems.at[which, step]
        )

    for step in range(steps):
        for which in range(len(sources)):
            copy(which, step).start()
    width = proj.shape[1]
    prepare_pairs(
        perm[0], kind[0], count[0, 0], proj, rows, depth // width, picks, puts, codes, proj_t, proj_n
    )
    total[...] = jnp.zeros_like(total)
    copy(0, 0).wait()

    def chunk(start, after, carry):
        values = at(b, layers, start)
        results, carry = stencil(values, after, *[at(array, layers, start) for array in (tx, ty, tz, st)], carry)
        here = pl.ds(start, SUB)
        squares, products = values[0] * values[0], values[0] * results[0]
        for layer in range(1, layers):
            squares = squares + values[layer] * values[layer]
            products = products + values[layer] * results[layer]
        total[0] += squares
        total[1] += products
        face_next[here, :] = results[0]
        s_first[here, :] = results[0]
        for layer in range(1, layers - 1):
            s_mid[layer - 1, here, :] = results[layer]
        s_last[here, :] = results[layers - 1]
        return carry

    carry = [jnp.zeros((SUB, depth), F32)] * layers
    for step in range(steps):
        for which in range(1, len(sources)):
            copy(which, step).wait()
        if step < steps - 1:
            copy(0, step + 1).wait()
        for start in range(step * ROWS, (step + 1) * ROWS, SUB):
            carry = chunk(start, None if start == rows - SUB else at(b, layers, start + SUB), carry)
    sums[...] = as_tile([jnp.sum(total[0]), jnp.sum(total[1])])


def up_places(layers):
    return 0, layers, 2 * layers, 3 * layers, 3 * layers + 1, 3 * layers + 2


def edge_kernel(
    sums_in, near_sums, b, right, up, down, tx, ty, tz, st, s_first_in, s_mid_in, s_last_in, w_last_in,
    s_first, s_mid, s_last, w_last, sums, image_ends, ends_sums, right_edges, w_up, w_down,
):
    layers, rows, depth = b.shape
    at_b, at_ty, at_w, at_back, at_right, at_right_ty = up_places(layers)
    product = 0.0
    for layer in range(layers):
        first, last = b[layer, 0:1, :], b[layer, rows - 1 :, :]
        low, high = edge_terms(
            up[at_b + layer : at_b + layer + 1, :], first, last, down[layer : layer + 1, :],
            up[at_ty + layer : at_ty + layer + 1, :], ty[layer, rows - 1 :, :],
        )
        pairs = [(s_first_in, s_first)] if layer == 0 else [(s_last_in, s_last), (w_last_in, w_last)]
        if 0 < layer < layers - 1:
            pairs = [(s_mid_in.at[layer - 1], s_mid.at[layer - 1])]
        for source, target in pairs:
            target[0:1, :] = source[0:1, :] + low
            target[rows - 1 :, :] = source[rows - 1 :, :] + high
        product = product + first * low + last * high
        w_up[layer : layer + 1, :] = up[at_w + layer : at_w + layer + 1, :] - low
        w_down[layer : layer + 1, :] = down[layers + layer : layers + layer + 1, :] - high
    sums[...] = sums_in[...] + as_tile([0.0, jnp.sum(product)])
    low, high = edge_terms(
        up[at_right : at_right + 1, :], right[0:1, :], right[rows - 1 : rows, :], down[2 * layers + 1 :, :],
        up[at_right_ty : at_right_ty + 1, :], right[rows + SUB - 1 :, :],
    )
    right_edges[0:1, :] = low
    right_edges[1:2, :] = high
    near = from_tile(near_sums[...], 2)
    own, read, plain = high_layers(layers, s_mid, s_last, w_last)
    terms = None
    for place, start in enumerate((0, rows - SUB)):
        values = read(start)
        if place == 0:
            after, carry = read(SUB), [jnp.zeros((SUB, depth), F32)] * len(own)
        else:
            after, carry = None, flux_from(start - SUB, own, read, 1, ty)
        new, _ = chunk_sums(
            start, values, after, carry, own, near, b, plain, tx, ty, tz, st, image_ends, place * SUB
        )
        terms = new if terms is None else [old + more for old, more in zip(terms, new)]
    ends_sums[...] = as_tile([0.0] * 3 + [jnp.sum(term) for term in terms])


def high_layers(layers, s_mid, s_last, w_last):
    split = layers // 2

    def read(start):
        here = pl.ds(start, SUB)
        return [s_mid[layer - 1, here, :] for layer in range(split - 1, layers - 1)] + [w_last[here, :]]

    def plain(layer, here):
        return s_last[here, :] if layer == layers - 1 else s_mid[layer - 1, here, :]

    return list(range(split, layers)), read, plain


def flux_from(start, own, read, skip, ty):
    row = None
    carry = []
    for layer, value, after in zip(own, read(start)[skip:], read(start + SUB)[skip:]):
        row = tile_ids(0, value.shape)
        follow = jnp.where(row == SUB - 1, pltpu.roll(after, SUB - 1, 0), pltpu.roll(value, SUB - 1, 0))
        carry.append(pltpu.roll(ty[layer, pl.ds(start, SUB), :] * (value - follow), 1, 0))
    return carry


def chunk_sums(start, values, after, carry, own, near, b, plain, tx, ty, tz, st, image, target, summed=None):
    layers = b.shape[0]
    here = pl.ds(start, SUB)
    below = (values[0], tx[own[0] - 1, here, :]) if own[0] > 0 else None
    above = values[-1] if own[-1] < layers - 1 else None
    skip = 0 if below is None else 1
    mine = values[skip : skip + len(own)]
    results, carry = stencil(
        mine, None if after is None else after[skip : skip + len(own)],
        *[[array[layer, here, :] for layer in own] for array in (tx, ty, tz, st)], carry, below, above,
    )
    terms = None
    for place, layer in enumerate(own):
        w, s = mine[place], results[place]
        image[place, pl.ds(target, SUB), :] = s
        if summed is not None and layer not in summed:
            continue
        u = b[layer, here, :] - near * w
        q = plain(layer, here) - near * s
        new = [u * u, u * w, w * w, u * q, u * s + w * q, w * s]
        terms = new if terms is None else [old + more for old, more in zip(terms, new)]
    return terms, carry


def mm(left, right):
    return lax.dot_general(left, right, (((1,), (0,)), ((), ())), preferred_element_type=F32)


def by_kind(codes, array, kinds):
    zero = jnp.zeros_like(array)
    return jnp.concatenate([jnp.where(codes == kind, array, zero) for kind in range(kinds)], axis=1)


def apply_proj(codes, high, low, proj, kinds, width):
    both = mm(by_kind(codes, high, kinds), proj[...])
    return both[:, :width] + both[:, width:] + mm(by_kind(codes, low, kinds), proj[:, :width])


def take_jump(group, faces, last, picks, codes_col, proj_t):
    width = proj_t.shape[1] // 2
    kinds = proj_t.shape[0] // width
    here = pl.ds(group * last.shape[0], last.shape[0])
    codes = codes_col[here, :]
    taken = mm(picks[here, :], faces)
    projected = apply_proj(codes, taken[:, :width].astype(BF16), taken[:, width:].astype(BF16), proj_t, kinds, width)
    return jnp.where(codes < kinds, last - projected, 0.0)


def turn_back(group, jump, codes_col, proj_n):
    width = proj_n.shape[1] // 2
    kinds = proj_n.shape[0] // width
    scale = jnp.where(lax.axis_index("sub") < lax.axis_size("sub") - 1, -penalty, 0.0)
    codes = codes_col[pl.ds(group * jump.shape[0], jump.shape[0]), :]
    return jnp.concatenate(two_parts(scale * apply_proj(codes, *two_parts(jump), proj_n, kinds, width)), axis=1)


def put_back(group, backs, puts, rows):
    width = backs.shape[1] // 2
    placed = mm(puts[pl.ds(group * rows, rows), :], backs)
    return placed[:, :width] + placed[:, width:]


def stack_parts(parts):
    return jnp.concatenate(two_parts(jnp.concatenate(parts, axis=0)), axis=1)


def jump_first_kernel(b, right, s_last, picks, codes, proj_t, w_last, jump_face, sums):
    width = proj_t.shape[1] // 2
    layers, rows, depth = b.shape
    parts = [pl.ds(group * width, width) for group in range(depth // width)]
    faces = stack_parts([right[:rows, part] for part in parts])
    square = jnp.zeros((rows, width), F32)
    for group, part in enumerate(parts):
        jump = take_jump(group, faces, b[layers - 1, :, part], picks, codes, proj_t)
        square = square + jump * jump
        jump_face[:, part] = jump
        w_last[:, part] = s_last[:, part] + penalty * jump
    sums[...] = as_tile([jnp.sum(square)])


def rows_kernel(right, b, ty, s_first, s_mid, w_last, back, up, down):
    layers, rows, _ = b.shape
    at_b, at_ty, at_w, at_back, at_right, at_right_ty = up_places(layers)
    end = pl.ds(rows - 1, 1)
    for layer in range(layers):
        image = s_first if layer == 0 else w_last if layer == layers - 1 else s_mid.at[layer - 1]
        up[at_b + layer : at_b + layer + 1, :] = b[layer, end, :]
        up[at_ty + layer : at_ty + layer + 1, :] = ty[layer, end, :]
        up[at_w + layer : at_w + layer + 1, :] = image[end, :]
        down[layer : layer + 1, :] = b[layer, 0:1, :]
        down[layers + layer : layers + layer + 1, :] = image[0:1, :]
    up[at_back : at_back + 1, :] = back[end, :]
    up[at_right : at_right + 1, :] = right[end, :]
    up[at_right_ty : at_right_ty + 1, :] = right[rows + SUB - 1 :, :]
    down[2 * layers : 2 * layers + 1, :] = back[0:1, :]
    down[2 * layers + 1 : 2 * layers + 2, :] = right[0:1, :]


def jump_second_kernel(
    near_sums, w_last, jump, right_before, right, right_edges, back_before, up, down, picks, codes, proj_t,
    jump_next, sums, missing, field,
):
    width = proj_t.shape[1] // 2
    rows, depth = right.shape
    layers = (up.shape[0] - 3) // 3
    parts = [pl.ds(group * width, width) for group in range(depth // width)]
    near = from_tile(near_sums[...], 2)
    field[...] = right[...] + back_before[...]
    field[0:1, :] += right_edges[0:1, :]
    field[rows - 1 :, :] += right_edges[1:2, :]
    faces = stack_parts([field[:, part] for part in parts])
    totals = [jnp.zeros((rows, width), F32)] * 3
    for group, part in enumerate(parts):
        later = take_jump(group, faces, w_last[:, part], picks, codes, proj_t)
        jump_next[:, part] = later
        close = jump[:, part] - near * later
        totals = [total + new for total, new in zip(totals, (close * close, close * later, later * later))]
    found = [jnp.sum(total) for total in totals]
    found = [penalty * found[0], 2.0 * penalty * found[1], penalty * found[2]]
    _, _, _, at_back, _, at_right_ty = up_places(layers)
    low = -up[at_right_ty : at_right_ty + 1, :] * up[at_back : at_back + 1, :]
    high = jnp.where(at_last_block(), 0.0, -right_before[rows + SUB - 1 :, :] * down[2 * layers : 2 * layers + 1, :])
    missing[0:1, :] = low
    missing[1:2, :] = high
    extra = [0.0] * 3
    for place, s in ((0, low), (rows - 1, high)):
        w = field[place : place + 1, :]
        u = right_before[place : place + 1, :] - near * w
        extra = [old + more for old, more in zip(extra, [-near * u * s, u * s - near * w * s, w * s])]
    sums[...] = as_tile([0.0] * 6 + [old + jnp.sum(more) for old, more in zip(found, extra)])


def back_second_kernel(jump_next, missing, puts, codes, proj_n, back):
    rows = jump_next.shape[0]
    back_kernel(jump_next, puts, codes, proj_n, back)
    back[rows : rows + 2, :] = missing[...]


def hold_kernel(later, back_in, back):
    back[back.shape[0] - SUB + 2 :, :] = jnp.zeros((SUB - 2, back.shape[1]), F32)


def back_kernel(jump_next, puts, codes, proj_n, back):
    width = proj_n.shape[1] // 2
    rows, depth = jump_next.shape
    parts = [pl.ds(group * width, width) for group in range(depth // width)]
    backs = [turn_back(group, jump_next[:, part], codes, proj_n) for group, part in enumerate(parts)]
    backs = jnp.concatenate(backs, axis=0)
    for group, part in enumerate(parts):
        back[:rows, part] = put_back(group, backs, puts, rows)


def stencil_sums(read, own, near, b, plain, tx, ty, tz, st, image, total, inner, summed=None):
    layers, rows, depth = b.shape
    total[...] = jnp.zeros_like(total)
    skip = 1 if own[0] > 0 else 0

    def several(start, count, carry, at_end=False):
        starts = [pl.multiple_of(start + SUB * place, SUB) for place in range(count + 1)]
        values = [read(place) for place in starts[:-1]] + [None if at_end else read(starts[-1])]
        terms = None
        for place in range(count):
            new, carry = chunk_sums(
                starts[place], values[place], values[place + 1], carry, own, near, b, plain, tx, ty, tz, st, image,
                starts[place], summed,
            )
            terms = new if terms is None else [old + more for old, more in zip(terms, new)]
        for place, term in enumerate(terms):
            total[place] += term
        return carry

    group = 2
    if inner:
        begin, count, carry = SUB, (rows // SUB - 2) // group, flux_from(0, own, read, skip, ty)
    else:
        begin, count, carry = 0, rows // (group * SUB) - 1, [jnp.zeros((SUB, depth), F32)] * len(own)
    carry = lax.fori_loop(
        0, count,
        lambda index, carry: tuple(
            several(pl.multiple_of(begin + index * group * SUB, SUB), group, list(carry))
        ),
        tuple(carry),
    )
    if not inner:
        several(rows - group * SUB, group, list(carry), True)
    return [jnp.sum(total[place]) for place in range(total.shape[0])]


def second_high_kernel(later, first_sums, jump_sums, b, s_mid, s_last, w_last, tx, ty, tz, st, image, sums, total):
    norm = from_tile(first_sums[...], 0)
    energy = from_tile(first_sums[...], 1) + penalty * from_tile(jump_sums[...], 0)
    safe = energy > 0.01 * norm
    ratio = jnp.full((SUB, LANES), norm, F32) / jnp.full((SUB, LANES), jnp.where(safe, energy, 1.0), F32)
    near = jnp.where(safe, jnp.max(ratio), 0.0)
    own, read, plain = high_layers(b.shape[0], s_mid, s_last, w_last)
    found = stencil_sums(read, own, near, b, plain, tx, ty, tz, st, image, total, True)
    sums[...] = as_tile([0.0, 0.0, near] + found)


def second_low_kernel(high_sums, b, s_first, s_mid, tx, ty, tz, st, image, sums, total):
    layers = b.shape[0]
    split = layers // 2
    near = from_tile(high_sums[...], 2)

    def read(start):
        here = pl.ds(start, SUB)
        return [s_first[here, :]] + [s_mid[layer - 1, here, :] for layer in range(1, split + 1)]

    def plain(layer, here):
        return s_mid[layer - 1, here, :]

    own = list(range(split))
    found = stencil_sums(read, own, near, b, plain, tx, ty, tz, st, image, total, False, own[1:])
    sums[...] = high_sums[...] + as_tile([0.0] * 3 + found)


def second_added_kernel(
    first_sums, jump_sums, low_sums, ends_sums, second_sums, b, s_first, s_mid, w_last, recv,
    w_up, w_down, up, tx, ty, tz, st, image_in, image, edge_high, table, total,
):
    layers, rows, depth = b.shape
    split = layers // 2
    near = from_tile(low_sums[...], 2)
    total[...] = jnp.zeros_like(total)
    first, second = 0, 1

    def several(start, count, carry, at_end=False):
        starts = [pl.multiple_of(start + SUB * place, SUB) for place in range(count + 1)]
        added = [recv[pl.ds(place, SUB), :] for place in starts[:-1]]
        added.append(None if at_end else recv[pl.ds(starts[-1], SUB), :])
        terms = None
        for place in range(count):
            here = pl.ds(starts[place], SUB)
            e, t_x = added[place], tx[first, here, :]
            (s,), carry = stencil(
                [e], None if added[place + 1] is None else [added[place + 1]], [t_x], [ty[first, here, :]],
                [tz[first, here, :]], [st[first, here, :] + t_x], carry,
            )
            s = image_in[first, here, :] + s
            image[first, here, :] = s
            plain = s_first[here, :]
            w = plain + e
            u = b[first, here, :] - near * w
            q = plain - near * s
            new = [u * u, u * w, w * w, u * q, u * s + w * q, w * s]
            added_s = -t_x * e
            image[second, here, :] = image_in[second, here, :] + added_s
            w = s_mid[second - 1, here, :]
            u = b[second, here, :] - near * w
            new[3] = new[3] - near * u * added_s
            new[4] = new[4] + (u - near * w) * added_s
            new[5] = new[5] + w * added_s
            terms = new if terms is None else [old + more for old, more in zip(terms, new)]
        for place, term in enumerate(terms):
            total[place] += term
        return carry

    group = 4
    carry = lax.fori_loop(
        0, rows // (group * SUB) - 1,
        lambda index, carry: several(pl.multiple_of(index * group * SUB, SUB), group, [carry])[0],
        jnp.zeros((SUB, depth), F32),
    )
    several(rows - group * SUB, group, [carry], True)
    found = [jnp.sum(total[place]) for place in range(total.shape[0])]

    def row(layer, place):
        here = pl.ds(place, 1)
        if layer == 0:
            return s_first[here, :] + recv[here, :]
        return w_last[here, :] if layer == layers - 1 else s_mid[layer - 1, here, :]

    extra = [jnp.zeros((1, depth), F32)] * 3
    for layer in range(layers):
        ends = row(layer, 0), row(layer, rows - 1)
        added = edge_terms(
            w_up[layer : layer + 1, :], *ends, w_down[layer : layer + 1, :],
            up[layers + layer : layers + layer + 1, :], ty[layer, rows - 1 :, :],
        )
        for side, (place, w, s) in enumerate(zip((0, rows - 1), ends, added)):
            u = b[layer, place : place + 1, :] - near * w
            extra = [old + more for old, more in zip(extra, [-near * u * s, u * s - near * w * s, w * s])]
            if layer < split:
                image[layer, place : place + 1, :] += s
            else:
                spot = side * (layers - split) + layer - split
                edge_high[spot : spot + 1, :] = s
    found[3:] = [old + jnp.sum(more) for old, more in zip(found[3:], extra)]
    norm = from_tile(first_sums[...], 0)
    energy = from_tile(first_sums[...], 1) + penalty * from_tile(jump_sums[...], 0)
    sums = low_sums[...] + ends_sums[...] + second_sums[...]
    sums = sums + as_tile([norm, energy, 0.0] + found)
    mine = lax.axis_index("sub") * lax.axis_size("blk") + lax.axis_index("blk")
    device = tile_ids(0, table.shape) * (LANES // FIELDS) + lax.div(tile_ids(1, table.shape), FIELDS)
    field = lax.rem(tile_ids(1, table.shape), FIELDS)
    filled = jnp.zeros(table.shape, F32)
    for place in range(9):
        filled = jnp.where((device == mine) & (field == place), jnp.sum(sums[0:1, place : place + 1]), filled)
    table[...] = filled


def final_kernel(
    tables, b, s_first, s_mid, w_last, recv, image_low, image_high, image_ends, edge_high, jump_next, recv_next, solution_hbm, residual_hbm,
    solution, residual, sems,
):
    layers, rows, depth = b.shape
    split = image_low.shape[0]
    flat = tables[...]
    norm, energy, near, uu, uw, ww, uq, cross, wq = [
        flat if place == 0 else pltpu.roll(flat, LANES - place, 1) for place in range(9)
    ]
    own = lax.rem(tile_ids(1, flat.shape), FIELDS) == 0

    def whole(array):
        array = jnp.sum(jnp.where(own, array, 0.0), axis=0, keepdims=True)
        return jnp.sum(array, axis=1, keepdims=True)

    norm, energy = whole(norm), whole(energy)
    alpha = norm / energy
    away = alpha - near
    norm_next = whole(uu - away * (2.0 * uw - away * ww))
    energy_next = whole(uq - away * (cross - away * wq))
    beta = norm_next / norm
    step_size = norm_next / (energy_next - beta * norm_next / alpha)
    c0 = jnp.broadcast_to(alpha + step_size * beta + step_size, (SUB, depth))
    c1 = jnp.broadcast_to(step_size * alpha, (SUB, depth))
    c2 = jnp.broadcast_to(alpha + step_size * (1.0 + beta), (SUB, depth))

    def copy(which, step):
        part = pl.ds(step * ROWS, ROWS)
        source, target = ((solution, solution_hbm), (residual, residual_hbm))[which]
        return pltpu.make_async_copy(source.at[:, part, :], target.at[:, part, :], sems.at[which, step])

    for step in range(rows // ROWS):
        for start in range(step * ROWS, (step + 1) * ROWS, SUB):
            here = pl.ds(start, SUB)
            for layer in range(layers):
                v = b[layer, here, :]
                if layer < split:
                    s = image_low[layer, here, :]
                elif start == 0:
                    s = image_ends[layer - split, :SUB, :]
                elif start == rows - SUB:
                    s = image_ends[layer - split, SUB:, :]
                else:
                    s = image_high[layer - split, here, :]
                if layer == 0:
                    w = s_first[here, :] + recv[here, :]
                    s = s + recv_next[here, :]
                elif layer < layers - 1:
                    w = s_mid[layer - 1, here, :]
                else:
                    w = w_last[here, :]
                    s = s + penalty * jump_next[here, :]
                solution[layer, here, :] = c0 * v - c1 * w
                residual[layer, here, :] = v - c2 * w + c1 * s
        for side, last_step in enumerate((0, rows // ROWS - 1)):
            if step == last_step:
                place = side * (rows - 1)
                residual[0, place : place + 1, :] += c1[0:1, :] * recv_next[rows + side : rows + side + 1, :]
                for layer in range(split, layers):
                    spot = side * (layers - split) + layer - split
                    residual[layer, place : place + 1, :] += c1[0:1, :] * edge_high[spot : spot + 1, :]
        for which in range(2):
            copy(which, step).start()
    for step in range(rows // ROWS):
        for which in range(2):
            copy(which, step).wait()


SMEM = pl.BlockSpec(memory_space=pltpu.SMEM)
VMEM = pl.BlockSpec(memory_space=pltpu.VMEM)
HBM = pl.BlockSpec(memory_space=pltpu.HBM)


def held(*dims, dtype=F32):
    return pltpu.VMEM(dims, dtype)


def near_core(*arrays):
    return [pltpu.with_memory_space_constraint(array, pltpu.VMEM) for array in arrays]


def in_hbm(*arrays):
    return [pltpu.with_memory_space_constraint(array, pltpu.HBM) for array in arrays]


def params(mib):
    return pltpu.CompilerParams(vmem_limit_bytes=mib * 1024 * 1024)


def shifted(array, axis, by):
    size = lax.axis_size(axis)
    return lax.ppermute(array, axis, [(i, i + by) for i in range(size) if 0 <= i + by < size])


def gather_rows(table):
    subs, blks = lax.axis_size("sub"), lax.axis_size("blk")
    steps = [(0, 1)]
    reach = 2
    while reach < blks:
        steps.append((0, reach + 1))
        reach *= 2
    reach = subs // 2
    while reach > 0:
        steps.append((reach, 1))
        reach //= 2
    for by_sub, by_blk in steps:
        pairs = [(s * blks + t, (s ^ by_sub) * blks + (t ^ by_blk)) for s in range(subs) for t in range(blks)]
        table = table + lax.ppermute(table, ("sub", "blk"), pairs)
    return table


def body(right_side, trans_x, trans_y, trans_z, storage, pair_perm, pair_type, pair_count, proj):
    layers, rows, depth = right_side.shape
    blocks, width, kinds = pair_perm.shape[2], proj.shape[1], proj.shape[0]
    subs, blks = lax.axis_size("sub"), lax.axis_size("blk")
    steps = rows // ROWS
    cells = layers * rows * depth
    cost = lambda flops, size: pl.CostEstimate(flops=int(flops), bytes_accessed=int(size), transcendentals=0)

    (face,) = pl.pallas_call(
        pack_kernel,
        in_specs=[HBM, HBM],
        out_specs=[VMEM],
        out_shape=[held(rows + SUB, depth)],
        scratch_shapes=[pltpu.SemaphoreType.DMA((2,))],
        compiler_params=params(2),
        cost_estimate=cost(0, 4 * rows * depth),
        name="pack",
    )(*in_hbm(right_side, trans_y))
    face_right = shifted(face, "sub", -1)

    b, tx, ty, tz, st, face_next, s_first, s_mid, s_last, first_sums, picks, puts, codes, proj_t, proj_n = pl.pallas_call(
        first_kernel,
        in_specs=[SMEM] + [VMEM] * 3 + [HBM] * 5,
        out_specs=[VMEM] * 15,
        out_shape=[held(layers, rows, depth)] * 5
        + [
            held(rows, depth), held(rows, depth), held(layers - 2, rows, depth), held(rows, depth), held(SUB, LANES),
            held(blocks, blocks, dtype=BF16), held(blocks, blocks, dtype=BF16), held(blocks, width, dtype=jnp.int32),
            held(kinds * width, 2 * width, dtype=BF16), held(kinds * width, 2 * width, dtype=BF16),
        ],
        scratch_shapes=[pltpu.VMEM((2, SUB, depth), F32), pltpu.SemaphoreType.DMA((5, steps))],
        compiler_params=params(16),
        cost_estimate=cost(20 * cells, 24 * cells),
        name="stencil_first",
    )(
        pair_count, pair_perm, pair_type, proj,
        *in_hbm(right_side, trans_x, trans_y, trans_z, storage),
    )
    face_right_next = shifted(face_next, "sub", -1)

    mortar_cost = cost(4 * blocks * blocks * width + 6 * kinds * blocks * width * width, 14 * rows * depth)
    w_last, jump, jump_sums = pl.pallas_call(
        jump_first_kernel,
        in_specs=[VMEM] * 6,
        out_specs=[VMEM] * 3,
        out_shape=[held(rows, depth), held(rows, depth), held(SUB, LANES)],
        compiler_params=params(16),
        cost_estimate=mortar_cost,
        name="jump_first",
    )(*near_core(b, face_right, s_last, picks, codes, proj_t))
    (back,) = pl.pallas_call(
        back_kernel,
        in_specs=[VMEM] * 4,
        out_specs=[VMEM],
        out_shape=[held(rows, depth)],
        compiler_params=params(16),
        cost_estimate=mortar_cost,
        name="back_first",
    )(*near_core(jump, puts, codes, proj_n))
    recv = shifted(back, "sub", 1)

    split = layers // 2
    image_high, high_sums = pl.pallas_call(
        second_high_kernel,
        in_specs=[VMEM] * 11,
        out_specs=[VMEM] * 2,
        out_shape=[held(layers - split, rows, depth), held(SUB, LANES)],
        scratch_shapes=[pltpu.VMEM((6, SUB, depth), F32)],
        compiler_params=params(8),
        cost_estimate=cost(20 * cells, 15 * cells),
        name="stencil_second_high",
    )(*near_core(back, first_sums, jump_sums, b, s_mid, s_last, w_last, tx, ty, tz, st))
    up_out, down_out = pl.pallas_call(
        rows_kernel,
        in_specs=[VMEM] * 7,
        out_specs=[VMEM] * 2,
        out_shape=[held(3 * layers + 3, depth), held(2 * layers + 2, depth)],
        compiler_params=params(2),
        cost_estimate=cost(0, 64 * depth),
        name="rows",
    )(*near_core(face_right, b, ty, s_first, s_mid, w_last, back))
    up = shifted(up_out, "blk", 1)
    down = shifted(down_out, "blk", -1)
    s_first, s_mid, s_last, w_last, edge_sums, image_ends, ends_sums, right_edges, w_up, w_down = pl.pallas_call(
        edge_kernel,
        in_specs=[VMEM] * 14,
        out_specs=[VMEM] * 10,
        out_shape=[held(rows, depth), held(layers - 2, rows, depth), held(rows, depth), held(rows, depth)]
        + [held(SUB, LANES), held(layers - split, 2 * SUB, depth), held(SUB, LANES)]
        + [held(2, depth), held(layers, depth), held(layers, depth)],
        input_output_aliases={10: 0, 11: 1, 12: 2, 13: 3},
        compiler_params=params(4),
        cost_estimate=cost(320 * depth, 640 * depth),
        name="edges_first",
    )(
        *near_core(
            first_sums, high_sums, b, face_right, up, down, tx, ty, tz, st, s_first, s_mid, s_last, w_last,
        )
    )

    image_low, low_sums = pl.pallas_call(
        second_low_kernel,
        in_specs=[VMEM] * 8,
        out_specs=[VMEM] * 2,
        out_shape=[held(split, rows, depth), held(SUB, LANES)],
        scratch_shapes=[pltpu.VMEM((6, SUB, depth), F32)],
        compiler_params=params(8),
        cost_estimate=cost(20 * cells, 15 * cells),
        name="stencil_second_low",
    )(*near_core(high_sums, b, s_first, s_mid, tx, ty, tz, st))

    jump_next, second_sums, missing = pl.pallas_call(
        jump_second_kernel,
        in_specs=[VMEM] * 12,
        out_specs=[VMEM] * 3,
        out_shape=[held(rows, depth), held(SUB, LANES), held(2, depth)],
        scratch_shapes=[pltpu.VMEM((rows, depth), F32)],
        compiler_params=params(16),
        cost_estimate=mortar_cost,
        name="jump_second",
    )(
        *near_core(
            low_sums, w_last, jump, face_right, face_right_next, right_edges, back, up, down, picks, codes, proj_t,
        )
    )
    (back_next,) = pl.pallas_call(
        back_second_kernel,
        in_specs=[VMEM] * 5,
        out_specs=[VMEM],
        out_shape=[held(rows + SUB, depth)],
        compiler_params=params(16),
        cost_estimate=mortar_cost,
        name="back_second",
    )(*near_core(jump_next, missing, puts, codes, proj_n))

    (back_next,) = pl.pallas_call(
        hold_kernel,
        in_specs=[VMEM] * 2,
        out_specs=[VMEM],
        out_shape=[held(rows + SUB, depth)],
        input_output_aliases={1: 0},
        compiler_params=params(2),
        cost_estimate=cost(0, 8 * depth),
        name="hold",
    )(*near_core(recv, back_next))
    recv_next = shifted(back_next, "sub", 1)

    count = subs * blks
    image_low, edge_high, table = pl.pallas_call(
        second_added_kernel,
        in_specs=[VMEM] * 18,
        out_specs=[VMEM] * 3,
        out_shape=[
            held(split, rows, depth), held(2 * (layers - split), depth), held(-(-count * FIELDS // LANES), LANES),
        ],
        input_output_aliases={17: 0},
        scratch_shapes=[pltpu.VMEM((6, SUB, depth), F32)],
        compiler_params=params(8),
        cost_estimate=cost(20 * cells, 15 * cells),
        name="stencil_second_added",
    )(
        *near_core(
            edge_sums, jump_sums, low_sums, ends_sums, second_sums, b, s_first, s_mid, w_last, recv,
            w_up, w_down, up, tx, ty, tz, st, image_low,
        )
    )
    tables = gather_rows(table)

    return pl.pallas_call(
        final_kernel,
        in_specs=[VMEM] * 12,
        out_specs=[HBM] * 2,
        out_shape=[jax.ShapeDtypeStruct((layers, rows, depth), F32)] * 2,
        scratch_shapes=[pltpu.VMEM((layers, rows, depth), F32)] * 2 + [pltpu.SemaphoreType.DMA((2, steps))],
        compiler_params=params(8),
        cost_estimate=cost(8 * cells, 22 * cells),
        name="final_update",
    )(*near_core(tables, b, s_first, s_mid, w_last, recv, image_low, image_high, image_ends, edge_high, jump_next, recv_next))


def solution(mesh):
    cells = P("sub", "blk", None)
    in_specs = (cells,) * 7 + (P("sub", "blk"), P())
    return jax.shard_map(body, mesh=mesh, in_specs=in_specs, out_specs=(cells, cells), check_vma=False)
```

```python
import jax
import jax.numpy as jnp
from jax import lax
from jax.experimental import pallas as pl
from jax.experimental.pallas import tpu as pltpu
from jax.sharding import PartitionSpec as P

ROWS = 32
FIELDS = 16
SUB = 8
LANES = 128
F32 = jnp.float32
BF16 = jnp.bfloat16
penalty = 4.0


def tile_ids(dim, shape):
    return lax.broadcasted_iota(jnp.int32, shape, dim)


def as_tile(scalars):
    lane = tile_ids(1, (SUB, LANES))
    tile = jnp.zeros((SUB, LANES), F32)
    for place, value in enumerate(scalars):
        tile = jnp.where(lane == place, value, tile)
    return tile


def from_tile(tile, place):
    pick = (tile_ids(1, tile.shape) == place) & (tile_ids(0, tile.shape) == 0)
    return jnp.sum(jnp.where(pick, tile, 0.0))


def fold(array):
    parts = [array[:, place : place + LANES] for place in range(0, array.shape[1], LANES)]
    while len(parts) > 1:
        parts = [one + other for one, other in zip(parts[::2], parts[1::2])]
    return parts[0]


def at(array, layers, start):
    return [array[layer, pl.ds(start, SUB), :] for layer in range(layers)]


def stencil(values, after, tx, ty, tz, st, carry, below=None, above=None):
    shape = values[0].shape
    row = tile_ids(0, shape)
    last_z = tile_ids(1, shape) == shape[1] - 1
    results, carries = [], []
    flux_x = None if below is None else below[1] * (below[0] - values[0])
    for layer, value in enumerate(values):
        follow = value if after is None else pltpu.roll(after[layer], SUB - 1, 0)
        follow = jnp.where(row == SUB - 1, follow, pltpu.roll(value, SUB - 1, 0))
        flux_y = ty[layer] * (value - follow)
        rolled = pltpu.roll(flux_y, 1, 0)
        carries.append(rolled)
        flux_z = jnp.where(last_z, 0.0, tz[layer] * (value - pltpu.roll(value, shape[1] - 1, 1)))
        result = st[layer] * value + (flux_y - jnp.where(row == 0, carry[layer], rolled))
        result = result + (flux_z - pltpu.roll(flux_z, 1, 1))
        if flux_x is not None:
            result = result - flux_x
        next_x = values[layer + 1] if layer < len(values) - 1 else above
        flux_x = None
        if next_x is not None:
            flux_x = tx[layer] * (value - next_x)
            result = result + flux_x
        results.append(result)
    return results, carries


def at_last_block():
    return lax.axis_index("blk") == lax.axis_size("blk") - 1


def edge_terms(before, first, last, beyond, ty_before, ty_last):
    low = ty_before * (first - before)
    high = jnp.where(at_last_block(), 0.0, ty_last * (last - beyond))
    return low, high


def pack_kernel(b_hbm, ty_hbm, face, sems):
    rows = b_hbm.shape[1]
    copies = [
        pltpu.make_async_copy(b_hbm.at[0], face.at[pl.ds(0, rows), :], sems.at[0]),
        pltpu.make_async_copy(ty_hbm.at[0, pl.ds(rows - SUB, SUB), :], face.at[pl.ds(rows, SUB), :], sems.at[1]),
    ]
    for copy in copies:
        copy.start()
    for copy in copies:
        copy.wait()


def two_parts(array):
    high = array.astype(BF16)
    return high, (array - high.astype(F32)).astype(BF16)


def prepare_pairs(perm, kind, count, proj, rows, groups, picks, puts, codes, code_row, proj_t, proj_n):
    kinds, width, _ = proj.shape
    blocks = rows * groups
    lane = tile_ids(1, (1, blocks))
    target = lax.rem(perm, groups) * rows + lax.div(perm, groups)
    shift = kinds.bit_length()
    keys = (target * (1 << shift) + jnp.where(lane < count, kind, kinds)).astype(F32)
    span = LANES // groups
    spread = tile_ids(1, (span, LANES)) - groups * tile_ids(0, (span, LANES))
    lanes = tile_ids(1, (rows, LANES))
    across = []
    for group in range(groups):
        column = jnp.concatenate(
            [
                jnp.sum(jnp.where(spread == group, keys[:, place * LANES : (place + 1) * LANES], 0.0), 1, keepdims=True)
                for place in range(blocks // LANES)
            ],
            axis=0,
        ).astype(jnp.int32)
        column = jnp.broadcast_to(column, (rows, LANES))
        here = pl.ds(group * rows, rows)
        for place in range(rows // LANES):
            turned = jnp.transpose(column[place * LANES : (place + 1) * LANES].astype(F32))
            across.append(turned[0:1, :].astype(jnp.int32))
        codes[here, :] = column & ((1 << shift) - 1)
        column = column >> shift
        for place in range(blocks // LANES):
            picks[here, pl.ds(place * LANES, LANES)] = jnp.where(column == lanes + place * LANES, 1.0, 0.0).astype(BF16)
    across = jnp.concatenate(across, axis=1)
    code_row[...] = (kinds - (across & ((1 << shift) - 1))).astype(F32)
    across = across >> shift
    down = tile_ids(0, (rows, blocks))
    for group in range(groups):
        puts[pl.ds(group * rows, rows), :] = jnp.where(across == down + group * rows, 1.0, 0.0).astype(BF16)
    for kind in range(kinds):
        here = pl.ds(kind * width, width)
        proj_t[here, :] = jnp.concatenate(two_parts(jnp.transpose(proj[kind])), axis=1)
        proj_n[here, :] = jnp.concatenate(two_parts(proj[kind]), axis=1)


def first_kernel(
    count, perm, kind, proj, b_hbm, tx_hbm, ty_hbm, tz_hbm, st_hbm,
    b, tx, ty, tz, st, face_next, s_first, s_mid, s_last, sums, picks, puts, codes, code_row, proj_t, proj_n, total, sems,
):
    layers, rows, depth = b.shape
    steps = rows // ROWS
    sources, targets = (b_hbm, tx_hbm, ty_hbm, tz_hbm, st_hbm), (b, tx, ty, tz, st)

    def copy(which, step):
        part = pl.ds(step * ROWS, ROWS)
        return pltpu.make_async_copy(
            sources[which].at[:, part, :], targets[which].at[:, part, :], sems.at[which, step]
        )

    for step in range(steps):
        for which in range(len(sources)):
            copy(which, step).start()
    width = proj.shape[1]
    prepare_pairs(
        perm[0], kind[0], count[0, 0], proj, rows, depth // width, picks, puts, codes, code_row, proj_t, proj_n
    )
    total[...] = jnp.zeros_like(total)
    copy(0, 0).wait()

    def chunk(start, after, carry):
        values = at(b, layers, start)
        results, carry = stencil(values, after, *[at(array, layers, start) for array in (tx, ty, tz, st)], carry)
        here = pl.ds(start, SUB)
        squares, products = values[0] * values[0], values[0] * results[0]
        for layer in range(1, layers):
            squares = squares + values[layer] * values[layer]
            products = products + values[layer] * results[layer]
        total[0] += fold(squares)
        total[1] += fold(products)
        face_next[here, :] = results[0]
        s_first[here, :] = results[0]
        for layer in range(1, layers - 1):
            s_mid[layer - 1, here, :] = results[layer]
        s_last[here, :] = results[layers - 1]
        return carry

    carry = [jnp.zeros((SUB, depth), F32)] * layers
    for step in range(steps):
        for which in range(1, len(sources)):
            copy(which, step).wait()
        if step < steps - 1:
            copy(0, step + 1).wait()
        for start in range(step * ROWS, (step + 1) * ROWS, SUB):
            carry = chunk(start, None if start == rows - SUB else at(b, layers, start + SUB), carry)
    sums[...] = as_tile([jnp.sum(total[0]), jnp.sum(total[1])])


def up_places(layers):
    return 0, layers, 2 * layers, 3 * layers, 3 * layers + 1, 3 * layers + 2


def edge_kernel(
    sums_in, near_sums, b, right, up, down, tx, ty, tz, st, s_first_in, s_mid_in, s_last_in, w_last_in, image_low_in,
    s_first, s_mid, s_last, w_last, image_low, sums, image_ends, ends_sums, right_edges, missing, w_up, w_down,
):
    layers, rows, depth = b.shape
    at_b, at_ty, at_w, at_back, at_right, at_right_ty = up_places(layers)
    product = 0.0
    for layer in range(layers):
        first, last = b[layer, 0:1, :], b[layer, rows - 1 :, :]
        low, high = edge_terms(
            up[at_b + layer : at_b + layer + 1, :], first, last, down[layer : layer + 1, :],
            up[at_ty + layer : at_ty + layer + 1, :], ty[layer, rows - 1 :, :],
        )
        pairs = [(s_first_in, s_first)] if layer == 0 else [(s_last_in, s_last), (w_last_in, w_last)]
        if 0 < layer < layers - 1:
            pairs = [(s_mid_in.at[layer - 1], s_mid.at[layer - 1])]
        for source, target in pairs:
            target[0:1, :] = source[0:1, :] + low
            target[rows - 1 :, :] = source[rows - 1 :, :] + high
        product = product + first * low + last * high
        w_up[layer : layer + 1, :] = up[at_w + layer : at_w + layer + 1, :] - low
        w_down[layer : layer + 1, :] = down[layers + layer : layers + layer + 1, :] - high
    sums[...] = sums_in[...] + as_tile([0.0, jnp.sum(product)])
    low, high = edge_terms(
        up[at_right : at_right + 1, :], right[0:1, :], right[rows - 1 : rows, :], down[2 * layers + 1 :, :],
        up[at_right_ty : at_right_ty + 1, :], right[rows + SUB - 1 :, :],
    )
    right_edges[0:1, :] = low
    right_edges[1:2, :] = high
    missing[0:1, :] = -up[at_right_ty : at_right_ty + 1, :] * up[at_back : at_back + 1, :]
    missing[1:2, :] = jnp.where(
        at_last_block(), 0.0, -right[rows + SUB - 1 :, :] * down[2 * layers : 2 * layers + 1, :]
    )
    near = from_tile(near_sums[...], 2)
    own, read, plain = high_layers(layers, s_mid, s_last, w_last)
    terms = None
    for place, start in enumerate((0, rows - SUB)):
        values = read(start)
        if place == 0:
            after, carry = read(SUB), [jnp.zeros((SUB, depth), F32)] * len(own)
        else:
            after, carry = None, flux_from(start - SUB, own, read, 1, ty)
        new, _ = chunk_sums(
            start, values, after, carry, own, near, b, plain, tx, ty, tz, st, image_ends, place * SUB
        )
        terms = new if terms is None else [old + more for old, more in zip(terms, new)]
    ends_sums[...] = as_tile([0.0] * 3 + [jnp.sum(term) for term in terms])
    own, read = low_layers(layers, s_first, s_mid)
    zero = [jnp.zeros((SUB, depth), F32)] * len(own)
    low_chunk(0, read(0), read(SUB), zero, own, tx, ty, tz, st, image_low)
    carry = flux_from(rows - 2 * SUB, own, read, 0, ty)
    low_chunk(rows - SUB, read(rows - SUB), None, carry, own, tx, ty, tz, st, image_low)


def high_layers(layers, s_mid, s_last, w_last):
    split = layers // 2

    def read(start):
        here = pl.ds(start, SUB)
        return [s_mid[layer - 1, here, :] for layer in range(split - 1, layers - 1)] + [w_last[here, :]]

    def plain(layer, here):
        return s_last[here, :] if layer == layers - 1 else s_mid[layer - 1, here, :]

    return list(range(split, layers)), read, plain


def flux_from(start, own, read, skip, ty):
    row = None
    carry = []
    for layer, value, after in zip(own, read(start)[skip:], read(start + SUB)[skip:]):
        row = tile_ids(0, value.shape)
        follow = jnp.where(row == SUB - 1, pltpu.roll(after, SUB - 1, 0), pltpu.roll(value, SUB - 1, 0))
        carry.append(pltpu.roll(ty[layer, pl.ds(start, SUB), :] * (value - follow), 1, 0))
    return carry


def chunk_sums(start, values, after, carry, own, near, b, plain, tx, ty, tz, st, image, target, summed=None):
    layers = b.shape[0]
    here = pl.ds(start, SUB)
    below = (values[0], tx[own[0] - 1, here, :]) if own[0] > 0 else None
    above = values[-1] if own[-1] < layers - 1 else None
    skip = 0 if below is None else 1
    mine = values[skip : skip + len(own)]
    results, carry = stencil(
        mine, None if after is None else after[skip : skip + len(own)],
        *[[array[layer, here, :] for layer in own] for array in (tx, ty, tz, st)], carry, below, above,
    )
    terms = None
    for place, layer in enumerate(own):
        w, s = mine[place], results[place]
        image[place, pl.ds(target, SUB), :] = s
        if summed is not None and layer not in summed:
            continue
        u = b[layer, here, :] - near * w
        q = plain(layer, here) - near * s
        new = [fold(term) for term in (u * u, u * w, w * w, u * q, u * s + w * q, w * s)]
        terms = new if terms is None else [old + more for old, more in zip(terms, new)]
    return terms, carry


def mm(left, right):
    return lax.dot_general(left, right, (((1,), (0,)), ((), ())), preferred_element_type=F32)


def by_kind(codes, array, kinds):
    zero = jnp.zeros_like(array)
    return jnp.concatenate([jnp.where(codes == kind, array, zero) for kind in range(kinds)], axis=1)


def apply_proj(codes, high, low, proj, kinds, width):
    both = mm(by_kind(codes, high, kinds), proj[...])
    return both[:, :width] + both[:, width:] + mm(by_kind(codes, low, kinds), proj[:, :width])


def take_jump(group, faces, last, picks, codes_col, proj_t):
    width = proj_t.shape[1] // 2
    kinds = proj_t.shape[0] // width
    here = pl.ds(group * last.shape[0], last.shape[0])
    codes = codes_col[here, :]
    taken = mm(picks[here, :], faces)
    projected = apply_proj(codes, taken[:, :width].astype(BF16), taken[:, width:].astype(BF16), proj_t, kinds, width)
    return jnp.where(codes < kinds, last - projected, 0.0)


def turn_back(group, jump, codes_col, proj_n):
    width = proj_n.shape[1] // 2
    kinds = proj_n.shape[0] // width
    scale = jnp.where(lax.axis_index("sub") < lax.axis_size("sub") - 1, -penalty, 0.0)
    codes = codes_col[pl.ds(group * jump.shape[0], jump.shape[0]), :]
    return jnp.concatenate(two_parts(scale * apply_proj(codes, *two_parts(jump), proj_n, kinds, width)), axis=1)


def put_back(group, backs, puts, rows):
    width = backs.shape[1] // 2
    placed = mm(puts[pl.ds(group * rows, rows), :], backs)
    return placed[:, :width] + placed[:, width:]


def stack_parts(parts):
    return jnp.concatenate(two_parts(jnp.concatenate(parts, axis=0)), axis=1)


def jump_first_kernel(earlier, b, right, s_last, picks, codes, proj_t, w_last, jump_face, sums):
    width = proj_t.shape[1] // 2
    layers, rows, depth = b.shape
    parts = [pl.ds(group * width, width) for group in range(depth // width)]
    faces = stack_parts([right[:rows, part] for part in parts])
    square = jnp.zeros((rows, width), F32)
    for group, part in enumerate(parts):
        jump = take_jump(group, faces, b[layers - 1, :, part], picks, codes, proj_t)
        square = square + jump * jump
        jump_face[:, part] = jump
        w_last[:, part] = s_last[:, part] + penalty * jump
    sums[...] = as_tile([jnp.sum(square)])


def kinds_kernel(code_row, picks, kinds_by_block):
    depth = kinds_by_block.shape[1]
    row = mm(jnp.broadcast_to(code_row[...], (2 * SUB, code_row.shape[1])).astype(BF16), picks[...])
    kinds_by_block[...] = jnp.zeros_like(kinds_by_block)
    for place in range(row.shape[1] // depth):
        kinds_by_block[place : place + 1, :] = row[0:1, place * depth : (place + 1) * depth]


def rows_kernel(right, b, ty, s_first, s_mid, w_last, back, up, down):
    layers, rows, _ = b.shape
    at_b, at_ty, at_w, at_back, at_right, at_right_ty = up_places(layers)
    end = pl.ds(rows - 1, 1)
    for layer in range(layers):
        image = s_first if layer == 0 else w_last if layer == layers - 1 else s_mid.at[layer - 1]
        up[at_b + layer : at_b + layer + 1, :] = b[layer, end, :]
        up[at_ty + layer : at_ty + layer + 1, :] = ty[layer, end, :]
        up[at_w + layer : at_w + layer + 1, :] = image[end, :]
        down[layer : layer + 1, :] = b[layer, 0:1, :]
        down[layers + layer : layers + layer + 1, :] = image[0:1, :]
    up[at_back : at_back + 1, :] = back[end, :]
    up[at_right : at_right + 1, :] = right[end, :]
    up[at_right_ty : at_right_ty + 1, :] = right[rows + SUB - 1 :, :]
    down[2 * layers : 2 * layers + 1, :] = back[0:1, :]
    down[2 * layers + 1 : 2 * layers + 2, :] = right[0:1, :]


def jump_second_kernel(
    near_sums, w_last, jump, right_before, right, right_edges, back_before, missing, picks, codes, proj_t,
    jump_next, sums, field,
):
    width = proj_t.shape[1] // 2
    rows, depth = right.shape
    parts = [pl.ds(group * width, width) for group in range(depth // width)]
    near = from_tile(near_sums[...], 2)
    field[...] = right[...] + back_before[:rows, :]
    field[0:1, :] += right_edges[0:1, :]
    field[rows - 1 :, :] += right_edges[1:2, :]
    faces = stack_parts([field[:, part] for part in parts])
    totals = [jnp.zeros((rows, width), F32)] * 3
    for group, part in enumerate(parts):
        later = take_jump(group, faces, w_last[:, part], picks, codes, proj_t)
        jump_next[:, part] = later
        close = jump[:, part] - near * later
        totals = [total + new for total, new in zip(totals, (close * close, close * later, later * later))]
    found = [jnp.sum(total) for total in totals]
    found = [penalty * found[0], 2.0 * penalty * found[1], penalty * found[2]]
    extra = [0.0] * 3
    for side, place in enumerate((0, rows - 1)):
        s = missing[side : side + 1, :]
        w = field[place : place + 1, :]
        u = right_before[place : place + 1, :] - near * w
        extra = [old + more for old, more in zip(extra, [-near * u * s, u * s - near * w * s, w * s])]
    sums[...] = as_tile([0.0] * 6 + [old + jnp.sum(more) for old, more in zip(found, extra)])


def back_first_kernel(jump, kinds_by_block, puts, codes, proj_n, back):
    rows = jump.shape[0]
    back_kernel(jump, puts, codes, proj_n, back)
    back[rows:, :] = kinds_by_block[...]


def back_second_kernel(w_last, missing, puts, codes, proj_n, back):
    rows = w_last.shape[0]
    back_kernel(w_last, puts, codes, proj_n, back)
    back[rows : rows + 2, :] = missing[...]


def own_second_kernel(s_first, recv, proj_t, proj_n, own):
    rows, depth = own.shape
    width = proj_t.shape[1] // 2
    kinds = proj_t.shape[0] // width
    for group in range(depth // width):
        part = pl.ds(group * width, width)
        codes = []
        for place in range(rows // LANES):
            start = group * rows + place * LANES
            row = recv[rows + start // depth : rows + start // depth + 1, start % depth : start % depth + LANES]
            codes.append(jnp.transpose(jnp.broadcast_to(row, (LANES, LANES))))
        codes = kinds - jnp.concatenate(codes, axis=0).astype(jnp.int32)
        field = s_first[:, part] + recv[:rows, part]
        projected = apply_proj(codes, *two_parts(field), proj_t, kinds, width)
        own[:, part] = penalty * apply_proj(codes, *two_parts(projected), proj_n, kinds, width)


def hold_kernel(later, back_in, back):
    back[back.shape[0] - SUB + 2 :, :] = jnp.zeros((SUB - 2, back.shape[1]), F32)


def back_kernel(jump_next, puts, codes, proj_n, back):
    width = proj_n.shape[1] // 2
    rows, depth = jump_next.shape
    parts = [pl.ds(group * width, width) for group in range(depth // width)]
    backs = [turn_back(group, jump_next[:, part], codes, proj_n) for group, part in enumerate(parts)]
    backs = jnp.concatenate(backs, axis=0)
    for group, part in enumerate(parts):
        back[:rows, part] = put_back(group, backs, puts, rows)


def stencil_sums(read, own, near, b, plain, tx, ty, tz, st, image, total, inner, summed=None):
    layers, rows, depth = b.shape
    total[...] = jnp.zeros_like(total)
    skip = 1 if own[0] > 0 else 0

    def several(start, count, carry, at_end=False):
        starts = [pl.multiple_of(start + SUB * place, SUB) for place in range(count + 1)]
        values = [read(place) for place in starts[:-1]] + [None if at_end else read(starts[-1])]
        terms = None
        for place in range(count):
            new, carry = chunk_sums(
                starts[place], values[place], values[place + 1], carry, own, near, b, plain, tx, ty, tz, st, image,
                starts[place], summed,
            )
            terms = new if terms is None else [old + more for old, more in zip(terms, new)]
        for place, term in enumerate(terms):
            total[place] += term
        return carry

    group = 2
    if inner:
        begin, count, carry = SUB, (rows // SUB - 2) // group, flux_from(0, own, read, skip, ty)
    else:
        begin, count, carry = 0, rows // (group * SUB) - 1, [jnp.zeros((SUB, depth), F32)] * len(own)
    carry = lax.fori_loop(
        0, count,
        lambda index, carry: tuple(
            several(pl.multiple_of(begin + index * group * SUB, SUB), group, list(carry))
        ),
        tuple(carry),
    )
    if not inner:
        several(rows - group * SUB, group, list(carry), True)
    return [jnp.sum(total[place]) for place in range(total.shape[0])]


def second_high_kernel(later, first_sums, jump_sums, b, s_mid, s_last, w_last, tx, ty, tz, st, image, sums, total):
    norm = from_tile(first_sums[...], 0)
    energy = from_tile(first_sums[...], 1) + penalty * from_tile(jump_sums[...], 0)
    safe = energy > 0.01 * norm
    ratio = jnp.full((SUB, LANES), norm, F32) / jnp.full((SUB, LANES), jnp.where(safe, energy, 1.0), F32)
    near = jnp.where(safe, jnp.max(ratio), 0.0)
    own, read, plain = high_layers(b.shape[0], s_mid, s_last, w_last)
    found = stencil_sums(read, own, near, b, plain, tx, ty, tz, st, image, total, True)
    sums[...] = as_tile([0.0, 0.0, near] + found)


def low_layers(layers, s_first, s_mid):
    split = layers // 2

    def read(start):
        here = pl.ds(start, SUB)
        return [s_first[here, :]] + [s_mid[layer - 1, here, :] for layer in range(1, split + 1)]

    return list(range(split)), read


def low_chunk(start, values, after, carry, own, tx, ty, tz, st, image):
    here = pl.ds(start, SUB)
    results, carry = stencil(
        values[:-1], None if after is None else after[:-1],
        *[[array[layer, here, :] for layer in own] for array in (tx, ty, tz, st)], carry, None, values[-1],
    )
    for layer in own:
        image[layer, here, :] = results[layer]
    return carry


def second_low_kernel(s_first, s_mid, tx, ty, tz, st, image):
    layers, rows = tx.shape[:2]
    own, read = low_layers(layers, s_first, s_mid)
    group = 3

    def several(index, carry):
        start = pl.multiple_of(SUB + index * group * SUB, SUB)
        starts = [pl.multiple_of(start + SUB * place, SUB) for place in range(group + 1)]
        values = [read(place) for place in starts]
        carry = list(carry)
        for place in range(group):
            carry = low_chunk(starts[place], values[place], values[place + 1], carry, own, tx, ty, tz, st, image)
        return tuple(carry)

    lax.fori_loop(0, (rows // SUB - 2) // group, several, tuple(flux_from(0, own, read, 0, ty)))


def second_added_kernel(
    first_sums, jump_sums, high_sums, ends_sums, second_sums, b, s_first, s_mid, w_last, recv,
    w_up, w_down, up, tx, ty, tz, st, image_in, image, edge_high, table, total,
):
    layers, rows, depth = b.shape
    split = layers // 2
    near = from_tile(high_sums[...], 2)
    total[...] = jnp.zeros_like(total)
    first, second = 0, 1

    def several(start, count, carry, at_end=False):
        starts = [pl.multiple_of(start + SUB * place, SUB) for place in range(count + 1)]
        added = [recv[pl.ds(place, SUB), :] for place in starts[:-1]]
        added.append(None if at_end else recv[pl.ds(starts[-1], SUB), :])
        terms = None
        for place in range(count):
            here = pl.ds(starts[place], SUB)
            e, t_x = added[place], tx[first, here, :]
            (s,), carry = stencil(
                [e], None if added[place + 1] is None else [added[place + 1]], [t_x], [ty[first, here, :]],
                [tz[first, here, :]], [st[first, here, :] + t_x], carry,
            )
            s = image_in[first, here, :] + s
            image[first, here, :] = s
            plain = s_first[here, :]
            w = plain + e
            u = b[first, here, :] - near * w
            q = plain - near * s
            new = [u * u, u * w, w * w, u * q, u * s + w * q, w * s]
            s = image_in[second, here, :] - t_x * e
            image[second, here, :] = s
            w = s_mid[second - 1, here, :]
            u = b[second, here, :] - near * w
            q = w - near * s
            more = [u * u, u * w, w * w, u * q, u * s + w * q, w * s]
            new = [fold(one + other) for one, other in zip(new, more)]
            terms = new if terms is None else [old + more for old, more in zip(terms, new)]
        for place, term in enumerate(terms):
            total[place] += term
        return carry

    group = 4
    carry = lax.fori_loop(
        0, rows // (group * SUB) - 1,
        lambda index, carry: several(pl.multiple_of(index * group * SUB, SUB), group, [carry])[0],
        jnp.zeros((SUB, depth), F32),
    )
    several(rows - group * SUB, group, [carry], True)
    found = [jnp.sum(total[place]) for place in range(total.shape[0])]

    def row(layer, place):
        here = pl.ds(place, 1)
        if layer == 0:
            return s_first[here, :] + recv[here, :]
        return w_last[here, :] if layer == layers - 1 else s_mid[layer - 1, here, :]

    extra = [jnp.zeros((1, depth), F32)] * 3
    for layer in range(layers):
        ends = row(layer, 0), row(layer, rows - 1)
        added = edge_terms(
            w_up[layer : layer + 1, :], *ends, w_down[layer : layer + 1, :],
            up[layers + layer : layers + layer + 1, :], ty[layer, rows - 1 :, :],
        )
        for side, (place, w, s) in enumerate(zip((0, rows - 1), ends, added)):
            u = b[layer, place : place + 1, :] - near * w
            extra = [old + more for old, more in zip(extra, [-near * u * s, u * s - near * w * s, w * s])]
            if layer < split:
                image[layer, place : place + 1, :] += s
            else:
                spot = side * (layers - split) + layer - split
                edge_high[spot : spot + 1, :] = s
    found[3:] = [old + jnp.sum(more) for old, more in zip(found[3:], extra)]
    norm = from_tile(first_sums[...], 0)
    energy = from_tile(first_sums[...], 1) + penalty * from_tile(jump_sums[...], 0)
    sums = high_sums[...] + ends_sums[...] + second_sums[...]
    sums = sums + as_tile([norm, energy, 0.0] + found)
    mine = lax.axis_index("sub") * lax.axis_size("blk") + lax.axis_index("blk")
    device = tile_ids(0, table.shape) * (LANES // FIELDS) + lax.div(tile_ids(1, table.shape), FIELDS)
    field = lax.rem(tile_ids(1, table.shape), FIELDS)
    filled = jnp.zeros(table.shape, F32)
    for place in range(9):
        filled = jnp.where((device == mine) & (field == place), jnp.sum(sums[0:1, place : place + 1]), filled)
    table[...] = filled


def final_kernel(
    tables, b, s_first, s_mid, w_last, recv, image_low, image_high, image_ends, edge_high, jump_next, recv_next, own_next, solution_hbm, residual_hbm,
    solution, residual, sems,
):
    layers, rows, depth = b.shape
    split = image_low.shape[0]
    flat = tables[...]
    norm, energy, near, uu, uw, ww, uq, cross, wq = [
        flat if place == 0 else pltpu.roll(flat, LANES - place, 1) for place in range(9)
    ]
    own = lax.rem(tile_ids(1, flat.shape), FIELDS) == 0

    def whole(array):
        array = jnp.sum(jnp.where(own, array, 0.0), axis=0, keepdims=True)
        return jnp.sum(array, axis=1, keepdims=True)

    norm, energy = whole(norm), whole(energy)
    alpha = norm / energy
    away = alpha - near
    norm_next = whole(uu - away * (2.0 * uw - away * ww))
    energy_next = whole(uq - away * (cross - away * wq))
    beta = norm_next / norm
    step_size = norm_next / (energy_next - beta * norm_next / alpha)
    c0 = jnp.broadcast_to(alpha + step_size * beta + step_size, (SUB, depth))
    c1 = jnp.broadcast_to(step_size * alpha, (SUB, depth))
    c2 = jnp.broadcast_to(alpha + step_size * (1.0 + beta), (SUB, depth))

    def copy(which, step):
        part = pl.ds(step * ROWS, ROWS)
        source, target = ((solution, solution_hbm), (residual, residual_hbm))[which]
        return pltpu.make_async_copy(source.at[:, part, :], target.at[:, part, :], sems.at[which, step])

    for step in range(rows // ROWS):
        for start in range(step * ROWS, (step + 1) * ROWS, SUB):
            here = pl.ds(start, SUB)
            for layer in range(layers):
                v = b[layer, here, :]
                if layer < split:
                    s = image_low[layer, here, :]
                elif start == 0:
                    s = image_ends[layer - split, :SUB, :]
                elif start == rows - SUB:
                    s = image_ends[layer - split, SUB:, :]
                else:
                    s = image_high[layer - split, here, :]
                if layer == 0:
                    w = s_first[here, :] + recv[here, :]
                    s = s + (recv_next[here, :] + own_next[here, :])
                elif layer < layers - 1:
                    w = s_mid[layer - 1, here, :]
                else:
                    w = w_last[here, :]
                    s = s + penalty * jump_next[here, :]
                solution[layer, here, :] = c0 * v - c1 * w
                residual[layer, here, :] = v - c2 * w + c1 * s
        for side, last_step in enumerate((0, rows // ROWS - 1)):
            if step == last_step:
                place = side * (rows - 1)
                residual[0, place : place + 1, :] += c1[0:1, :] * recv_next[rows + side : rows + side + 1, :]
                for layer in range(split, layers):
                    spot = side * (layers - split) + layer - split
                    residual[layer, place : place + 1, :] += c1[0:1, :] * edge_high[spot : spot + 1, :]
        for which in range(2):
            copy(which, step).start()
    for step in range(rows // ROWS):
        for which in range(2):
            copy(which, step).wait()


SMEM = pl.BlockSpec(memory_space=pltpu.SMEM)
VMEM = pl.BlockSpec(memory_space=pltpu.VMEM)
HBM = pl.BlockSpec(memory_space=pltpu.HBM)


def held(*dims, dtype=F32):
    return pltpu.VMEM(dims, dtype)


def near_core(*arrays):
    return [pltpu.with_memory_space_constraint(array, pltpu.VMEM) for array in arrays]


def in_hbm(*arrays):
    return [pltpu.with_memory_space_constraint(array, pltpu.HBM) for array in arrays]


def scaled(estimate, by):
    return pl.CostEstimate(
        flops=int(estimate.flops * by) + 1, bytes_accessed=int(estimate.bytes_accessed * by) + 1, transcendentals=0
    )


def params(mib):
    return pltpu.CompilerParams(vmem_limit_bytes=mib * 1024 * 1024)


def shifted(array, axis, by):
    size = lax.axis_size(axis)
    return lax.ppermute(array, axis, [(i, i + by) for i in range(size) if 0 <= i + by < size])


def gather_rows(table):
    subs, blks = lax.axis_size("sub"), lax.axis_size("blk")
    steps = [(0, 1)]
    reach = 2
    while reach < blks:
        steps.append((0, reach + 1))
        reach *= 2
    reach = subs // 2
    while reach > 0:
        steps.append((reach, 1))
        reach //= 2
    for by_sub, by_blk in steps:
        pairs = [(s * blks + t, (s ^ by_sub) * blks + (t ^ by_blk)) for s in range(subs) for t in range(blks)]
        table = table + lax.ppermute(table, ("sub", "blk"), pairs)
    return table


def body(right_side, trans_x, trans_y, trans_z, storage, pair_perm, pair_type, pair_count, proj):
    layers, rows, depth = right_side.shape
    blocks, width, kinds = pair_perm.shape[2], proj.shape[1], proj.shape[0]
    subs, blks = lax.axis_size("sub"), lax.axis_size("blk")
    steps = rows // ROWS
    cells = layers * rows * depth
    cost = lambda flops, size: pl.CostEstimate(flops=int(flops), bytes_accessed=int(size), transcendentals=0)

    (face,) = pl.pallas_call(
        pack_kernel,
        in_specs=[HBM, HBM],
        out_specs=[VMEM],
        out_shape=[held(rows + SUB, depth)],
        scratch_shapes=[pltpu.SemaphoreType.DMA((2,))],
        compiler_params=params(2),
        cost_estimate=scaled(cost(0, 4 * rows * depth), 100),
        name="pack",
    )(*in_hbm(right_side, trans_y))
    face_right = shifted(face, "sub", -1)

    b, tx, ty, tz, st, face_next, s_first, s_mid, s_last, first_sums, picks, puts, codes, code_row, proj_t, proj_n = pl.pallas_call(
        first_kernel,
        in_specs=[SMEM] + [VMEM] * 3 + [HBM] * 5,
        out_specs=[VMEM] * 16,
        out_shape=[held(layers, rows, depth)] * 5
        + [
            held(rows, depth), held(rows, depth), held(layers - 2, rows, depth), held(rows, depth), held(SUB, LANES),
            held(blocks, blocks, dtype=BF16), held(blocks, blocks, dtype=BF16), held(blocks, width, dtype=jnp.int32), held(1, blocks),
            held(kinds * width, 2 * width, dtype=BF16), held(kinds * width, 2 * width, dtype=BF16),
        ],
        scratch_shapes=[pltpu.VMEM((2, SUB, LANES), F32), pltpu.SemaphoreType.DMA((5, steps))],
        compiler_params=params(16),
        cost_estimate=scaled(cost(20 * cells, 24 * cells), 1),
        name="stencil_first",
    )(
        pair_count, pair_perm, pair_type, proj,
        *in_hbm(right_side, trans_x, trans_y, trans_z, storage),
    )
    face_right_next = shifted(face_next, "sub", -1)

    split = layers // 2
    (image_low,) = pl.pallas_call(
        second_low_kernel,
        in_specs=[VMEM] * 6,
        out_specs=[VMEM],
        out_shape=[held(split, rows, depth)],
        compiler_params=params(8),
        cost_estimate=scaled(cost(20 * cells, 15 * cells), 0),
        name="stencil_second_low",
    )(*near_core(s_first, s_mid, tx, ty, tz, st))

    mortar_cost = cost(4 * blocks * blocks * width + 6 * kinds * blocks * width * width, 14 * rows * depth)
    w_last, jump, jump_sums = pl.pallas_call(
        jump_first_kernel,
        in_specs=[VMEM] * 7,
        out_specs=[VMEM] * 3,
        out_shape=[held(rows, depth), held(rows, depth), held(SUB, LANES)],
        compiler_params=params(16),
        cost_estimate=scaled(mortar_cost, 100),
        name="jump_first",
    )(*near_core(image_low, b, face_right, s_last, picks, codes, proj_t))
    (kinds_by_block,) = pl.pallas_call(
        kinds_kernel,
        in_specs=[VMEM] * 2,
        out_specs=[VMEM],
        out_shape=[held(SUB, depth)],
        compiler_params=params(8),
        cost_estimate=scaled(cost(16 * blocks * blocks, 2 * blocks * blocks), 3),
        name="kinds",
    )(*near_core(code_row, picks))
    (back,) = pl.pallas_call(
        back_first_kernel,
        in_specs=[VMEM] * 5,
        out_specs=[VMEM],
        out_shape=[held(rows + SUB, depth)],
        compiler_params=params(16),
        cost_estimate=scaled(mortar_cost, 1),
        name="back_first",
    )(*near_core(jump, kinds_by_block, puts, codes, proj_n))
    recv = shifted(back, "sub", 1)

    split = layers // 2
    image_high, high_sums = pl.pallas_call(
        second_high_kernel,
        in_specs=[VMEM] * 11,
        out_specs=[VMEM] * 2,
        out_shape=[held(layers - split, rows, depth), held(SUB, LANES)],
        scratch_shapes=[pltpu.VMEM((6, SUB, LANES), F32)],
        compiler_params=params(8),
        cost_estimate=scaled(cost(20 * cells, 15 * cells), 10),
        name="stencil_second_high",
    )(*near_core(back, first_sums, jump_sums, b, s_mid, s_last, w_last, tx, ty, tz, st))
    up_out, down_out = pl.pallas_call(
        rows_kernel,
        in_specs=[VMEM] * 7,
        out_specs=[VMEM] * 2,
        out_shape=[held(3 * layers + 3, depth), held(2 * layers + 2, depth)],
        compiler_params=params(2),
        cost_estimate=scaled(cost(0, 64 * depth), 1),
        name="rows",
    )(*near_core(face_right, b, ty, s_first, s_mid, w_last, back))
    up = shifted(up_out, "blk", 1)
    down = shifted(down_out, "blk", -1)
    s_first, s_mid, s_last, w_last, image_low, edge_sums, image_ends, ends_sums, right_edges, missing, w_up, w_down = pl.pallas_call(
        edge_kernel,
        in_specs=[VMEM] * 15,
        out_specs=[VMEM] * 12,
        out_shape=[held(rows, depth), held(layers - 2, rows, depth), held(rows, depth), held(rows, depth)]
        + [held(split, rows, depth), held(SUB, LANES), held(layers - split, 2 * SUB, depth), held(SUB, LANES)]
        + [held(2, depth), held(2, depth), held(layers, depth), held(layers, depth)],
        input_output_aliases={10: 0, 11: 1, 12: 2, 13: 3, 14: 4},
        compiler_params=params(4),
        cost_estimate=scaled(cost(320 * depth, 640 * depth), 3),
        name="edges_first",
    )(
        *near_core(
            first_sums, high_sums, b, face_right, up, down, tx, ty, tz, st, s_first, s_mid, s_last, w_last, image_low,
        )
    )

    jump_next, second_sums = pl.pallas_call(
        jump_second_kernel,
        in_specs=[VMEM] * 11,
        out_specs=[VMEM] * 2,
        out_shape=[held(rows, depth), held(SUB, LANES)],
        scratch_shapes=[pltpu.VMEM((rows, depth), F32)],
        compiler_params=params(16),
        cost_estimate=scaled(mortar_cost, 0.3),
        name="jump_second",
    )(
        *near_core(
            high_sums, w_last, jump, face_right, face_right_next, right_edges, back, missing, picks, codes, proj_t,
        )
    )
    (back_next,) = pl.pallas_call(
        back_second_kernel,
        in_specs=[VMEM] * 5,
        out_specs=[VMEM],
        out_shape=[held(rows + SUB, depth)],
        compiler_params=params(16),
        cost_estimate=scaled(mortar_cost, 0.3),
        name="back_second",
    )(*near_core(w_last, missing, puts, codes, proj_n))

    recv_next = shifted(back_next, "sub", 1)

    count = subs * blks
    image_low, edge_high, table = pl.pallas_call(
        second_added_kernel,
        in_specs=[VMEM] * 18,
        out_specs=[VMEM] * 3,
        out_shape=[
            held(split, rows, depth), held(2 * (layers - split), depth), held(-(-count * FIELDS // LANES), LANES),
        ],
        input_output_aliases={17: 0},
        scratch_shapes=[pltpu.VMEM((6, SUB, LANES), F32)],
        compiler_params=params(8),
        cost_estimate=scaled(cost(20 * cells, 15 * cells), 0.3),
        name="stencil_second_added",
    )(
        *near_core(
            edge_sums, jump_sums, high_sums, ends_sums, second_sums, b, s_first, s_mid, w_last, recv,
            w_up, w_down, up, tx, ty, tz, st, image_low,
        )
    )
    (own_next,) = pl.pallas_call(
        own_second_kernel,
        in_specs=[VMEM] * 4,
        out_specs=[VMEM],
        out_shape=[held(rows, depth)],
        compiler_params=params(16),
        cost_estimate=scaled(mortar_cost, 1),
        name="own_second",
    )(*near_core(s_first, recv, proj_t, proj_n))
    tables = gather_rows(table)

    return pl.pallas_call(
        final_kernel,
        in_specs=[VMEM] * 13,
        out_specs=[HBM] * 2,
        out_shape=[jax.ShapeDtypeStruct((layers, rows, depth), F32)] * 2,
        scratch_shapes=[pltpu.VMEM((layers, rows, depth), F32)] * 2 + [pltpu.SemaphoreType.DMA((2, steps))],
        compiler_params=params(8),
        cost_estimate=scaled(cost(8 * cells, 22 * cells), 1),
        name="final_update",
    )(*near_core(tables, b, s_first, s_mid, w_last, recv, image_low, image_high, image_ends, edge_high, jump_next, recv_next, own_next))


def solution(mesh):
    cells = P("sub", "blk", None)
    in_specs = (cells,) * 7 + (P("sub", "blk"), P())
    return jax.shard_map(body, mesh=mesh, in_specs=in_specs, out_specs=(cells, cells), check_vma=False)
```

```python
import jax
import jax.numpy as jnp
from jax import lax
from jax.experimental import pallas as pl
from jax.experimental.pallas import tpu as pltpu
from jax.sharding import PartitionSpec as P

ROWS = 32
FIELDS = 16
SUB = 8
LANES = 128
F32 = jnp.float32
BF16 = jnp.bfloat16
penalty = 4.0


def tile_ids(dim, shape):
    return lax.broadcasted_iota(jnp.int32, shape, dim)


def as_tile(scalars):
    lane = tile_ids(1, (SUB, LANES))
    tile = jnp.zeros((SUB, LANES), F32)
    for place, value in enumerate(scalars):
        tile = jnp.where(lane == place, value, tile)
    return tile


def from_tile(tile, place):
    pick = (tile_ids(1, tile.shape) == place) & (tile_ids(0, tile.shape) == 0)
    return jnp.sum(jnp.where(pick, tile, 0.0))


def fold(array):
    parts = [array[:, place : place + LANES] for place in range(0, array.shape[1], LANES)]
    while len(parts) > 1:
        parts = [one + other for one, other in zip(parts[::2], parts[1::2])]
    return parts[0]


def at(array, layers, start):
    return [array[layer, pl.ds(start, SUB), :] for layer in range(layers)]


def stencil(values, after, tx, ty, tz, st, carry, below=None, above=None):
    shape = values[0].shape
    row = tile_ids(0, shape)
    last_z = tile_ids(1, shape) == shape[1] - 1
    results, carries = [], []
    flux_x = None if below is None else below[1] * (below[0] - values[0])
    for layer, value in enumerate(values):
        follow = value if after is None else pltpu.roll(after[layer], SUB - 1, 0)
        follow = jnp.where(row == SUB - 1, follow, pltpu.roll(value, SUB - 1, 0))
        flux_y = ty[layer] * (value - follow)
        rolled = pltpu.roll(flux_y, 1, 0)
        carries.append(rolled)
        flux_z = jnp.where(last_z, 0.0, tz[layer] * (value - pltpu.roll(value, shape[1] - 1, 1)))
        result = st[layer] * value + (flux_y - jnp.where(row == 0, carry[layer], rolled))
        result = result + (flux_z - pltpu.roll(flux_z, 1, 1))
        if flux_x is not None:
            result = result - flux_x
        next_x = values[layer + 1] if layer < len(values) - 1 else above
        flux_x = None
        if next_x is not None:
            flux_x = tx[layer] * (value - next_x)
            result = result + flux_x
        results.append(result)
    return results, carries


def at_last_block():
    return lax.axis_index("blk") == lax.axis_size("blk") - 1


def edge_terms(before, first, last, beyond, ty_before, ty_last):
    low = ty_before * (first - before)
    high = jnp.where(at_last_block(), 0.0, ty_last * (last - beyond))
    return low, high


def pack_kernel(b_hbm, ty_hbm, face, sems):
    rows = b_hbm.shape[1]
    copies = [
        pltpu.make_async_copy(b_hbm.at[0], face.at[pl.ds(0, rows), :], sems.at[0]),
        pltpu.make_async_copy(ty_hbm.at[0, pl.ds(rows - SUB, SUB), :], face.at[pl.ds(rows, SUB), :], sems.at[1]),
    ]
    for copy in copies:
        copy.start()
    for copy in copies:
        copy.wait()


def two_parts(array):
    high = array.astype(BF16)
    return high, (array - high.astype(F32)).astype(BF16)


def prepare_pairs(perm, kind, count, proj, rows, groups, picks, puts, codes, code_row, proj_t, proj_n):
    kinds, width, _ = proj.shape
    blocks = rows * groups
    lane = tile_ids(1, (1, blocks))
    target = lax.rem(perm, groups) * rows + lax.div(perm, groups)
    shift = kinds.bit_length()
    keys = (target * (1 << shift) + jnp.where(lane < count, kind, kinds)).astype(F32)
    span = LANES // groups
    spread = tile_ids(1, (span, LANES)) - groups * tile_ids(0, (span, LANES))
    lanes = tile_ids(1, (rows, LANES))
    across = []
    for group in range(groups):
        column = jnp.concatenate(
            [
                jnp.sum(jnp.where(spread == group, keys[:, place * LANES : (place + 1) * LANES], 0.0), 1, keepdims=True)
                for place in range(blocks // LANES)
            ],
            axis=0,
        ).astype(jnp.int32)
        column = jnp.broadcast_to(column, (rows, LANES))
        here = pl.ds(group * rows, rows)
        for place in range(rows // LANES):
            turned = jnp.transpose(column[place * LANES : (place + 1) * LANES].astype(F32))
            across.append(turned[0:1, :].astype(jnp.int32))
        codes[here, :] = column & ((1 << shift) - 1)
        column = column >> shift
        for place in range(blocks // LANES):
            picks[here, pl.ds(place * LANES, LANES)] = jnp.where(column == lanes + place * LANES, 1.0, 0.0).astype(BF16)
    across = jnp.concatenate(across, axis=1)
    code_row[...] = (kinds - (across & ((1 << shift) - 1))).astype(F32)
    across = across >> shift
    down = tile_ids(0, (rows, blocks))
    for group in range(groups):
        puts[pl.ds(group * rows, rows), :] = jnp.where(across == down + group * rows, 1.0, 0.0).astype(BF16)
    for kind in range(kinds):
        here = pl.ds(kind * width, width)
        proj_t[here, :] = jnp.concatenate(two_parts(jnp.transpose(proj[kind])), axis=1)
        proj_n[here, :] = jnp.concatenate(two_parts(proj[kind]), axis=1)


def first_kernel(
    count, perm, kind, proj, b_hbm, tx_hbm, ty_hbm, tz_hbm, st_hbm,
    b, tx, ty, tz, st, face_next, s_first, s_mid, s_last, sums, picks, puts, codes, code_row, proj_t, proj_n, total, sems,
):
    layers, rows, depth = b.shape
    steps = rows // ROWS
    sources, targets = (b_hbm, tx_hbm, ty_hbm, tz_hbm, st_hbm), (b, tx, ty, tz, st)

    def copy(which, step):
        part = pl.ds(step * ROWS, ROWS)
        return pltpu.make_async_copy(
            sources[which].at[:, part, :], targets[which].at[:, part, :], sems.at[which, step]
        )

    for step in range(steps):
        for which in range(len(sources)):
            copy(which, step).start()
    width = proj.shape[1]
    prepare_pairs(
        perm[0], kind[0], count[0, 0], proj, rows, depth // width, picks, puts, codes, code_row, proj_t, proj_n
    )
    total[...] = jnp.zeros_like(total)
    copy(0, 0).wait()

    def chunk(start, after, carry):
        values = at(b, layers, start)
        results, carry = stencil(values, after, *[at(array, layers, start) for array in (tx, ty, tz, st)], carry)
        here = pl.ds(start, SUB)
        squares, products = values[0] * values[0], values[0] * results[0]
        for layer in range(1, layers):
            squares = squares + values[layer] * values[layer]
            products = products + values[layer] * results[layer]
        total[0] += fold(squares)
        total[1] += fold(products)
        face_next[here, :] = results[0]
        s_first[here, :] = results[0]
        for layer in range(1, layers - 1):
            s_mid[layer - 1, here, :] = results[layer]
        s_last[here, :] = results[layers - 1]
        return carry

    carry = [jnp.zeros((SUB, depth), F32)] * layers
    for step in range(steps):
        for which in range(1, len(sources)):
            copy(which, step).wait()
        if step < steps - 1:
            copy(0, step + 1).wait()
        for start in range(step * ROWS, (step + 1) * ROWS, SUB):
            carry = chunk(start, None if start == rows - SUB else at(b, layers, start + SUB), carry)
    sums[...] = as_tile([jnp.sum(total[0]), jnp.sum(total[1])])


def up_places(layers):
    return 0, layers, 2 * layers, 3 * layers, 3 * layers + 1, 3 * layers + 2


def edge_kernel(
    sums_in, near_sums, b, right, up, down, tx, ty, tz, st, s_first_in, s_mid_in, s_last_in, w_last_in, image_low_in,
    s_first, s_mid, s_last, w_last, image_low, sums, image_ends, ends_sums, right_edges, missing, w_up, w_down,
):
    layers, rows, depth = b.shape
    at_b, at_ty, at_w, at_back, at_right, at_right_ty = up_places(layers)
    product = 0.0
    for layer in range(layers):
        first, last = b[layer, 0:1, :], b[layer, rows - 1 :, :]
        low, high = edge_terms(
            up[at_b + layer : at_b + layer + 1, :], first, last, down[layer : layer + 1, :],
            up[at_ty + layer : at_ty + layer + 1, :], ty[layer, rows - 1 :, :],
        )
        pairs = [(s_first_in, s_first)] if layer == 0 else [(s_last_in, s_last), (w_last_in, w_last)]
        if 0 < layer < layers - 1:
            pairs = [(s_mid_in.at[layer - 1], s_mid.at[layer - 1])]
        for source, target in pairs:
            target[0:1, :] = source[0:1, :] + low
            target[rows - 1 :, :] = source[rows - 1 :, :] + high
        product = product + first * low + last * high
        w_up[layer : layer + 1, :] = up[at_w + layer : at_w + layer + 1, :] - low
        w_down[layer : layer + 1, :] = down[layers + layer : layers + layer + 1, :] - high
    sums[...] = sums_in[...] + as_tile([0.0, jnp.sum(product)])
    low, high = edge_terms(
        up[at_right : at_right + 1, :], right[0:1, :], right[rows - 1 : rows, :], down[2 * layers + 1 :, :],
        up[at_right_ty : at_right_ty + 1, :], right[rows + SUB - 1 :, :],
    )
    right_edges[0:1, :] = low
    right_edges[1:2, :] = high
    missing[0:1, :] = -up[at_right_ty : at_right_ty + 1, :] * up[at_back : at_back + 1, :]
    missing[1:2, :] = jnp.where(
        at_last_block(), 0.0, -right[rows + SUB - 1 :, :] * down[2 * layers : 2 * layers + 1, :]
    )
    near = from_tile(near_sums[...], 2)
    own, read, plain = high_layers(layers, s_mid, s_last, w_last)
    terms = None
    for place, start in enumerate((0, rows - SUB)):
        values = read(start)
        if place == 0:
            after, carry = read(SUB), [jnp.zeros((SUB, depth), F32)] * len(own)
        else:
            after, carry = None, flux_from(start - SUB, own, read, 1, ty)
        new, _ = chunk_sums(
            start, values, after, carry, own, near, b, plain, tx, ty, tz, st, image_ends, place * SUB
        )
        terms = new if terms is None else [old + more for old, more in zip(terms, new)]
    ends_sums[...] = as_tile([0.0] * 3 + [jnp.sum(term) for term in terms])
    own, read = low_layers(layers, s_first, s_mid)
    zero = [jnp.zeros((SUB, depth), F32)] * len(own)
    low_chunk(0, read(0), read(SUB), zero, own, tx, ty, tz, st, image_low)
    carry = flux_from(rows - 2 * SUB, own, read, 0, ty)
    low_chunk(rows - SUB, read(rows - SUB), None, carry, own, tx, ty, tz, st, image_low)


def high_layers(layers, s_mid, s_last, w_last):
    split = layers // 2

    def read(start):
        here = pl.ds(start, SUB)
        return [s_mid[layer - 1, here, :] for layer in range(split - 1, layers - 1)] + [w_last[here, :]]

    def plain(layer, here):
        return s_last[here, :] if layer == layers - 1 else s_mid[layer - 1, here, :]

    return list(range(split, layers)), read, plain


def flux_from(start, own, read, skip, ty):
    row = None
    carry = []
    for layer, value, after in zip(own, read(start)[skip:], read(start + SUB)[skip:]):
        row = tile_ids(0, value.shape)
        follow = jnp.where(row == SUB - 1, pltpu.roll(after, SUB - 1, 0), pltpu.roll(value, SUB - 1, 0))
        carry.append(pltpu.roll(ty[layer, pl.ds(start, SUB), :] * (value - follow), 1, 0))
    return carry


def chunk_sums(start, values, after, carry, own, near, b, plain, tx, ty, tz, st, image, target, summed=None):
    layers = b.shape[0]
    here = pl.ds(start, SUB)
    below = (values[0], tx[own[0] - 1, here, :]) if own[0] > 0 else None
    above = values[-1] if own[-1] < layers - 1 else None
    skip = 0 if below is None else 1
    mine = values[skip : skip + len(own)]
    results, carry = stencil(
        mine, None if after is None else after[skip : skip + len(own)],
        *[[array[layer, here, :] for layer in own] for array in (tx, ty, tz, st)], carry, below, above,
    )
    terms = None
    for place, layer in enumerate(own):
        w, s = mine[place], results[place]
        image[place, pl.ds(target, SUB), :] = s
        if summed is not None and layer not in summed:
            continue
        u = b[layer, here, :] - near * w
        q = plain(layer, here) - near * s
        new = [fold(term) for term in (u * u, u * w, w * w, u * q, u * s + w * q, w * s)]
        terms = new if terms is None else [old + more for old, more in zip(terms, new)]
    return terms, carry


def mm(left, right):
    return lax.dot_general(left, right, (((1,), (0,)), ((), ())), preferred_element_type=F32)


def by_kind(codes, array, kinds):
    zero = jnp.zeros_like(array)
    return jnp.concatenate([jnp.where(codes == kind, array, zero) for kind in range(kinds)], axis=1)


def apply_proj(codes, high, low, proj, kinds, width):
    both = mm(by_kind(codes, high, kinds), proj[...])
    return both[:, :width] + both[:, width:] + mm(by_kind(codes, low, kinds), proj[:, :width])


def take_jump(group, faces, last, picks, codes_col, proj_t):
    width = proj_t.shape[1] // 2
    kinds = proj_t.shape[0] // width
    here = pl.ds(group * last.shape[0], last.shape[0])
    codes = codes_col[here, :]
    taken = mm(picks[here, :], faces)
    projected = apply_proj(codes, taken[:, :width].astype(BF16), taken[:, width:].astype(BF16), proj_t, kinds, width)
    return jnp.where(codes < kinds, last - projected, 0.0)


def turn_back(group, jump, codes_col, proj_n):
    width = proj_n.shape[1] // 2
    kinds = proj_n.shape[0] // width
    scale = jnp.where(lax.axis_index("sub") < lax.axis_size("sub") - 1, -penalty, 0.0)
    codes = codes_col[pl.ds(group * jump.shape[0], jump.shape[0]), :]
    return jnp.concatenate(two_parts(scale * apply_proj(codes, *two_parts(jump), proj_n, kinds, width)), axis=1)


def put_back(group, backs, puts, rows):
    width = backs.shape[1] // 2
    placed = mm(puts[pl.ds(group * rows, rows), :], backs)
    return placed[:, :width] + placed[:, width:]


def stack_parts(parts):
    return jnp.concatenate(two_parts(jnp.concatenate(parts, axis=0)), axis=1)


def jump_first_kernel(earlier, b, right, s_last, picks, codes, proj_t, w_last, jump_face, sums):
    width = proj_t.shape[1] // 2
    layers, rows, depth = b.shape
    parts = [pl.ds(group * width, width) for group in range(depth // width)]
    faces = stack_parts([right[:rows, part] for part in parts])
    square = jnp.zeros((rows, width), F32)
    for group, part in enumerate(parts):
        jump = take_jump(group, faces, b[layers - 1, :, part], picks, codes, proj_t)
        square = square + jump * jump
        jump_face[:, part] = jump
        w_last[:, part] = s_last[:, part] + penalty * jump
    sums[...] = as_tile([jnp.sum(square)])


def kinds_kernel(code_row, picks, kinds_by_block):
    depth = kinds_by_block.shape[1]
    row = mm(jnp.broadcast_to(code_row[...], (2 * SUB, code_row.shape[1])).astype(BF16), picks[...])
    kinds_by_block[...] = jnp.zeros_like(kinds_by_block)
    for place in range(row.shape[1] // depth):
        kinds_by_block[place : place + 1, :] = row[0:1, place * depth : (place + 1) * depth]


def rows_kernel(right, b, ty, s_first, s_mid, w_last, back, up, down):
    layers, rows, _ = b.shape
    at_b, at_ty, at_w, at_back, at_right, at_right_ty = up_places(layers)
    end = pl.ds(rows - 1, 1)
    for layer in range(layers):
        image = s_first if layer == 0 else w_last if layer == layers - 1 else s_mid.at[layer - 1]
        up[at_b + layer : at_b + layer + 1, :] = b[layer, end, :]
        up[at_ty + layer : at_ty + layer + 1, :] = ty[layer, end, :]
        up[at_w + layer : at_w + layer + 1, :] = image[end, :]
        down[layer : layer + 1, :] = b[layer, 0:1, :]
        down[layers + layer : layers + layer + 1, :] = image[0:1, :]
    up[at_back : at_back + 1, :] = back[end, :]
    up[at_right : at_right + 1, :] = right[end, :]
    up[at_right_ty : at_right_ty + 1, :] = right[rows + SUB - 1 :, :]
    down[2 * layers : 2 * layers + 1, :] = back[0:1, :]
    down[2 * layers + 1 : 2 * layers + 2, :] = right[0:1, :]


def jump_second_kernel(
    near_sums, w_last, jump, right_before, right, right_edges, back_before, missing, picks, codes, proj_t,
    jump_next, sums, field,
):
    width = proj_t.shape[1] // 2
    rows, depth = right.shape
    parts = [pl.ds(group * width, width) for group in range(depth // width)]
    near = from_tile(near_sums[...], 2)
    field[...] = right[...] + back_before[:rows, :]
    field[0:1, :] += right_edges[0:1, :]
    field[rows - 1 :, :] += right_edges[1:2, :]
    faces = stack_parts([field[:, part] for part in parts])
    totals = [jnp.zeros((rows, width), F32)] * 3
    for group, part in enumerate(parts):
        later = take_jump(group, faces, w_last[:, part], picks, codes, proj_t)
        jump_next[:, part] = later
        close = jump[:, part] - near * later
        totals = [total + new for total, new in zip(totals, (close * close, close * later, later * later))]
    found = [jnp.sum(total) for total in totals]
    found = [penalty * found[0], 2.0 * penalty * found[1], penalty * found[2]]
    extra = [0.0] * 3
    for side, place in enumerate((0, rows - 1)):
        s = missing[side : side + 1, :]
        w = field[place : place + 1, :]
        u = right_before[place : place + 1, :] - near * w
        extra = [old + more for old, more in zip(extra, [-near * u * s, u * s - near * w * s, w * s])]
    sums[...] = as_tile([0.0] * 6 + [old + jnp.sum(more) for old, more in zip(found, extra)])


def back_first_kernel(jump, kinds_by_block, puts, codes, proj_n, back):
    rows = jump.shape[0]
    back_kernel(jump, puts, codes, proj_n, back)
    back[rows:, :] = kinds_by_block[...]


def back_second_kernel(w_last, missing, puts, codes, proj_n, back):
    rows = w_last.shape[0]
    back_kernel(w_last, puts, codes, proj_n, back)
    back[rows : rows + 2, :] = missing[...]


def own_second_kernel(s_first, recv, proj_t, proj_n, own):
    rows, depth = own.shape
    width = proj_t.shape[1] // 2
    kinds = proj_t.shape[0] // width
    for group in range(depth // width):
        part = pl.ds(group * width, width)
        codes = []
        for place in range(rows // LANES):
            start = group * rows + place * LANES
            row = recv[rows + start // depth : rows + start // depth + 1, start % depth : start % depth + LANES]
            codes.append(jnp.transpose(jnp.broadcast_to(row, (LANES, LANES))))
        codes = kinds - jnp.concatenate(codes, axis=0).astype(jnp.int32)
        field = s_first[:, part] + recv[:rows, part]
        projected = apply_proj(codes, *two_parts(field), proj_t, kinds, width)
        own[:, part] = penalty * apply_proj(codes, *two_parts(projected), proj_n, kinds, width)


def hold_kernel(later, back_in, back):
    back[back.shape[0] - SUB + 2 :, :] = jnp.zeros((SUB - 2, back.shape[1]), F32)


def back_kernel(jump_next, puts, codes, proj_n, back):
    width = proj_n.shape[1] // 2
    rows, depth = jump_next.shape
    parts = [pl.ds(group * width, width) for group in range(depth // width)]
    backs = [turn_back(group, jump_next[:, part], codes, proj_n) for group, part in enumerate(parts)]
    backs = jnp.concatenate(backs, axis=0)
    for group, part in enumerate(parts):
        back[:rows, part] = put_back(group, backs, puts, rows)


def stencil_sums(read, own, near, b, plain, tx, ty, tz, st, image, total, inner, summed=None):
    layers, rows, depth = b.shape
    total[...] = jnp.zeros_like(total)
    skip = 1 if own[0] > 0 else 0

    def several(start, count, carry, at_end=False):
        starts = [pl.multiple_of(start + SUB * place, SUB) for place in range(count + 1)]
        values = [read(place) for place in starts[:-1]] + [None if at_end else read(starts[-1])]
        terms = None
        for place in range(count):
            new, carry = chunk_sums(
                starts[place], values[place], values[place + 1], carry, own, near, b, plain, tx, ty, tz, st, image,
                starts[place], summed,
            )
            terms = new if terms is None else [old + more for old, more in zip(terms, new)]
        for place, term in enumerate(terms):
            total[place] += term
        return carry

    group = 2
    if inner:
        begin, count, carry = SUB, (rows // SUB - 2) // group, flux_from(0, own, read, skip, ty)
    else:
        begin, count, carry = 0, rows // (group * SUB) - 1, [jnp.zeros((SUB, depth), F32)] * len(own)
    carry = lax.fori_loop(
        0, count,
        lambda index, carry: tuple(
            several(pl.multiple_of(begin + index * group * SUB, SUB), group, list(carry))
        ),
        tuple(carry),
    )
    if not inner:
        several(rows - group * SUB, group, list(carry), True)
    return [jnp.sum(total[place]) for place in range(total.shape[0])]


def second_high_kernel(later, first_sums, jump_sums, b, s_mid, s_last, w_last, tx, ty, tz, st, image, sums, total):
    norm = from_tile(first_sums[...], 0)
    energy = from_tile(first_sums[...], 1) + penalty * from_tile(jump_sums[...], 0)
    safe = energy > 0.01 * norm
    ratio = jnp.full((SUB, LANES), norm, F32) / jnp.full((SUB, LANES), jnp.where(safe, energy, 1.0), F32)
    near = jnp.where(safe, jnp.max(ratio), 0.0)
    own, read, plain = high_layers(b.shape[0], s_mid, s_last, w_last)
    found = stencil_sums(read, own, near, b, plain, tx, ty, tz, st, image, total, True)
    sums[...] = as_tile([0.0, 0.0, near] + found)


def low_layers(layers, s_first, s_mid):
    split = layers // 2

    def read(start):
        here = pl.ds(start, SUB)
        return [s_first[here, :]] + [s_mid[layer - 1, here, :] for layer in range(1, split + 1)]

    return list(range(split)), read


def low_chunk(start, values, after, carry, own, tx, ty, tz, st, image):
    here = pl.ds(start, SUB)
    results, carry = stencil(
        values[:-1], None if after is None else after[:-1],
        *[[array[layer, here, :] for layer in own] for array in (tx, ty, tz, st)], carry, None, values[-1],
    )
    for layer in own:
        image[layer, here, :] = results[layer]
    return carry


def second_low_kernel(s_first, s_mid, tx, ty, tz, st, image):
    layers, rows = tx.shape[:2]
    own, read = low_layers(layers, s_first, s_mid)
    group = 3

    def several(index, carry):
        start = pl.multiple_of(SUB + index * group * SUB, SUB)
        starts = [pl.multiple_of(start + SUB * place, SUB) for place in range(group + 1)]
        values = [read(place) for place in starts]
        carry = list(carry)
        for place in range(group):
            carry = low_chunk(starts[place], values[place], values[place + 1], carry, own, tx, ty, tz, st, image)
        return tuple(carry)

    lax.fori_loop(0, (rows // SUB - 2) // group, several, tuple(flux_from(0, own, read, 0, ty)))


def second_added_kernel(
    first_sums, jump_sums, high_sums, ends_sums, second_sums, b, s_first, s_mid, w_last, recv,
    w_up, w_down, up, tx, ty, tz, st, image_in, image, edge_high, table, total,
):
    layers, rows, depth = b.shape
    split = layers // 2
    near = from_tile(high_sums[...], 2)
    total[...] = jnp.zeros_like(total)
    first, second = 0, 1

    def several(start, count, carry, at_end=False):
        starts = [pl.multiple_of(start + SUB * place, SUB) for place in range(count + 1)]
        added = [recv[pl.ds(place, SUB), :] for place in starts[:-1]]
        added.append(None if at_end else recv[pl.ds(starts[-1], SUB), :])
        terms = None
        for place in range(count):
            here = pl.ds(starts[place], SUB)
            e, t_x = added[place], tx[first, here, :]
            (s,), carry = stencil(
                [e], None if added[place + 1] is None else [added[place + 1]], [t_x], [ty[first, here, :]],
                [tz[first, here, :]], [st[first, here, :] + t_x], carry,
            )
            s = image_in[first, here, :] + s
            image[first, here, :] = s
            plain = s_first[here, :]
            w = plain + e
            u = b[first, here, :] - near * w
            q = plain - near * s
            new = [u * u, u * w, w * w, u * q, u * s + w * q, w * s]
            s = image_in[second, here, :] - t_x * e
            image[second, here, :] = s
            w = s_mid[second - 1, here, :]
            u = b[second, here, :] - near * w
            q = w - near * s
            more = [u * u, u * w, w * w, u * q, u * s + w * q, w * s]
            new = [fold(one + other) for one, other in zip(new, more)]
            terms = new if terms is None else [old + more for old, more in zip(terms, new)]
        for place, term in enumerate(terms):
            total[place] += term
        return carry

    group = 4
    carry = lax.fori_loop(
        0, rows // (group * SUB) - 1,
        lambda index, carry: several(pl.multiple_of(index * group * SUB, SUB), group, [carry])[0],
        jnp.zeros((SUB, depth), F32),
    )
    several(rows - group * SUB, group, [carry], True)
    found = [jnp.sum(total[place]) for place in range(total.shape[0])]

    def row(layer, place):
        here = pl.ds(place, 1)
        if layer == 0:
            return s_first[here, :] + recv[here, :]
        return w_last[here, :] if layer == layers - 1 else s_mid[layer - 1, here, :]

    extra = [jnp.zeros((1, depth), F32)] * 3
    for layer in range(layers):
        ends = row(layer, 0), row(layer, rows - 1)
        added = edge_terms(
            w_up[layer : layer + 1, :], *ends, w_down[layer : layer + 1, :],
            up[layers + layer : layers + layer + 1, :], ty[layer, rows - 1 :, :],
        )
        for side, (place, w, s) in enumerate(zip((0, rows - 1), ends, added)):
            u = b[layer, place : place + 1, :] - near * w
            extra = [old + more for old, more in zip(extra, [-near * u * s, u * s - near * w * s, w * s])]
            if layer < split:
                image[layer, place : place + 1, :] += s
            else:
                spot = side * (layers - split) + layer - split
                edge_high[spot : spot + 1, :] = s
    found[3:] = [old + jnp.sum(more) for old, more in zip(found[3:], extra)]
    norm = from_tile(first_sums[...], 0)
    energy = from_tile(first_sums[...], 1) + penalty * from_tile(jump_sums[...], 0)
    sums = high_sums[...] + ends_sums[...] + second_sums[...]
    sums = sums + as_tile([norm, energy, 0.0] + found)
    mine = lax.axis_index("sub") * lax.axis_size("blk") + lax.axis_index("blk")
    device = tile_ids(0, table.shape) * (LANES // FIELDS) + lax.div(tile_ids(1, table.shape), FIELDS)
    field = lax.rem(tile_ids(1, table.shape), FIELDS)
    filled = jnp.zeros(table.shape, F32)
    for place in range(9):
        filled = jnp.where((device == mine) & (field == place), jnp.sum(sums[0:1, place : place + 1]), filled)
    table[...] = filled


def add_kernel(earlier, one, other, both):
    both[...] = one[...] + other[...]


def final_kernel(
    tables, b, s_first, s_mid, w_last, recv, image_low, image_high, image_ends, edge_high, jump_next, recv_next, own_next, solution_hbm, residual_hbm,
    solution, residual, sems,
):
    layers, rows, depth = b.shape
    split = image_low.shape[0]
    flat = tables[...]
    norm, energy, near, uu, uw, ww, uq, cross, wq = [
        flat if place == 0 else pltpu.roll(flat, LANES - place, 1) for place in range(9)
    ]
    own = lax.rem(tile_ids(1, flat.shape), FIELDS) == 0

    def whole(array):
        array = jnp.sum(jnp.where(own, array, 0.0), axis=0, keepdims=True)
        return jnp.sum(array, axis=1, keepdims=True)

    norm, energy = whole(norm), whole(energy)
    alpha = norm / energy
    away = alpha - near
    norm_next = whole(uu - away * (2.0 * uw - away * ww))
    energy_next = whole(uq - away * (cross - away * wq))
    beta = norm_next / norm
    step_size = norm_next / (energy_next - beta * norm_next / alpha)
    c0 = jnp.broadcast_to(alpha + step_size * beta + step_size, (SUB, depth))
    c1 = jnp.broadcast_to(step_size * alpha, (SUB, depth))
    c2 = jnp.broadcast_to(alpha + step_size * (1.0 + beta), (SUB, depth))

    def copy(which, step):
        part = pl.ds(step * ROWS, ROWS)
        source, target = ((solution, solution_hbm), (residual, residual_hbm))[which]
        return pltpu.make_async_copy(source.at[:, part, :], target.at[:, part, :], sems.at[which, step])

    for step in range(rows // ROWS):
        for start in range(step * ROWS, (step + 1) * ROWS, SUB):
            here = pl.ds(start, SUB)
            for layer in range(layers):
                v = b[layer, here, :]
                if layer < split:
                    s = image_low[layer, here, :]
                elif start == 0:
                    s = image_ends[layer - split, :SUB, :]
                elif start == rows - SUB:
                    s = image_ends[layer - split, SUB:, :]
                else:
                    s = image_high[layer - split, here, :]
                if layer == 0:
                    w = s_first[here, :] + recv[here, :]
                    s = s + (recv_next[here, :] + own_next[here, :])
                elif layer < layers - 1:
                    w = s_mid[layer - 1, here, :]
                else:
                    w = w_last[here, :]
                    s = s + penalty * jump_next[here, :]
                solution[layer, here, :] = c0 * v - c1 * w
                residual[layer, here, :] = v - c2 * w + c1 * s
        for side, last_step in enumerate((0, rows // ROWS - 1)):
            if step == last_step:
                place = side * (rows - 1)
                residual[0, place : place + 1, :] += c1[0:1, :] * recv_next[rows + side : rows + side + 1, :]
                for layer in range(split, layers):
                    spot = side * (layers - split) + layer - split
                    residual[layer, place : place + 1, :] += c1[0:1, :] * edge_high[spot : spot + 1, :]
        for which in range(2):
            copy(which, step).start()
    for step in range(rows // ROWS):
        for which in range(2):
            copy(which, step).wait()


SMEM = pl.BlockSpec(memory_space=pltpu.SMEM)
VMEM = pl.BlockSpec(memory_space=pltpu.VMEM)
HBM = pl.BlockSpec(memory_space=pltpu.HBM)


def held(*dims, dtype=F32):
    return pltpu.VMEM(dims, dtype)


def near_core(*arrays):
    return [pltpu.with_memory_space_constraint(array, pltpu.VMEM) for array in arrays]


def in_hbm(*arrays):
    return [pltpu.with_memory_space_constraint(array, pltpu.HBM) for array in arrays]


def cost(flops, size):
    return pl.CostEstimate(flops=int(flops), bytes_accessed=int(size), transcendentals=0)


def params(mib):
    return pltpu.CompilerParams(vmem_limit_bytes=mib * 1024 * 1024)


def shifted(array, axis, by):
    size = lax.axis_size(axis)
    return lax.ppermute(array, axis, [(i, i + by) for i in range(size) if 0 <= i + by < size])


def gather_rows(table, own):
    subs, blks = lax.axis_size("sub"), lax.axis_size("blk")
    steps = [(0, 1)]
    reach = 2
    while reach < blks:
        steps.append((0, reach + 1))
        reach *= 2
    reach = subs // 2
    while reach > 0:
        steps.append((reach, 1))
        reach //= 2
    for place, (by_sub, by_blk) in enumerate(steps):
        pairs = [(s * blks + t, (s ^ by_sub) * blks + (t ^ by_blk)) for s in range(subs) for t in range(blks)]
        other = lax.ppermute(table, ("sub", "blk"), pairs)
        if place == 0:
            (table,) = pl.pallas_call(
                add_kernel,
                in_specs=[VMEM] * 3,
                out_specs=[VMEM],
                out_shape=[held(*table.shape)],
                compiler_params=params(2),
                cost_estimate=cost(table.size, 12 * table.size),
                name="add",
            )(*near_core(own, table, other))
        else:
            table = table + other
    return table


def body(right_side, trans_x, trans_y, trans_z, storage, pair_perm, pair_type, pair_count, proj):
    layers, rows, depth = right_side.shape
    blocks, width, kinds = pair_perm.shape[2], proj.shape[1], proj.shape[0]
    subs, blks = lax.axis_size("sub"), lax.axis_size("blk")
    steps = rows // ROWS
    cells = layers * rows * depth

    (face,) = pl.pallas_call(
        pack_kernel,
        in_specs=[HBM, HBM],
        out_specs=[VMEM],
        out_shape=[held(rows + SUB, depth)],
        scratch_shapes=[pltpu.SemaphoreType.DMA((2,))],
        compiler_params=params(2),
        cost_estimate=cost(0, 4 * rows * depth),
        name="pack",
    )(*in_hbm(right_side, trans_y))
    face_right = shifted(face, "sub", -1)

    b, tx, ty, tz, st, face_next, s_first, s_mid, s_last, first_sums, picks, puts, codes, code_row, proj_t, proj_n = pl.pallas_call(
        first_kernel,
        in_specs=[SMEM] + [VMEM] * 3 + [HBM] * 5,
        out_specs=[VMEM] * 16,
        out_shape=[held(layers, rows, depth)] * 5
        + [
            held(rows, depth), held(rows, depth), held(layers - 2, rows, depth), held(rows, depth), held(SUB, LANES),
            held(blocks, blocks, dtype=BF16), held(blocks, blocks, dtype=BF16), held(blocks, width, dtype=jnp.int32), held(1, blocks),
            held(kinds * width, 2 * width, dtype=BF16), held(kinds * width, 2 * width, dtype=BF16),
        ],
        scratch_shapes=[pltpu.VMEM((2, SUB, LANES), F32), pltpu.SemaphoreType.DMA((5, steps))],
        compiler_params=params(16),
        cost_estimate=cost(20 * cells, 24 * cells),
        name="stencil_first",
    )(
        pair_count, pair_perm, pair_type, proj,
        *in_hbm(right_side, trans_x, trans_y, trans_z, storage),
    )
    face_right_next = shifted(face_next, "sub", -1)

    split = layers // 2
    (image_low,) = pl.pallas_call(
        second_low_kernel,
        in_specs=[VMEM] * 6,
        out_specs=[VMEM],
        out_shape=[held(split, rows, depth)],
        compiler_params=params(8),
        cost_estimate=cost(20 * cells, 15 * cells),
        name="stencil_second_low",
    )(*near_core(s_first, s_mid, tx, ty, tz, st))

    mortar_cost = cost(4 * blocks * blocks * width + 6 * kinds * blocks * width * width, 14 * rows * depth)
    w_last, jump, jump_sums = pl.pallas_call(
        jump_first_kernel,
        in_specs=[VMEM] * 7,
        out_specs=[VMEM] * 3,
        out_shape=[held(rows, depth), held(rows, depth), held(SUB, LANES)],
        compiler_params=params(16),
        cost_estimate=mortar_cost,
        name="jump_first",
    )(*near_core(image_low, b, face_right, s_last, picks, codes, proj_t))
    (kinds_by_block,) = pl.pallas_call(
        kinds_kernel,
        in_specs=[VMEM] * 2,
        out_specs=[VMEM],
        out_shape=[held(SUB, depth)],
        compiler_params=params(8),
        cost_estimate=cost(16 * blocks * blocks, 2 * blocks * blocks),
        name="kinds",
    )(*near_core(code_row, picks))
    (back,) = pl.pallas_call(
        back_first_kernel,
        in_specs=[VMEM] * 5,
        out_specs=[VMEM],
        out_shape=[held(rows + SUB, depth)],
        compiler_params=params(16),
        cost_estimate=mortar_cost,
        name="back_first",
    )(*near_core(jump, kinds_by_block, puts, codes, proj_n))
    recv = shifted(back, "sub", 1)

    split = layers // 2
    image_high, high_sums = pl.pallas_call(
        second_high_kernel,
        in_specs=[VMEM] * 11,
        out_specs=[VMEM] * 2,
        out_shape=[held(layers - split, rows, depth), held(SUB, LANES)],
        scratch_shapes=[pltpu.VMEM((6, SUB, LANES), F32)],
        compiler_params=params(8),
        cost_estimate=cost(20 * cells, 15 * cells),
        name="stencil_second_high",
    )(*near_core(back, first_sums, jump_sums, b, s_mid, s_last, w_last, tx, ty, tz, st))
    up_out, down_out = pl.pallas_call(
        rows_kernel,
        in_specs=[VMEM] * 7,
        out_specs=[VMEM] * 2,
        out_shape=[held(3 * layers + 3, depth), held(2 * layers + 2, depth)],
        compiler_params=params(2),
        cost_estimate=cost(0, 64 * depth),
        name="rows",
    )(*near_core(face_right, b, ty, s_first, s_mid, w_last, back))
    up = shifted(up_out, "blk", 1)
    down = shifted(down_out, "blk", -1)
    s_first, s_mid, s_last, w_last, image_low, edge_sums, image_ends, ends_sums, right_edges, missing, w_up, w_down = pl.pallas_call(
        edge_kernel,
        in_specs=[VMEM] * 15,
        out_specs=[VMEM] * 12,
        out_shape=[held(rows, depth), held(layers - 2, rows, depth), held(rows, depth), held(rows, depth)]
        + [held(split, rows, depth), held(SUB, LANES), held(layers - split, 2 * SUB, depth), held(SUB, LANES)]
        + [held(2, depth), held(2, depth), held(layers, depth), held(layers, depth)],
        input_output_aliases={10: 0, 11: 1, 12: 2, 13: 3, 14: 4},
        compiler_params=params(4),
        cost_estimate=cost(320 * depth, 640 * depth),
        name="edges_first",
    )(
        *near_core(
            first_sums, high_sums, b, face_right, up, down, tx, ty, tz, st, s_first, s_mid, s_last, w_last, image_low,
        )
    )

    jump_next, second_sums = pl.pallas_call(
        jump_second_kernel,
        in_specs=[VMEM] * 11,
        out_specs=[VMEM] * 2,
        out_shape=[held(rows, depth), held(SUB, LANES)],
        scratch_shapes=[pltpu.VMEM((rows, depth), F32)],
        compiler_params=params(16),
        cost_estimate=mortar_cost,
        name="jump_second",
    )(
        *near_core(
            high_sums, w_last, jump, face_right, face_right_next, right_edges, back, missing, picks, codes, proj_t,
        )
    )
    (back_next,) = pl.pallas_call(
        back_second_kernel,
        in_specs=[VMEM] * 5,
        out_specs=[VMEM],
        out_shape=[held(rows + SUB, depth)],
        compiler_params=params(16),
        cost_estimate=mortar_cost,
        name="back_second",
    )(*near_core(w_last, missing, puts, codes, proj_n))

    (back_next,) = pl.pallas_call(
        hold_kernel,
        in_specs=[VMEM] * 2,
        out_specs=[VMEM],
        out_shape=[held(rows + SUB, depth)],
        input_output_aliases={1: 0},
        compiler_params=params(2),
        cost_estimate=cost(0, 8 * depth),
        name="hold",
    )(*near_core(second_sums, back_next))
    recv_next = shifted(back_next, "sub", 1)

    count = subs * blks
    image_low, edge_high, table = pl.pallas_call(
        second_added_kernel,
        in_specs=[VMEM] * 18,
        out_specs=[VMEM] * 3,
        out_shape=[
            held(split, rows, depth), held(2 * (layers - split), depth), held(-(-count * FIELDS // LANES), LANES),
        ],
        input_output_aliases={17: 0},
        scratch_shapes=[pltpu.VMEM((6, SUB, LANES), F32)],
        compiler_params=params(8),
        cost_estimate=cost(20 * cells, 15 * cells),
        name="stencil_second_added",
    )(
        *near_core(
            edge_sums, jump_sums, high_sums, ends_sums, second_sums, b, s_first, s_mid, w_last, recv,
            w_up, w_down, up, tx, ty, tz, st, image_low,
        )
    )
    (own_next,) = pl.pallas_call(
        own_second_kernel,
        in_specs=[VMEM] * 4,
        out_specs=[VMEM],
        out_shape=[held(rows, depth)],
        compiler_params=params(16),
        cost_estimate=mortar_cost,
        name="own_second",
    )(*near_core(s_first, recv, proj_t, proj_n))
    tables = gather_rows(table, own_next)

    return pl.pallas_call(
        final_kernel,
        in_specs=[VMEM] * 13,
        out_specs=[HBM] * 2,
        out_shape=[jax.ShapeDtypeStruct((layers, rows, depth), F32)] * 2,
        scratch_shapes=[pltpu.VMEM((layers, rows, depth), F32)] * 2 + [pltpu.SemaphoreType.DMA((2, steps))],
        compiler_params=params(8),
        cost_estimate=cost(8 * cells, 22 * cells),
        name="final_update",
    )(*near_core(tables, b, s_first, s_mid, w_last, recv, image_low, image_high, image_ends, edge_high, jump_next, recv_next, own_next))


def solution(mesh):
    cells = P("sub", "blk", None)
    in_specs = (cells,) * 7 + (P("sub", "blk"), P())
    return jax.shard_map(body, mesh=mesh, in_specs=in_specs, out_specs=(cells, cells), check_vma=False)
```

```python
import jax
import jax.numpy as jnp
from jax import lax
from jax.experimental import pallas as pl
from jax.experimental.pallas import tpu as pltpu
from jax.sharding import PartitionSpec as P

ROWS = 32
FIELDS = 16
SUB = 8
LANES = 128
F32 = jnp.float32
BF16 = jnp.bfloat16
penalty = 4.0


def tile_ids(dim, shape):
    return lax.broadcasted_iota(jnp.int32, shape, dim)


def as_tile(scalars):
    lane = tile_ids(1, (SUB, LANES))
    tile = jnp.zeros((SUB, LANES), F32)
    for place, value in enumerate(scalars):
        tile = jnp.where(lane == place, value, tile)
    return tile


def from_tile(tile, place):
    pick = (tile_ids(1, tile.shape) == place) & (tile_ids(0, tile.shape) == 0)
    return jnp.sum(jnp.where(pick, tile, 0.0))


def fold(array):
    parts = [array[:, place : place + LANES] for place in range(0, array.shape[1], LANES)]
    while len(parts) > 1:
        parts = [one + other for one, other in zip(parts[::2], parts[1::2])]
    return parts[0]


def at(array, layers, start):
    return [array[layer, pl.ds(start, SUB), :] for layer in range(layers)]


def stencil(values, after, tx, ty, tz, st, carry, below=None, above=None):
    shape = values[0].shape
    row = tile_ids(0, shape)
    last_z = tile_ids(1, shape) == shape[1] - 1
    results, carries = [], []
    flux_x = None if below is None else below[1] * (below[0] - values[0])
    for layer, value in enumerate(values):
        follow = value if after is None else pltpu.roll(after[layer], SUB - 1, 0)
        follow = jnp.where(row == SUB - 1, follow, pltpu.roll(value, SUB - 1, 0))
        flux_y = ty[layer] * (value - follow)
        rolled = pltpu.roll(flux_y, 1, 0)
        carries.append(rolled)
        flux_z = jnp.where(last_z, 0.0, tz[layer] * (value - pltpu.roll(value, shape[1] - 1, 1)))
        result = st[layer] * value + (flux_y - jnp.where(row == 0, carry[layer], rolled))
        result = result + (flux_z - pltpu.roll(flux_z, 1, 1))
        if flux_x is not None:
            result = result - flux_x
        next_x = values[layer + 1] if layer < len(values) - 1 else above
        flux_x = None
        if next_x is not None:
            flux_x = tx[layer] * (value - next_x)
            result = result + flux_x
        results.append(result)
    return results, carries


def at_last_block():
    return lax.axis_index("blk") == lax.axis_size("blk") - 1


def edge_terms(before, first, last, beyond, ty_before, ty_last):
    low = ty_before * (first - before)
    high = jnp.where(at_last_block(), 0.0, ty_last * (last - beyond))
    return low, high


def pack_kernel(b_hbm, ty_hbm, face, sems):
    rows = b_hbm.shape[1]
    copies = [
        pltpu.make_async_copy(b_hbm.at[0], face.at[pl.ds(0, rows), :], sems.at[0]),
        pltpu.make_async_copy(ty_hbm.at[0, pl.ds(rows - SUB, SUB), :], face.at[pl.ds(rows, SUB), :], sems.at[1]),
    ]
    for copy in copies:
        copy.start()
    for copy in copies:
        copy.wait()


def two_parts(array):
    high = array.astype(BF16)
    return high, (array - high.astype(F32)).astype(BF16)


def prepare_pairs(perm, kind, count, proj, rows, groups, picks, puts, codes, code_row, proj_t, proj_n):
    kinds, width, _ = proj.shape
    blocks = rows * groups
    lane = tile_ids(1, (1, blocks))
    target = lax.rem(perm, groups) * rows + lax.div(perm, groups)
    shift = kinds.bit_length()
    keys = (target * (1 << shift) + jnp.where(lane < count, kind, kinds)).astype(F32)
    span = LANES // groups
    spread = tile_ids(1, (span, LANES)) - groups * tile_ids(0, (span, LANES))
    lanes = tile_ids(1, (rows, LANES))
    across = []
    for group in range(groups):
        column = jnp.concatenate(
            [
                jnp.sum(jnp.where(spread == group, keys[:, place * LANES : (place + 1) * LANES], 0.0), 1, keepdims=True)
                for place in range(blocks // LANES)
            ],
            axis=0,
        ).astype(jnp.int32)
        column = jnp.broadcast_to(column, (rows, LANES))
        here = pl.ds(group * rows, rows)
        for place in range(rows // LANES):
            turned = jnp.transpose(column[place * LANES : (place + 1) * LANES].astype(F32))
            across.append(turned[0:1, :].astype(jnp.int32))
        codes[here, :] = column & ((1 << shift) - 1)
        column = column >> shift
        for place in range(blocks // LANES):
            picks[here, pl.ds(place * LANES, LANES)] = jnp.where(column == lanes + place * LANES, 1.0, 0.0).astype(BF16)
    across = jnp.concatenate(across, axis=1)
    code_row[...] = (kinds - (across & ((1 << shift) - 1))).astype(F32)
    across = across >> shift
    down = tile_ids(0, (rows, blocks))
    for group in range(groups):
        puts[pl.ds(group * rows, rows), :] = jnp.where(across == down + group * rows, 1.0, 0.0).astype(BF16)
    for kind in range(kinds):
        here = pl.ds(kind * width, width)
        proj_t[here, :] = jnp.concatenate(two_parts(jnp.transpose(proj[kind])), axis=1)
        proj_n[here, :] = jnp.concatenate(two_parts(proj[kind]), axis=1)


def first_kernel(
    count, perm, kind, proj, b_hbm, tx_hbm, ty_hbm, tz_hbm, st_hbm,
    b, tx, ty, tz, st, face_next, s_first, s_mid, s_last, sums, picks, puts, codes, code_row, proj_t, proj_n, total, sems,
):
    layers, rows, depth = b.shape
    steps = rows // ROWS
    sources, targets = (b_hbm, tx_hbm, ty_hbm, tz_hbm, st_hbm), (b, tx, ty, tz, st)

    def copy(which, step):
        part = pl.ds(step * ROWS, ROWS)
        return pltpu.make_async_copy(
            sources[which].at[:, part, :], targets[which].at[:, part, :], sems.at[which, step]
        )

    for step in range(steps):
        for which in range(len(sources)):
            copy(which, step).start()
    width = proj.shape[1]
    prepare_pairs(
        perm[0], kind[0], count[0, 0], proj, rows, depth // width, picks, puts, codes, code_row, proj_t, proj_n
    )
    total[...] = jnp.zeros_like(total)
    copy(0, 0).wait()

    def chunk(start, after, carry):
        values = at(b, layers, start)
        results, carry = stencil(values, after, *[at(array, layers, start) for array in (tx, ty, tz, st)], carry)
        here = pl.ds(start, SUB)
        squares, products = values[0] * values[0], values[0] * results[0]
        for layer in range(1, layers):
            squares = squares + values[layer] * values[layer]
            products = products + values[layer] * results[layer]
        total[0] += fold(squares)
        total[1] += fold(products)
        face_next[here, :] = results[0]
        s_first[here, :] = results[0]
        for layer in range(1, layers - 1):
            s_mid[layer - 1, here, :] = results[layer]
        s_last[here, :] = results[layers - 1]
        return carry

    carry = [jnp.zeros((SUB, depth), F32)] * layers
    for step in range(steps):
        for which in range(1, len(sources)):
            copy(which, step).wait()
        if step < steps - 1:
            copy(0, step + 1).wait()
        for start in range(step * ROWS, (step + 1) * ROWS, SUB):
            carry = chunk(start, None if start == rows - SUB else at(b, layers, start + SUB), carry)
    sums[...] = as_tile([jnp.sum(total[0]), jnp.sum(total[1])])


def up_places(layers):
    return 0, layers, 2 * layers, 3 * layers, 3 * layers + 1, 3 * layers + 2


def edge_kernel(
    sums_in, near_sums, b, right, up, down, tx, ty, tz, st, s_first_in, s_mid_in, s_last_in, w_last_in, image_low_in,
    s_first, s_mid, s_last, w_last, image_low, sums, image_ends, ends_sums, right_edges, missing, w_up, w_down,
):
    layers, rows, depth = b.shape
    at_b, at_ty, at_w, at_back, at_right, at_right_ty = up_places(layers)
    product = 0.0
    for layer in range(layers):
        first, last = b[layer, 0:1, :], b[layer, rows - 1 :, :]
        low, high = edge_terms(
            up[at_b + layer : at_b + layer + 1, :], first, last, down[layer : layer + 1, :],
            up[at_ty + layer : at_ty + layer + 1, :], ty[layer, rows - 1 :, :],
        )
        pairs = [(s_first_in, s_first)] if layer == 0 else [(s_last_in, s_last), (w_last_in, w_last)]
        if 0 < layer < layers - 1:
            pairs = [(s_mid_in.at[layer - 1], s_mid.at[layer - 1])]
        for source, target in pairs:
            target[0:1, :] = source[0:1, :] + low
            target[rows - 1 :, :] = source[rows - 1 :, :] + high
        product = product + first * low + last * high
        w_up[layer : layer + 1, :] = up[at_w + layer : at_w + layer + 1, :] - low
        w_down[layer : layer + 1, :] = down[layers + layer : layers + layer + 1, :] - high
    sums[...] = sums_in[...] + as_tile([0.0, jnp.sum(product)])
    low, high = edge_terms(
        up[at_right : at_right + 1, :], right[0:1, :], right[rows - 1 : rows, :], down[2 * layers + 1 :, :],
        up[at_right_ty : at_right_ty + 1, :], right[rows + SUB - 1 :, :],
    )
    right_edges[0:1, :] = low
    right_edges[1:2, :] = high
    missing[0:1, :] = -up[at_right_ty : at_right_ty + 1, :] * up[at_back : at_back + 1, :]
    missing[1:2, :] = jnp.where(
        at_last_block(), 0.0, -right[rows + SUB - 1 :, :] * down[2 * layers : 2 * layers + 1, :]
    )
    near = from_tile(near_sums[...], 2)
    own, read, plain = high_layers(layers, s_mid, s_last, w_last)
    terms = None
    for place, start in enumerate((0, rows - SUB)):
        values = read(start)
        if place == 0:
            after, carry = read(SUB), [jnp.zeros((SUB, depth), F32)] * len(own)
        else:
            after, carry = None, flux_from(start - SUB, own, read, 1, ty)
        new, _ = chunk_sums(
            start, values, after, carry, own, near, b, plain, tx, ty, tz, st, image_ends, place * SUB
        )
        terms = new if terms is None else [old + more for old, more in zip(terms, new)]
    ends_sums[...] = as_tile([0.0] * 3 + [jnp.sum(term) for term in terms])
    own, read = low_layers(layers, s_first, s_mid)
    zero = [jnp.zeros((SUB, depth), F32)] * len(own)
    low_chunk(0, read(0), read(SUB), zero, own, tx, ty, tz, st, image_low)
    carry = flux_from(rows - 2 * SUB, own, read, 0, ty)
    low_chunk(rows - SUB, read(rows - SUB), None, carry, own, tx, ty, tz, st, image_low)


def high_layers(layers, s_mid, s_last, w_last):
    split = layers // 2

    def read(start):
        here = pl.ds(start, SUB)
        return [s_mid[layer - 1, here, :] for layer in range(split - 1, layers - 1)] + [w_last[here, :]]

    def plain(layer, here):
        return s_last[here, :] if layer == layers - 1 else s_mid[layer - 1, here, :]

    return list(range(split, layers)), read, plain


def flux_from(start, own, read, skip, ty):
    row = None
    carry = []
    for layer, value, after in zip(own, read(start)[skip:], read(start + SUB)[skip:]):
        row = tile_ids(0, value.shape)
        follow = jnp.where(row == SUB - 1, pltpu.roll(after, SUB - 1, 0), pltpu.roll(value, SUB - 1, 0))
        carry.append(pltpu.roll(ty[layer, pl.ds(start, SUB), :] * (value - follow), 1, 0))
    return carry


def chunk_sums(start, values, after, carry, own, near, b, plain, tx, ty, tz, st, image, target, summed=None):
    layers = b.shape[0]
    here = pl.ds(start, SUB)
    below = (values[0], tx[own[0] - 1, here, :]) if own[0] > 0 else None
    above = values[-1] if own[-1] < layers - 1 else None
    skip = 0 if below is None else 1
    mine = values[skip : skip + len(own)]
    results, carry = stencil(
        mine, None if after is None else after[skip : skip + len(own)],
        *[[array[layer, here, :] for layer in own] for array in (tx, ty, tz, st)], carry, below, above,
    )
    terms = None
    for place, layer in enumerate(own):
        w, s = mine[place], results[place]
        image[place, pl.ds(target, SUB), :] = s
        if summed is not None and layer not in summed:
            continue
        u = b[layer, here, :] - near * w
        q = plain(layer, here) - near * s
        new = [fold(term) for term in (u * u, u * w, w * w, u * q, u * s + w * q, w * s)]
        terms = new if terms is None else [old + more for old, more in zip(terms, new)]
    return terms, carry


def mm(left, right):
    return lax.dot_general(left, right, (((1,), (0,)), ((), ())), preferred_element_type=F32)


def by_kind(codes, array, kinds):
    zero = jnp.zeros_like(array)
    return jnp.concatenate([jnp.where(codes == kind, array, zero) for kind in range(kinds)], axis=1)


def apply_proj(codes, high, low, proj, kinds, width):
    both = mm(by_kind(codes, high, kinds), proj[...])
    return both[:, :width] + both[:, width:] + mm(by_kind(codes, low, kinds), proj[:, :width])


def take_jump(group, faces, last, picks, codes_col, proj_t):
    width = proj_t.shape[1] // 2
    kinds = proj_t.shape[0] // width
    here = pl.ds(group * last.shape[0], last.shape[0])
    codes = codes_col[here, :]
    taken = mm(picks[here, :], faces)
    projected = apply_proj(codes, taken[:, :width].astype(BF16), taken[:, width:].astype(BF16), proj_t, kinds, width)
    return jnp.where(codes < kinds, last - projected, 0.0)


def turn_back(group, jump, codes_col, proj_n):
    width = proj_n.shape[1] // 2
    kinds = proj_n.shape[0] // width
    scale = jnp.where(lax.axis_index("sub") < lax.axis_size("sub") - 1, -penalty, 0.0)
    codes = codes_col[pl.ds(group * jump.shape[0], jump.shape[0]), :]
    return jnp.concatenate(two_parts(scale * apply_proj(codes, *two_parts(jump), proj_n, kinds, width)), axis=1)


def put_back(group, backs, puts, rows):
    width = backs.shape[1] // 2
    placed = mm(puts[pl.ds(group * rows, rows), :], backs)
    return placed[:, :width] + placed[:, width:]


def stack_parts(parts):
    return jnp.concatenate(two_parts(jnp.concatenate(parts, axis=0)), axis=1)


def jump_first_kernel(earlier, b, right, s_last, picks, codes, proj_t, w_last, jump_face, sums):
    width = proj_t.shape[1] // 2
    layers, rows, depth = b.shape
    parts = [pl.ds(group * width, width) for group in range(depth // width)]
    faces = stack_parts([right[:rows, part] for part in parts])
    square = jnp.zeros((rows, width), F32)
    for group, part in enumerate(parts):
        jump = take_jump(group, faces, b[layers - 1, :, part], picks, codes, proj_t)
        square = square + jump * jump
        jump_face[:, part] = jump
        w_last[:, part] = s_last[:, part] + penalty * jump
    sums[...] = as_tile([jnp.sum(square)])


def kinds_kernel(code_row, picks, kinds_by_block):
    depth = kinds_by_block.shape[1]
    row = mm(jnp.broadcast_to(code_row[...], (2 * SUB, code_row.shape[1])).astype(BF16), picks[...])
    kinds_by_block[...] = jnp.zeros_like(kinds_by_block)
    for place in range(row.shape[1] // depth):
        kinds_by_block[place : place + 1, :] = row[0:1, place * depth : (place + 1) * depth]


def rows_kernel(right, b, ty, s_first, s_mid, w_last, back, up, down):
    layers, rows, _ = b.shape
    at_b, at_ty, at_w, at_back, at_right, at_right_ty = up_places(layers)
    end = pl.ds(rows - 1, 1)
    for layer in range(layers):
        image = s_first if layer == 0 else w_last if layer == layers - 1 else s_mid.at[layer - 1]
        up[at_b + layer : at_b + layer + 1, :] = b[layer, end, :]
        up[at_ty + layer : at_ty + layer + 1, :] = ty[layer, end, :]
        up[at_w + layer : at_w + layer + 1, :] = image[end, :]
        down[layer : layer + 1, :] = b[layer, 0:1, :]
        down[layers + layer : layers + layer + 1, :] = image[0:1, :]
    up[at_back : at_back + 1, :] = back[end, :]
    up[at_right : at_right + 1, :] = right[end, :]
    up[at_right_ty : at_right_ty + 1, :] = right[rows + SUB - 1 :, :]
    down[2 * layers : 2 * layers + 1, :] = back[0:1, :]
    down[2 * layers + 1 : 2 * layers + 2, :] = right[0:1, :]


def jump_second_kernel(
    near_sums, w_last, jump, right_before, right, right_edges, back_before, missing, picks, codes, proj_t,
    jump_next, sums, field,
):
    width = proj_t.shape[1] // 2
    rows, depth = right.shape
    parts = [pl.ds(group * width, width) for group in range(depth // width)]
    near = from_tile(near_sums[...], 2)
    field[...] = right[...] + back_before[:rows, :]
    field[0:1, :] += right_edges[0:1, :]
    field[rows - 1 :, :] += right_edges[1:2, :]
    faces = stack_parts([field[:, part] for part in parts])
    totals = [jnp.zeros((rows, width), F32)] * 3
    for group, part in enumerate(parts):
        later = take_jump(group, faces, w_last[:, part], picks, codes, proj_t)
        jump_next[:, part] = later
        close = jump[:, part] - near * later
        totals = [total + new for total, new in zip(totals, (close * close, close * later, later * later))]
    found = [jnp.sum(total) for total in totals]
    found = [penalty * found[0], 2.0 * penalty * found[1], penalty * found[2]]
    extra = [0.0] * 3
    for side, place in enumerate((0, rows - 1)):
        s = missing[side : side + 1, :]
        w = field[place : place + 1, :]
        u = right_before[place : place + 1, :] - near * w
        extra = [old + more for old, more in zip(extra, [-near * u * s, u * s - near * w * s, w * s])]
    sums[...] = as_tile([0.0] * 6 + [old + jnp.sum(more) for old, more in zip(found, extra)])


def back_first_kernel(jump, kinds_by_block, puts, codes, proj_n, back):
    rows = jump.shape[0]
    back_kernel(jump, puts, codes, proj_n, back)
    back[rows:, :] = kinds_by_block[...]


def back_second_kernel(w_last, missing, puts, codes, proj_n, back):
    rows = w_last.shape[0]
    back_kernel(w_last, puts, codes, proj_n, back)
    back[rows : rows + 2, :] = missing[...]


def own_second_kernel(s_first, recv, proj_t, proj_n, own):
    rows, depth = own.shape
    width = proj_t.shape[1] // 2
    kinds = proj_t.shape[0] // width
    for group in range(depth // width):
        part = pl.ds(group * width, width)
        codes = []
        for place in range(rows // LANES):
            start = group * rows + place * LANES
            row = recv[rows + start // depth : rows + start // depth + 1, start % depth : start % depth + LANES]
            codes.append(jnp.transpose(jnp.broadcast_to(row, (LANES, LANES))))
        codes = kinds - jnp.concatenate(codes, axis=0).astype(jnp.int32)
        field = s_first[:, part] + recv[:rows, part]
        projected = apply_proj(codes, *two_parts(field), proj_t, kinds, width)
        own[:, part] = penalty * apply_proj(codes, *two_parts(projected), proj_n, kinds, width)


def wait_kernel(earlier, back_in, back):
    last = pl.ds(back.shape[0] - SUB, SUB)
    back[last, :] = back_in[last, :]


def hold_kernel(later, much_later, back_in, back):
    back[back.shape[0] - SUB + 2 :, :] = jnp.zeros((SUB - 2, back.shape[1]), F32)


def back_kernel(jump_next, puts, codes, proj_n, back):
    width = proj_n.shape[1] // 2
    rows, depth = jump_next.shape
    parts = [pl.ds(group * width, width) for group in range(depth // width)]
    backs = [turn_back(group, jump_next[:, part], codes, proj_n) for group, part in enumerate(parts)]
    backs = jnp.concatenate(backs, axis=0)
    for group, part in enumerate(parts):
        back[:rows, part] = put_back(group, backs, puts, rows)


def stencil_sums(read, own, near, b, plain, tx, ty, tz, st, image, total, inner, summed=None):
    layers, rows, depth = b.shape
    total[...] = jnp.zeros_like(total)
    skip = 1 if own[0] > 0 else 0

    def several(start, count, carry, at_end=False):
        starts = [pl.multiple_of(start + SUB * place, SUB) for place in range(count + 1)]
        values = [read(place) for place in starts[:-1]] + [None if at_end else read(starts[-1])]
        terms = None
        for place in range(count):
            new, carry = chunk_sums(
                starts[place], values[place], values[place + 1], carry, own, near, b, plain, tx, ty, tz, st, image,
                starts[place], summed,
            )
            terms = new if terms is None else [old + more for old, more in zip(terms, new)]
        for place, term in enumerate(terms):
            total[place] += term
        return carry

    group = 2
    if inner:
        begin, count, carry = SUB, (rows // SUB - 2) // group, flux_from(0, own, read, skip, ty)
    else:
        begin, count, carry = 0, rows // (group * SUB) - 1, [jnp.zeros((SUB, depth), F32)] * len(own)
    carry = lax.fori_loop(
        0, count,
        lambda index, carry: tuple(
            several(pl.multiple_of(begin + index * group * SUB, SUB), group, list(carry))
        ),
        tuple(carry),
    )
    if not inner:
        several(rows - group * SUB, group, list(carry), True)
    return [jnp.sum(total[place]) for place in range(total.shape[0])]


def second_high_kernel(later, first_sums, jump_sums, b, s_mid, s_last, w_last, tx, ty, tz, st, image, sums, total):
    norm = from_tile(first_sums[...], 0)
    energy = from_tile(first_sums[...], 1) + penalty * from_tile(jump_sums[...], 0)
    safe = energy > 0.01 * norm
    ratio = jnp.full((SUB, LANES), norm, F32) / jnp.full((SUB, LANES), jnp.where(safe, energy, 1.0), F32)
    near = jnp.where(safe, jnp.max(ratio), 0.0)
    own, read, plain = high_layers(b.shape[0], s_mid, s_last, w_last)
    found = stencil_sums(read, own, near, b, plain, tx, ty, tz, st, image, total, True)
    sums[...] = as_tile([0.0, 0.0, near] + found)


def low_layers(layers, s_first, s_mid):
    split = layers // 2

    def read(start):
        here = pl.ds(start, SUB)
        return [s_first[here, :]] + [s_mid[layer - 1, here, :] for layer in range(1, split + 1)]

    return list(range(split)), read


def low_chunk(start, values, after, carry, own, tx, ty, tz, st, image):
    here = pl.ds(start, SUB)
    results, carry = stencil(
        values[:-1], None if after is None else after[:-1],
        *[[array[layer, here, :] for layer in own] for array in (tx, ty, tz, st)], carry, None, values[-1],
    )
    for layer in own:
        image[layer, here, :] = results[layer]
    return carry


def second_low_kernel(s_first, s_mid, tx, ty, tz, st, image):
    layers, rows = tx.shape[:2]
    own, read = low_layers(layers, s_first, s_mid)
    group = 3

    def several(index, carry):
        start = pl.multiple_of(SUB + index * group * SUB, SUB)
        starts = [pl.multiple_of(start + SUB * place, SUB) for place in range(group + 1)]
        values = [read(place) for place in starts]
        carry = list(carry)
        for place in range(group):
            carry = low_chunk(starts[place], values[place], values[place + 1], carry, own, tx, ty, tz, st, image)
        return tuple(carry)

    lax.fori_loop(0, (rows // SUB - 2) // group, several, tuple(flux_from(0, own, read, 0, ty)))


def second_added_kernel(
    first_sums, jump_sums, high_sums, ends_sums, second_sums, b, s_first, s_mid, w_last, recv,
    w_up, w_down, up, tx, ty, tz, st, image_in, image, edge_high, table, total,
):
    layers, rows, depth = b.shape
    split = layers // 2
    near = from_tile(high_sums[...], 2)
    total[...] = jnp.zeros_like(total)
    first, second = 0, 1

    def several(start, count, carry, at_end=False):
        starts = [pl.multiple_of(start + SUB * place, SUB) for place in range(count + 1)]
        added = [recv[pl.ds(place, SUB), :] for place in starts[:-1]]
        added.append(None if at_end else recv[pl.ds(starts[-1], SUB), :])
        terms = None
        for place in range(count):
            here = pl.ds(starts[place], SUB)
            e, t_x = added[place], tx[first, here, :]
            (s,), carry = stencil(
                [e], None if added[place + 1] is None else [added[place + 1]], [t_x], [ty[first, here, :]],
                [tz[first, here, :]], [st[first, here, :] + t_x], carry,
            )
            s = image_in[first, here, :] + s
            image[first, here, :] = s
            plain = s_first[here, :]
            w = plain + e
            u = b[first, here, :] - near * w
            q = plain - near * s
            new = [u * u, u * w, w * w, u * q, u * s + w * q, w * s]
            s = image_in[second, here, :] - t_x * e
            image[second, here, :] = s
            w = s_mid[second - 1, here, :]
            u = b[second, here, :] - near * w
            q = w - near * s
            more = [u * u, u * w, w * w, u * q, u * s + w * q, w * s]
            new = [fold(one + other) for one, other in zip(new, more)]
            terms = new if terms is None else [old + more for old, more in zip(terms, new)]
        for place, term in enumerate(terms):
            total[place] += term
        return carry

    group = 4
    carry = lax.fori_loop(
        0, rows // (group * SUB) - 1,
        lambda index, carry: several(pl.multiple_of(index * group * SUB, SUB), group, [carry])[0],
        jnp.zeros((SUB, depth), F32),
    )
    several(rows - group * SUB, group, [carry], True)
    found = [jnp.sum(total[place]) for place in range(total.shape[0])]

    def row(layer, place):
        here = pl.ds(place, 1)
        if layer == 0:
            return s_first[here, :] + recv[here, :]
        return w_last[here, :] if layer == layers - 1 else s_mid[layer - 1, here, :]

    extra = [jnp.zeros((1, depth), F32)] * 3
    for layer in range(layers):
        ends = row(layer, 0), row(layer, rows - 1)
        added = edge_terms(
            w_up[layer : layer + 1, :], *ends, w_down[layer : layer + 1, :],
            up[layers + layer : layers + layer + 1, :], ty[layer, rows - 1 :, :],
        )
        for side, (place, w, s) in enumerate(zip((0, rows - 1), ends, added)):
            u = b[layer, place : place + 1, :] - near * w
            extra = [old + more for old, more in zip(extra, [-near * u * s, u * s - near * w * s, w * s])]
            if layer < split:
                image[layer, place : place + 1, :] += s
            else:
                spot = side * (layers - split) + layer - split
                edge_high[spot : spot + 1, :] = s
    found[3:] = [old + jnp.sum(more) for old, more in zip(found[3:], extra)]
    norm = from_tile(first_sums[...], 0)
    energy = from_tile(first_sums[...], 1) + penalty * from_tile(jump_sums[...], 0)
    sums = high_sums[...] + ends_sums[...] + second_sums[...]
    sums = sums + as_tile([norm, energy, 0.0] + found)
    mine = lax.axis_index("sub") * lax.axis_size("blk") + lax.axis_index("blk")
    device = tile_ids(0, table.shape) * (LANES // FIELDS) + lax.div(tile_ids(1, table.shape), FIELDS)
    field = lax.rem(tile_ids(1, table.shape), FIELDS)
    filled = jnp.zeros(table.shape, F32)
    for place in range(9):
        filled = jnp.where((device == mine) & (field == place), jnp.sum(sums[0:1, place : place + 1]), filled)
    table[...] = filled


def add_kernel(earlier, one, other, both):
    both[...] = one[...] + other[...]


def final_kernel(
    tables, b, s_first, s_mid, w_last, recv, image_low, image_high, image_ends, edge_high, jump_next, recv_next, own_next, solution_hbm, residual_hbm,
    solution, residual, sems,
):
    layers, rows, depth = b.shape
    split = image_low.shape[0]
    flat = tables[...]
    norm, energy, near, uu, uw, ww, uq, cross, wq = [
        flat if place == 0 else pltpu.roll(flat, LANES - place, 1) for place in range(9)
    ]
    own = lax.rem(tile_ids(1, flat.shape), FIELDS) == 0

    def whole(array):
        array = jnp.sum(jnp.where(own, array, 0.0), axis=0, keepdims=True)
        return jnp.sum(array, axis=1, keepdims=True)

    norm, energy = whole(norm), whole(energy)
    alpha = norm / energy
    away = alpha - near
    norm_next = whole(uu - away * (2.0 * uw - away * ww))
    energy_next = whole(uq - away * (cross - away * wq))
    beta = norm_next / norm
    step_size = norm_next / (energy_next - beta * norm_next / alpha)
    c0 = jnp.broadcast_to(alpha + step_size * beta + step_size, (SUB, depth))
    c1 = jnp.broadcast_to(step_size * alpha, (SUB, depth))
    c2 = jnp.broadcast_to(alpha + step_size * (1.0 + beta), (SUB, depth))

    def copy(which, step):
        part = pl.ds(step * ROWS, ROWS)
        source, target = ((solution, solution_hbm), (residual, residual_hbm))[which]
        return pltpu.make_async_copy(source.at[:, part, :], target.at[:, part, :], sems.at[which, step])

    for step in range(rows // ROWS):
        for start in range(step * ROWS, (step + 1) * ROWS, SUB):
            here = pl.ds(start, SUB)
            for layer in range(layers):
                v = b[layer, here, :]
                if layer < split:
                    s = image_low[layer, here, :]
                elif start == 0:
                    s = image_ends[layer - split, :SUB, :]
                elif start == rows - SUB:
                    s = image_ends[layer - split, SUB:, :]
                else:
                    s = image_high[layer - split, here, :]
                if layer == 0:
                    w = s_first[here, :] + recv[here, :]
                    s = s + (recv_next[here, :] + own_next[here, :])
                elif layer < layers - 1:
                    w = s_mid[layer - 1, here, :]
                else:
                    w = w_last[here, :]
                    s = s + penalty * jump_next[here, :]
                solution[layer, here, :] = c0 * v - c1 * w
                residual[layer, here, :] = v - c2 * w + c1 * s
        for side, last_step in enumerate((0, rows // ROWS - 1)):
            if step == last_step:
                place = side * (rows - 1)
                residual[0, place : place + 1, :] += c1[0:1, :] * recv_next[rows + side : rows + side + 1, :]
                for layer in range(split, layers):
                    spot = side * (layers - split) + layer - split
                    residual[layer, place : place + 1, :] += c1[0:1, :] * edge_high[spot : spot + 1, :]
        for which in range(2):
            copy(which, step).start()
    for step in range(rows // ROWS):
        for which in range(2):
            copy(which, step).wait()


SMEM = pl.BlockSpec(memory_space=pltpu.SMEM)
VMEM = pl.BlockSpec(memory_space=pltpu.VMEM)
HBM = pl.BlockSpec(memory_space=pltpu.HBM)


def held(*dims, dtype=F32):
    return pltpu.VMEM(dims, dtype)


def near_core(*arrays):
    return [pltpu.with_memory_space_constraint(array, pltpu.VMEM) for array in arrays]


def in_hbm(*arrays):
    return [pltpu.with_memory_space_constraint(array, pltpu.HBM) for array in arrays]


def cost(flops, size):
    return pl.CostEstimate(flops=int(flops), bytes_accessed=int(size), transcendentals=0)


def params(mib):
    return pltpu.CompilerParams(vmem_limit_bytes=mib * 1024 * 1024)


def shifted(array, axis, by):
    size = lax.axis_size(axis)
    return lax.ppermute(array, axis, [(i, i + by) for i in range(size) if 0 <= i + by < size])


def gather_rows(table, own):
    subs, blks = lax.axis_size("sub"), lax.axis_size("blk")
    steps = [(0, 1)]
    reach = 2
    while reach < blks:
        steps.append((0, reach + 1))
        reach *= 2
    reach = subs // 2
    while reach > 0:
        steps.append((reach, 1))
        reach //= 2
    for place, (by_sub, by_blk) in enumerate(steps):
        pairs = [(s * blks + t, (s ^ by_sub) * blks + (t ^ by_blk)) for s in range(subs) for t in range(blks)]
        other = lax.ppermute(table, ("sub", "blk"), pairs)
        if place == 0:
            (table,) = pl.pallas_call(
                add_kernel,
                in_specs=[VMEM] * 3,
                out_specs=[VMEM],
                out_shape=[held(*table.shape)],
                compiler_params=params(2),
                cost_estimate=cost(table.size, 12 * table.size),
                name="add",
            )(*near_core(own, table, other))
        else:
            table = table + other
    return table


def body(right_side, trans_x, trans_y, trans_z, storage, pair_perm, pair_type, pair_count, proj):
    layers, rows, depth = right_side.shape
    blocks, width, kinds = pair_perm.shape[2], proj.shape[1], proj.shape[0]
    subs, blks = lax.axis_size("sub"), lax.axis_size("blk")
    steps = rows // ROWS
    cells = layers * rows * depth

    (face,) = pl.pallas_call(
        pack_kernel,
        in_specs=[HBM, HBM],
        out_specs=[VMEM],
        out_shape=[held(rows + SUB, depth)],
        scratch_shapes=[pltpu.SemaphoreType.DMA((2,))],
        compiler_params=params(2),
        cost_estimate=cost(0, 4 * rows * depth),
        name="pack",
    )(*in_hbm(right_side, trans_y))
    face_right = shifted(face, "sub", -1)

    b, tx, ty, tz, st, face_next, s_first, s_mid, s_last, first_sums, picks, puts, codes, code_row, proj_t, proj_n = pl.pallas_call(
        first_kernel,
        in_specs=[SMEM] + [VMEM] * 3 + [HBM] * 5,
        out_specs=[VMEM] * 16,
        out_shape=[held(layers, rows, depth)] * 5
        + [
            held(rows, depth), held(rows, depth), held(layers - 2, rows, depth), held(rows, depth), held(SUB, LANES),
            held(blocks, blocks, dtype=BF16), held(blocks, blocks, dtype=BF16), held(blocks, width, dtype=jnp.int32), held(1, blocks),
            held(kinds * width, 2 * width, dtype=BF16), held(kinds * width, 2 * width, dtype=BF16),
        ],
        scratch_shapes=[pltpu.VMEM((2, SUB, LANES), F32), pltpu.SemaphoreType.DMA((5, steps))],
        compiler_params=params(16),
        cost_estimate=cost(20 * cells, 24 * cells),
        name="stencil_first",
    )(
        pair_count, pair_perm, pair_type, proj,
        *in_hbm(right_side, trans_x, trans_y, trans_z, storage),
    )
    face_right_next = shifted(face_next, "sub", -1)

    split = layers // 2
    (image_low,) = pl.pallas_call(
        second_low_kernel,
        in_specs=[VMEM] * 6,
        out_specs=[VMEM],
        out_shape=[held(split, rows, depth)],
        compiler_params=params(8),
        cost_estimate=cost(20 * cells, 15 * cells),
        name="stencil_second_low",
    )(*near_core(s_first, s_mid, tx, ty, tz, st))

    mortar_cost = cost(4 * blocks * blocks * width + 6 * kinds * blocks * width * width, 14 * rows * depth)
    w_last, jump, jump_sums = pl.pallas_call(
        jump_first_kernel,
        in_specs=[VMEM] * 7,
        out_specs=[VMEM] * 3,
        out_shape=[held(rows, depth), held(rows, depth), held(SUB, LANES)],
        compiler_params=params(16),
        cost_estimate=mortar_cost,
        name="jump_first",
    )(*near_core(image_low, b, face_right, s_last, picks, codes, proj_t))
    (kinds_by_block,) = pl.pallas_call(
        kinds_kernel,
        in_specs=[VMEM] * 2,
        out_specs=[VMEM],
        out_shape=[held(SUB, depth)],
        compiler_params=params(8),
        cost_estimate=cost(16 * blocks * blocks, 2 * blocks * blocks),
        name="kinds",
    )(*near_core(code_row, picks))
    (back,) = pl.pallas_call(
        back_first_kernel,
        in_specs=[VMEM] * 5,
        out_specs=[VMEM],
        out_shape=[held(rows + SUB, depth)],
        compiler_params=params(16),
        cost_estimate=mortar_cost,
        name="back_first",
    )(*near_core(jump, kinds_by_block, puts, codes, proj_n))

    split = layers // 2
    image_high, high_sums = pl.pallas_call(
        second_high_kernel,
        in_specs=[VMEM] * 11,
        out_specs=[VMEM] * 2,
        out_shape=[held(layers - split, rows, depth), held(SUB, LANES)],
        scratch_shapes=[pltpu.VMEM((6, SUB, LANES), F32)],
        compiler_params=params(8),
        cost_estimate=cost(20 * cells, 15 * cells),
        name="stencil_second_high",
    )(*near_core(back, first_sums, jump_sums, b, s_mid, s_last, w_last, tx, ty, tz, st))
    up_out, down_out = pl.pallas_call(
        rows_kernel,
        in_specs=[VMEM] * 7,
        out_specs=[VMEM] * 2,
        out_shape=[held(3 * layers + 3, depth), held(2 * layers + 2, depth)],
        compiler_params=params(2),
        cost_estimate=cost(0, 64 * depth),
        name="rows",
    )(*near_core(face_right, b, ty, s_first, s_mid, w_last, back))
    (back,) = pl.pallas_call(
        wait_kernel,
        in_specs=[VMEM] * 2,
        out_specs=[VMEM],
        out_shape=[held(rows + SUB, depth)],
        input_output_aliases={1: 0},
        compiler_params=params(2),
        cost_estimate=cost(0, 8 * depth),
        name="wait",
    )(*near_core(up_out, back))
    recv = shifted(back, "sub", 1)
    up = shifted(up_out, "blk", 1)
    down = shifted(down_out, "blk", -1)
    s_first, s_mid, s_last, w_last, image_low, edge_sums, image_ends, ends_sums, right_edges, missing, w_up, w_down = pl.pallas_call(
        edge_kernel,
        in_specs=[VMEM] * 15,
        out_specs=[VMEM] * 12,
        out_shape=[held(rows, depth), held(layers - 2, rows, depth), held(rows, depth), held(rows, depth)]
        + [held(split, rows, depth), held(SUB, LANES), held(layers - split, 2 * SUB, depth), held(SUB, LANES)]
        + [held(2, depth), held(2, depth), held(layers, depth), held(layers, depth)],
        input_output_aliases={10: 0, 11: 1, 12: 2, 13: 3, 14: 4},
        compiler_params=params(4),
        cost_estimate=cost(320 * depth, 640 * depth),
        name="edges_first",
    )(
        *near_core(
            first_sums, high_sums, b, face_right, up, down, tx, ty, tz, st, s_first, s_mid, s_last, w_last, image_low,
        )
    )

    jump_next, second_sums = pl.pallas_call(
        jump_second_kernel,
        in_specs=[VMEM] * 11,
        out_specs=[VMEM] * 2,
        out_shape=[held(rows, depth), held(SUB, LANES)],
        scratch_shapes=[pltpu.VMEM((rows, depth), F32)],
        compiler_params=params(16),
        cost_estimate=mortar_cost,
        name="jump_second",
    )(
        *near_core(
            high_sums, w_last, jump, face_right, face_right_next, right_edges, back, missing, picks, codes, proj_t,
        )
    )
    (back_next,) = pl.pallas_call(
        back_second_kernel,
        in_specs=[VMEM] * 5,
        out_specs=[VMEM],
        out_shape=[held(rows + SUB, depth)],
        compiler_params=params(16),
        cost_estimate=mortar_cost,
        name="back_second",
    )(*near_core(w_last, missing, puts, codes, proj_n))

    (back_next,) = pl.pallas_call(
        hold_kernel,
        in_specs=[VMEM] * 3,
        out_specs=[VMEM],
        out_shape=[held(rows + SUB, depth)],
        input_output_aliases={2: 0},
        compiler_params=params(2),
        cost_estimate=cost(0, 8 * depth),
        name="hold",
    )(*near_core(second_sums, recv, back_next))
    recv_next = shifted(back_next, "sub", 1)

    count = subs * blks
    image_low, edge_high, table = pl.pallas_call(
        second_added_kernel,
        in_specs=[VMEM] * 18,
        out_specs=[VMEM] * 3,
        out_shape=[
            held(split, rows, depth), held(2 * (layers - split), depth), held(-(-count * FIELDS // LANES), LANES),
        ],
        input_output_aliases={17: 0},
        scratch_shapes=[pltpu.VMEM((6, SUB, LANES), F32)],
        compiler_params=params(8),
        cost_estimate=cost(20 * cells, 15 * cells),
        name="stencil_second_added",
    )(
        *near_core(
            edge_sums, jump_sums, high_sums, ends_sums, second_sums, b, s_first, s_mid, w_last, recv,
            w_up, w_down, up, tx, ty, tz, st, image_low,
        )
    )
    (own_next,) = pl.pallas_call(
        own_second_kernel,
        in_specs=[VMEM] * 4,
        out_specs=[VMEM],
        out_shape=[held(rows, depth)],
        compiler_params=params(16),
        cost_estimate=mortar_cost,
        name="own_second",
    )(*near_core(s_first, recv, proj_t, proj_n))
    tables = gather_rows(table, own_next)

    return pl.pallas_call(
        final_kernel,
        in_specs=[VMEM] * 13,
        out_specs=[HBM] * 2,
        out_shape=[jax.ShapeDtypeStruct((layers, rows, depth), F32)] * 2,
        scratch_shapes=[pltpu.VMEM((layers, rows, depth), F32)] * 2 + [pltpu.SemaphoreType.DMA((2, steps))],
        compiler_params=params(8),
        cost_estimate=cost(8 * cells, 22 * cells),
        name="final_update",
    )(*near_core(tables, b, s_first, s_mid, w_last, recv, image_low, image_high, image_ends, edge_high, jump_next, recv_next, own_next))


def solution(mesh):
    cells = P("sub", "blk", None)
    in_specs = (cells,) * 7 + (P("sub", "blk"), P())
    return jax.shard_map(body, mesh=mesh, in_specs=in_specs, out_specs=(cells, cells), check_vma=False)
```

```python
import jax
import jax.numpy as jnp
from jax import lax
from jax.experimental import pallas as pl
from jax.experimental.pallas import tpu as pltpu
from jax.sharding import PartitionSpec as P

ROWS = 32
FIELDS = 16
SUB = 8
LANES = 128
F32 = jnp.float32
BF16 = jnp.bfloat16
penalty = 4.0


def tile_ids(dim, shape):
    return lax.broadcasted_iota(jnp.int32, shape, dim)


def as_tile(scalars):
    lane = tile_ids(1, (SUB, LANES))
    tile = jnp.zeros((SUB, LANES), F32)
    for place, value in enumerate(scalars):
        tile = jnp.where(lane == place, value, tile)
    return tile


def from_tile(tile, place):
    pick = (tile_ids(1, tile.shape) == place) & (tile_ids(0, tile.shape) == 0)
    return jnp.sum(jnp.where(pick, tile, 0.0))


def fold(array):
    parts = [array[:, place : place + LANES] for place in range(0, array.shape[1], LANES)]
    while len(parts) > 1:
        parts = [one + other for one, other in zip(parts[::2], parts[1::2])]
    return parts[0]


def at(array, layers, start):
    return [array[layer, pl.ds(start, SUB), :] for layer in range(layers)]


def stencil(values, after, tx, ty, tz, st, carry, below=None, above=None):
    shape = values[0].shape
    row = tile_ids(0, shape)
    last_z = tile_ids(1, shape) == shape[1] - 1
    results, carries = [], []
    flux_x = None if below is None else below[1] * (below[0] - values[0])
    for layer, value in enumerate(values):
        follow = value if after is None else pltpu.roll(after[layer], SUB - 1, 0)
        follow = jnp.where(row == SUB - 1, follow, pltpu.roll(value, SUB - 1, 0))
        flux_y = ty[layer] * (value - follow)
        rolled = pltpu.roll(flux_y, 1, 0)
        carries.append(rolled)
        flux_z = jnp.where(last_z, 0.0, tz[layer] * (value - pltpu.roll(value, shape[1] - 1, 1)))
        result = st[layer] * value + (flux_y - jnp.where(row == 0, carry[layer], rolled))
        result = result + (flux_z - pltpu.roll(flux_z, 1, 1))
        if flux_x is not None:
            result = result - flux_x
        next_x = values[layer + 1] if layer < len(values) - 1 else above
        flux_x = None
        if next_x is not None:
            flux_x = tx[layer] * (value - next_x)
            result = result + flux_x
        results.append(result)
    return results, carries


def at_last_block():
    return lax.axis_index("blk") == lax.axis_size("blk") - 1


def edge_terms(before, first, last, beyond, ty_before, ty_last):
    low = ty_before * (first - before)
    high = jnp.where(at_last_block(), 0.0, ty_last * (last - beyond))
    return low, high


def pack_kernel(b_hbm, ty_hbm, face, sems):
    rows = b_hbm.shape[1]
    copies = [
        pltpu.make_async_copy(b_hbm.at[0], face.at[pl.ds(0, rows), :], sems.at[0]),
        pltpu.make_async_copy(ty_hbm.at[0, pl.ds(rows - SUB, SUB), :], face.at[pl.ds(rows, SUB), :], sems.at[1]),
    ]
    for copy in copies:
        copy.start()
    for copy in copies:
        copy.wait()


def two_parts(array):
    high = array.astype(BF16)
    return high, (array - high.astype(F32)).astype(BF16)


def prepare_pairs(perm, kind, count, proj, rows, groups, picks, puts, codes, code_row, proj_t, proj_n):
    kinds, width, _ = proj.shape
    blocks = rows * groups
    lane = tile_ids(1, (1, blocks))
    target = lax.rem(perm, groups) * rows + lax.div(perm, groups)
    shift = kinds.bit_length()
    keys = (target * (1 << shift) + jnp.where(lane < count, kind, kinds)).astype(F32)
    span = LANES // groups
    spread = tile_ids(1, (span, LANES)) - groups * tile_ids(0, (span, LANES))
    lanes = tile_ids(1, (rows, LANES))
    across = []
    for group in range(groups):
        column = jnp.concatenate(
            [
                jnp.sum(jnp.where(spread == group, keys[:, place * LANES : (place + 1) * LANES], 0.0), 1, keepdims=True)
                for place in range(blocks // LANES)
            ],
            axis=0,
        ).astype(jnp.int32)
        column = jnp.broadcast_to(column, (rows, LANES))
        here = pl.ds(group * rows, rows)
        for place in range(rows // LANES):
            turned = jnp.transpose(column[place * LANES : (place + 1) * LANES].astype(F32))
            across.append(turned[0:1, :].astype(jnp.int32))
        codes[here, :] = column & ((1 << shift) - 1)
        column = column >> shift
        for place in range(blocks // LANES):
            picks[here, pl.ds(place * LANES, LANES)] = jnp.where(column == lanes + place * LANES, 1.0, 0.0).astype(BF16)
    across = jnp.concatenate(across, axis=1)
    code_row[...] = (kinds - (across & ((1 << shift) - 1))).astype(F32)
    across = across >> shift
    down = tile_ids(0, (rows, blocks))
    for group in range(groups):
        puts[pl.ds(group * rows, rows), :] = jnp.where(across == down + group * rows, 1.0, 0.0).astype(BF16)
    for kind in range(kinds):
        here = pl.ds(kind * width, width)
        proj_t[here, :] = jnp.concatenate(two_parts(jnp.transpose(proj[kind])), axis=1)
        proj_n[here, :] = jnp.concatenate(two_parts(proj[kind]), axis=1)


def first_kernel(
    count, perm, kind, proj, b_hbm, tx_hbm, ty_hbm, tz_hbm, st_hbm,
    b, tx, ty, tz, st, face_next, s_first, s_mid, s_last, sums, picks, puts, codes, code_row, proj_t, proj_n, total, sems,
):
    layers, rows, depth = b.shape
    steps = rows // ROWS
    sources, targets = (b_hbm, tx_hbm, ty_hbm, tz_hbm, st_hbm), (b, tx, ty, tz, st)

    def copy(which, step):
        part = pl.ds(step * ROWS, ROWS)
        return pltpu.make_async_copy(
            sources[which].at[:, part, :], targets[which].at[:, part, :], sems.at[which, step]
        )

    for step in range(steps):
        for which in range(len(sources)):
            copy(which, step).start()
    width = proj.shape[1]
    prepare_pairs(
        perm[0], kind[0], count[0, 0], proj, rows, depth // width, picks, puts, codes, code_row, proj_t, proj_n
    )
    total[...] = jnp.zeros_like(total)
    copy(0, 0).wait()

    def chunk(start, after, carry):
        values = at(b, layers, start)
        results, carry = stencil(values, after, *[at(array, layers, start) for array in (tx, ty, tz, st)], carry)
        here = pl.ds(start, SUB)
        squares, products = values[0] * values[0], values[0] * results[0]
        for layer in range(1, layers):
            squares = squares + values[layer] * values[layer]
            products = products + values[layer] * results[layer]
        total[0] += fold(squares)
        total[1] += fold(products)
        face_next[here, :] = results[0]
        s_first[here, :] = results[0]
        for layer in range(1, layers - 1):
            s_mid[layer - 1, here, :] = results[layer]
        s_last[here, :] = results[layers - 1]
        return carry

    carry = [jnp.zeros((SUB, depth), F32)] * layers
    for step in range(steps):
        for which in range(1, len(sources)):
            copy(which, step).wait()
        if step < steps - 1:
            copy(0, step + 1).wait()
        for start in range(step * ROWS, (step + 1) * ROWS, SUB):
            carry = chunk(start, None if start == rows - SUB else at(b, layers, start + SUB), carry)
    sums[...] = as_tile([jnp.sum(total[0]), jnp.sum(total[1])])


def up_places(layers):
    return 0, layers, 2 * layers, 3 * layers, 3 * layers + 1, 3 * layers + 2


def edge_kernel(
    sums_in, near_sums, b, right, up, down, tx, ty, tz, st, s_first_in, s_mid_in, s_last_in, w_last_in, image_low_in,
    s_first, s_mid, s_last, w_last, image_low, sums, image_ends, ends_sums, right_edges, missing, w_up, w_down,
):
    layers, rows, depth = b.shape
    at_b, at_ty, at_w, at_back, at_right, at_right_ty = up_places(layers)
    product = 0.0
    for layer in range(layers):
        first, last = b[layer, 0:1, :], b[layer, rows - 1 :, :]
        low, high = edge_terms(
            up[at_b + layer : at_b + layer + 1, :], first, last, down[layer : layer + 1, :],
            up[at_ty + layer : at_ty + layer + 1, :], ty[layer, rows - 1 :, :],
        )
        pairs = [(s_first_in, s_first)] if layer == 0 else [(s_last_in, s_last), (w_last_in, w_last)]
        if 0 < layer < layers - 1:
            pairs = [(s_mid_in.at[layer - 1], s_mid.at[layer - 1])]
        for source, target in pairs:
            target[0:1, :] = source[0:1, :] + low
            target[rows - 1 :, :] = source[rows - 1 :, :] + high
        product = product + first * low + last * high
        w_up[layer : layer + 1, :] = up[at_w + layer : at_w + layer + 1, :] - low
        w_down[layer : layer + 1, :] = down[layers + layer : layers + layer + 1, :] - high
    sums[...] = sums_in[...] + as_tile([0.0, jnp.sum(product)])
    low, high = edge_terms(
        up[at_right : at_right + 1, :], right[0:1, :], right[rows - 1 : rows, :], down[2 * layers + 1 :, :],
        up[at_right_ty : at_right_ty + 1, :], right[rows + SUB - 1 :, :],
    )
    right_edges[0:1, :] = low
    right_edges[1:2, :] = high
    missing[0:1, :] = -up[at_right_ty : at_right_ty + 1, :] * up[at_back : at_back + 1, :]
    missing[1:2, :] = jnp.where(
        at_last_block(), 0.0, -right[rows + SUB - 1 :, :] * down[2 * layers : 2 * layers + 1, :]
    )
    near = from_tile(near_sums[...], 2)
    own, read, plain = high_layers(layers, s_mid, s_last, w_last)
    terms = None
    for place, start in enumerate((0, rows - SUB)):
        values = read(start)
        if place == 0:
            after, carry = read(SUB), [jnp.zeros((SUB, depth), F32)] * len(own)
        else:
            after, carry = None, flux_from(start - SUB, own, read, 1, ty)
        new, _ = chunk_sums(
            start, values, after, carry, own, near, b, plain, tx, ty, tz, st, image_ends, place * SUB
        )
        terms = new if terms is None else [old + more for old, more in zip(terms, new)]
    ends_sums[...] = as_tile([0.0] * 3 + [jnp.sum(term) for term in terms])
    own, read = low_layers(layers, s_first, s_mid)
    zero = [jnp.zeros((SUB, depth), F32)] * len(own)
    low_chunk(0, read(0), read(SUB), zero, own, tx, ty, tz, st, image_low)
    carry = flux_from(rows - 2 * SUB, own, read, 0, ty)
    low_chunk(rows - SUB, read(rows - SUB), None, carry, own, tx, ty, tz, st, image_low)


def high_layers(layers, s_mid, s_last, w_last):
    split = layers // 2

    def read(start):
        here = pl.ds(start, SUB)
        return [s_mid[layer - 1, here, :] for layer in range(split - 1, layers - 1)] + [w_last[here, :]]

    def plain(layer, here):
        return s_last[here, :] if layer == layers - 1 else s_mid[layer - 1, here, :]

    return list(range(split, layers)), read, plain


def flux_from(start, own, read, skip, ty):
    row = None
    carry = []
    for layer, value, after in zip(own, read(start)[skip:], read(start + SUB)[skip:]):
        row = tile_ids(0, value.shape)
        follow = jnp.where(row == SUB - 1, pltpu.roll(after, SUB - 1, 0), pltpu.roll(value, SUB - 1, 0))
        carry.append(pltpu.roll(ty[layer, pl.ds(start, SUB), :] * (value - follow), 1, 0))
    return carry


def chunk_sums(start, values, after, carry, own, near, b, plain, tx, ty, tz, st, image, target, summed=None):
    layers = b.shape[0]
    here = pl.ds(start, SUB)
    below = (values[0], tx[own[0] - 1, here, :]) if own[0] > 0 else None
    above = values[-1] if own[-1] < layers - 1 else None
    skip = 0 if below is None else 1
    mine = values[skip : skip + len(own)]
    results, carry = stencil(
        mine, None if after is None else after[skip : skip + len(own)],
        *[[array[layer, here, :] for layer in own] for array in (tx, ty, tz, st)], carry, below, above,
    )
    terms = None
    for place, layer in enumerate(own):
        w, s = mine[place], results[place]
        image[place, pl.ds(target, SUB), :] = s
        if summed is not None and layer not in summed:
            continue
        u = b[layer, here, :] - near * w
        q = plain(layer, here) - near * s
        new = [fold(term) for term in (u * u, u * w, w * w, u * q, u * s + w * q, w * s)]
        terms = new if terms is None else [old + more for old, more in zip(terms, new)]
    return terms, carry


def mm(left, right):
    return lax.dot_general(left, right, (((1,), (0,)), ((), ())), preferred_element_type=F32)


def by_kind(codes, array, kinds):
    zero = jnp.zeros_like(array)
    return jnp.concatenate([jnp.where(codes == kind, array, zero) for kind in range(kinds)], axis=1)


def apply_proj(codes, high, low, proj, kinds, width):
    both = mm(by_kind(codes, high, kinds), proj[...])
    return both[:, :width] + both[:, width:] + mm(by_kind(codes, low, kinds), proj[:, :width])


def take_jump(group, faces, last, picks, codes_col, proj_t):
    width = proj_t.shape[1] // 2
    kinds = proj_t.shape[0] // width
    here = pl.ds(group * last.shape[0], last.shape[0])
    codes = codes_col[here, :]
    taken = mm(picks[here, :], faces)
    projected = apply_proj(codes, taken[:, :width].astype(BF16), taken[:, width:].astype(BF16), proj_t, kinds, width)
    return jnp.where(codes < kinds, last - projected, 0.0)


def turn_back(group, jump, codes_col, proj_n):
    width = proj_n.shape[1] // 2
    kinds = proj_n.shape[0] // width
    scale = jnp.where(lax.axis_index("sub") < lax.axis_size("sub") - 1, -penalty, 0.0)
    codes = codes_col[pl.ds(group * jump.shape[0], jump.shape[0]), :]
    return jnp.concatenate(two_parts(scale * apply_proj(codes, *two_parts(jump), proj_n, kinds, width)), axis=1)


def put_back(group, backs, puts, rows):
    width = backs.shape[1] // 2
    placed = mm(puts[pl.ds(group * rows, rows), :], backs)
    return placed[:, :width] + placed[:, width:]


def stack_parts(parts):
    return jnp.concatenate(two_parts(jnp.concatenate(parts, axis=0)), axis=1)


def jump_first_kernel(earlier, b, right, s_last, picks, codes, proj_t, w_last, jump_face, sums):
    width = proj_t.shape[1] // 2
    layers, rows, depth = b.shape
    parts = [pl.ds(group * width, width) for group in range(depth // width)]
    faces = stack_parts([right[:rows, part] for part in parts])
    square = jnp.zeros((rows, width), F32)
    for group, part in enumerate(parts):
        jump = take_jump(group, faces, b[layers - 1, :, part], picks, codes, proj_t)
        square = square + jump * jump
        jump_face[:, part] = jump
        w_last[:, part] = s_last[:, part] + penalty * jump
    sums[...] = as_tile([jnp.sum(square)])


def kinds_kernel(code_row, picks, proj_t, proj_n, kinds_by_block, squares):
    width = proj_t.shape[1] // 2
    for kind in range(proj_t.shape[0] // width):
        here = pl.ds(kind * width, width)
        left, right = proj_t[here, :], proj_n[here, :]
        both = mm(left[:, :width], right)
        square = both[:, :width] + both[:, width:] + mm(left[:, width:], right[:, :width])
        squares[here, :] = jnp.concatenate(two_parts(square), axis=1)
    depth = kinds_by_block.shape[1]
    row = mm(jnp.broadcast_to(code_row[...], (2 * SUB, code_row.shape[1])).astype(BF16), picks[...])
    kinds_by_block[...] = jnp.zeros_like(kinds_by_block)
    for place in range(row.shape[1] // depth):
        kinds_by_block[place : place + 1, :] = row[0:1, place * depth : (place + 1) * depth]


def rows_kernel(right, b, ty, s_first, s_mid, w_last, back, up, down):
    layers, rows, _ = b.shape
    at_b, at_ty, at_w, at_back, at_right, at_right_ty = up_places(layers)
    end = pl.ds(rows - 1, 1)
    for layer in range(layers):
        image = s_first if layer == 0 else w_last if layer == layers - 1 else s_mid.at[layer - 1]
        up[at_b + layer : at_b + layer + 1, :] = b[layer, end, :]
        up[at_ty + layer : at_ty + layer + 1, :] = ty[layer, end, :]
        up[at_w + layer : at_w + layer + 1, :] = image[end, :]
        down[layer : layer + 1, :] = b[layer, 0:1, :]
        down[layers + layer : layers + layer + 1, :] = image[0:1, :]
    up[at_back : at_back + 1, :] = back[end, :]
    up[at_right : at_right + 1, :] = right[end, :]
    up[at_right_ty : at_right_ty + 1, :] = right[rows + SUB - 1 :, :]
    down[2 * layers : 2 * layers + 1, :] = back[0:1, :]
    down[2 * layers + 1 : 2 * layers + 2, :] = right[0:1, :]


def jump_second_kernel(
    near_sums, w_last, jump, right_before, right, right_edges, back_before, missing, picks, codes, proj_t,
    jump_next, sums, field,
):
    width = proj_t.shape[1] // 2
    rows, depth = right.shape
    parts = [pl.ds(group * width, width) for group in range(depth // width)]
    near = from_tile(near_sums[...], 2)
    field[...] = right[...] + back_before[:rows, :]
    field[0:1, :] += right_edges[0:1, :]
    field[rows - 1 :, :] += right_edges[1:2, :]
    faces = stack_parts([field[:, part] for part in parts])
    totals = [jnp.zeros((rows, width), F32)] * 3
    for group, part in enumerate(parts):
        later = take_jump(group, faces, w_last[:, part], picks, codes, proj_t)
        jump_next[:, part] = later
        close = jump[:, part] - near * later
        totals = [total + new for total, new in zip(totals, (close * close, close * later, later * later))]
    found = [jnp.sum(total) for total in totals]
    found = [penalty * found[0], 2.0 * penalty * found[1], penalty * found[2]]
    extra = [0.0] * 3
    for side, place in enumerate((0, rows - 1)):
        s = missing[side : side + 1, :]
        w = field[place : place + 1, :]
        u = right_before[place : place + 1, :] - near * w
        extra = [old + more for old, more in zip(extra, [-near * u * s, u * s - near * w * s, w * s])]
    sums[...] = as_tile([0.0] * 6 + [old + jnp.sum(more) for old, more in zip(found, extra)])


def back_first_kernel(jump, kinds_by_block, puts, codes, proj_n, back):
    rows = jump.shape[0]
    back_kernel(jump, puts, codes, proj_n, back)
    back[rows:, :] = kinds_by_block[...]


def back_second_kernel(w_last, missing, puts, codes, proj_n, back):
    rows = w_last.shape[0]
    back_kernel(w_last, puts, codes, proj_n, back)
    back[rows : rows + 2, :] = missing[...]


def own_second_kernel(s_first, recv, squares, own):
    rows, depth = own.shape
    width = squares.shape[1] // 2
    kinds = squares.shape[0] // width
    for group in range(depth // width):
        part = pl.ds(group * width, width)
        codes = []
        for place in range(rows // LANES):
            start = group * rows + place * LANES
            row = recv[rows + start // depth : rows + start // depth + 1, start % depth : start % depth + LANES]
            codes.append(jnp.transpose(jnp.broadcast_to(row, (LANES, LANES))))
        codes = kinds - jnp.concatenate(codes, axis=0).astype(jnp.int32)
        field = s_first[:, part] + recv[:rows, part]
        own[:, part] = penalty * apply_proj(codes, *two_parts(field), squares, kinds, width)


def hold_kernel(later, back_in, back):
    back[back.shape[0] - SUB + 2 :, :] = jnp.zeros((SUB - 2, back.shape[1]), F32)


def back_kernel(jump_next, puts, codes, proj_n, back):
    width = proj_n.shape[1] // 2
    rows, depth = jump_next.shape
    parts = [pl.ds(group * width, width) for group in range(depth // width)]
    backs = [turn_back(group, jump_next[:, part], codes, proj_n) for group, part in enumerate(parts)]
    backs = jnp.concatenate(backs, axis=0)
    for group, part in enumerate(parts):
        back[:rows, part] = put_back(group, backs, puts, rows)


def stencil_sums(read, own, near, b, plain, tx, ty, tz, st, image, total, inner, summed=None):
    layers, rows, depth = b.shape
    total[...] = jnp.zeros_like(total)
    skip = 1 if own[0] > 0 else 0

    def several(start, count, carry, at_end=False):
        starts = [pl.multiple_of(start + SUB * place, SUB) for place in range(count + 1)]
        values = [read(place) for place in starts[:-1]] + [None if at_end else read(starts[-1])]
        terms = None
        for place in range(count):
            new, carry = chunk_sums(
                starts[place], values[place], values[place + 1], carry, own, near, b, plain, tx, ty, tz, st, image,
                starts[place], summed,
            )
            terms = new if terms is None else [old + more for old, more in zip(terms, new)]
        for place, term in enumerate(terms):
            total[place] += term
        return carry

    group = 2
    if inner:
        begin, count, carry = SUB, (rows // SUB - 2) // group, flux_from(0, own, read, skip, ty)
    else:
        begin, count, carry = 0, rows // (group * SUB) - 1, [jnp.zeros((SUB, depth), F32)] * len(own)
    carry = lax.fori_loop(
        0, count,
        lambda index, carry: tuple(
            several(pl.multiple_of(begin + index * group * SUB, SUB), group, list(carry))
        ),
        tuple(carry),
    )
    if not inner:
        several(rows - group * SUB, group, list(carry), True)
    return [jnp.sum(total[place]) for place in range(total.shape[0])]


def second_high_kernel(later, first_sums, jump_sums, b, s_mid, s_last, w_last, tx, ty, tz, st, image, sums, total):
    norm = from_tile(first_sums[...], 0)
    energy = from_tile(first_sums[...], 1) + penalty * from_tile(jump_sums[...], 0)
    safe = energy > 0.01 * norm
    ratio = jnp.full((SUB, LANES), norm, F32) / jnp.full((SUB, LANES), jnp.where(safe, energy, 1.0), F32)
    near = jnp.where(safe, jnp.max(ratio), 0.0)
    own, read, plain = high_layers(b.shape[0], s_mid, s_last, w_last)
    found = stencil_sums(read, own, near, b, plain, tx, ty, tz, st, image, total, True)
    sums[...] = as_tile([0.0, 0.0, near] + found)


def low_layers(layers, s_first, s_mid):
    split = layers // 2

    def read(start):
        here = pl.ds(start, SUB)
        return [s_first[here, :]] + [s_mid[layer - 1, here, :] for layer in range(1, split + 1)]

    return list(range(split)), read


def low_chunk(start, values, after, carry, own, tx, ty, tz, st, image):
    here = pl.ds(start, SUB)
    results, carry = stencil(
        values[:-1], None if after is None else after[:-1],
        *[[array[layer, here, :] for layer in own] for array in (tx, ty, tz, st)], carry, None, values[-1],
    )
    for layer in own:
        image[layer, here, :] = results[layer]
    return carry


def second_low_kernel(s_first, s_mid, tx, ty, tz, st, image):
    layers, rows = tx.shape[:2]
    own, read = low_layers(layers, s_first, s_mid)
    group = 3

    def several(index, carry):
        start = pl.multiple_of(SUB + index * group * SUB, SUB)
        starts = [pl.multiple_of(start + SUB * place, SUB) for place in range(group + 1)]
        values = [read(place) for place in starts]
        carry = list(carry)
        for place in range(group):
            carry = low_chunk(starts[place], values[place], values[place + 1], carry, own, tx, ty, tz, st, image)
        return tuple(carry)

    lax.fori_loop(0, (rows // SUB - 2) // group, several, tuple(flux_from(0, own, read, 0, ty)))


def second_added_kernel(
    first_sums, jump_sums, high_sums, ends_sums, second_sums, b, s_first, s_mid, w_last, recv,
    w_up, w_down, up, tx, ty, tz, st, image_in, image, edge_high, table, total,
):
    layers, rows, depth = b.shape
    split = layers // 2
    near = from_tile(high_sums[...], 2)
    total[...] = jnp.zeros_like(total)
    first, second = 0, 1

    def several(start, count, carry, at_end=False):
        starts = [pl.multiple_of(start + SUB * place, SUB) for place in range(count + 1)]
        added = [recv[pl.ds(place, SUB), :] for place in starts[:-1]]
        added.append(None if at_end else recv[pl.ds(starts[-1], SUB), :])
        terms = None
        for place in range(count):
            here = pl.ds(starts[place], SUB)
            e, t_x = added[place], tx[first, here, :]
            (s,), carry = stencil(
                [e], None if added[place + 1] is None else [added[place + 1]], [t_x], [ty[first, here, :]],
                [tz[first, here, :]], [st[first, here, :] + t_x], carry,
            )
            s = image_in[first, here, :] + s
            image[first, here, :] = s
            plain = s_first[here, :]
            w = plain + e
            u = b[first, here, :] - near * w
            q = plain - near * s
            new = [u * u, u * w, w * w, u * q, u * s + w * q, w * s]
            s = image_in[second, here, :] - t_x * e
            image[second, here, :] = s
            w = s_mid[second - 1, here, :]
            u = b[second, here, :] - near * w
            q = w - near * s
            more = [u * u, u * w, w * w, u * q, u * s + w * q, w * s]
            new = [fold(one + other) for one, other in zip(new, more)]
            terms = new if terms is None else [old + more for old, more in zip(terms, new)]
        for place, term in enumerate(terms):
            total[place] += term
        return carry

    group = 4
    carry = lax.fori_loop(
        0, rows // (group * SUB) - 1,
        lambda index, carry: several(pl.multiple_of(index * group * SUB, SUB), group, [carry])[0],
        jnp.zeros((SUB, depth), F32),
    )
    several(rows - group * SUB, group, [carry], True)
    found = [jnp.sum(total[place]) for place in range(total.shape[0])]

    def row(layer, place):
        here = pl.ds(place, 1)
        if layer == 0:
            return s_first[here, :] + recv[here, :]
        return w_last[here, :] if layer == layers - 1 else s_mid[layer - 1, here, :]

    extra = [jnp.zeros((1, depth), F32)] * 3
    for layer in range(layers):
        ends = row(layer, 0), row(layer, rows - 1)
        added = edge_terms(
            w_up[layer : layer + 1, :], *ends, w_down[layer : layer + 1, :],
            up[layers + layer : layers + layer + 1, :], ty[layer, rows - 1 :, :],
        )
        for side, (place, w, s) in enumerate(zip((0, rows - 1), ends, added)):
            u = b[layer, place : place + 1, :] - near * w
            extra = [old + more for old, more in zip(extra, [-near * u * s, u * s - near * w * s, w * s])]
            if layer < split:
                image[layer, place : place + 1, :] += s
            else:
                spot = side * (layers - split) + layer - split
                edge_high[spot : spot + 1, :] = s
    found[3:] = [old + jnp.sum(more) for old, more in zip(found[3:], extra)]
    norm = from_tile(first_sums[...], 0)
    energy = from_tile(first_sums[...], 1) + penalty * from_tile(jump_sums[...], 0)
    sums = high_sums[...] + ends_sums[...] + second_sums[...]
    sums = sums + as_tile([norm, energy, 0.0] + found)
    mine = lax.axis_index("sub") * lax.axis_size("blk") + lax.axis_index("blk")
    device = tile_ids(0, table.shape) * (LANES // FIELDS) + lax.div(tile_ids(1, table.shape), FIELDS)
    field = lax.rem(tile_ids(1, table.shape), FIELDS)
    filled = jnp.zeros(table.shape, F32)
    for place in range(9):
        filled = jnp.where((device == mine) & (field == place), jnp.sum(sums[0:1, place : place + 1]), filled)
    table[...] = filled


def add_kernel(earlier, one, other, both):
    both[...] = one[...] + other[...]


def final_kernel(
    tables, b, s_first, s_mid, w_last, recv, image_low, image_high, image_ends, edge_high, jump_next, recv_next, own_next, solution_hbm, residual_hbm,
    solution, residual, sems,
):
    layers, rows, depth = b.shape
    split = image_low.shape[0]
    flat = tables[...]
    norm, energy, near, uu, uw, ww, uq, cross, wq = [
        flat if place == 0 else pltpu.roll(flat, LANES - place, 1) for place in range(9)
    ]
    own = lax.rem(tile_ids(1, flat.shape), FIELDS) == 0

    def whole(array):
        array = jnp.sum(jnp.where(own, array, 0.0), axis=0, keepdims=True)
        return jnp.sum(array, axis=1, keepdims=True)

    norm, energy = whole(norm), whole(energy)
    alpha = norm / energy
    away = alpha - near
    norm_next = whole(uu - away * (2.0 * uw - away * ww))
    energy_next = whole(uq - away * (cross - away * wq))
    beta = norm_next / norm
    step_size = norm_next / (energy_next - beta * norm_next / alpha)
    c0 = jnp.broadcast_to(alpha + step_size * beta + step_size, (SUB, depth))
    c1 = jnp.broadcast_to(step_size * alpha, (SUB, depth))
    c2 = jnp.broadcast_to(alpha + step_size * (1.0 + beta), (SUB, depth))

    def copy(which, step):
        part = pl.ds(step * ROWS, ROWS)
        source, target = ((solution, solution_hbm), (residual, residual_hbm))[which]
        return pltpu.make_async_copy(source.at[:, part, :], target.at[:, part, :], sems.at[which, step])

    for step in range(rows // ROWS):
        for start in range(step * ROWS, (step + 1) * ROWS, SUB):
            here = pl.ds(start, SUB)
            for layer in range(layers):
                v = b[layer, here, :]
                if layer < split:
                    s = image_low[layer, here, :]
                elif start == 0:
                    s = image_ends[layer - split, :SUB, :]
                elif start == rows - SUB:
                    s = image_ends[layer - split, SUB:, :]
                else:
                    s = image_high[layer - split, here, :]
                if layer == 0:
                    w = s_first[here, :] + recv[here, :]
                    s = s + (recv_next[here, :] + own_next[here, :])
                elif layer < layers - 1:
                    w = s_mid[layer - 1, here, :]
                else:
                    w = w_last[here, :]
                    s = s + penalty * jump_next[here, :]
                solution[layer, here, :] = c0 * v - c1 * w
                residual[layer, here, :] = v - c2 * w + c1 * s
        for side, last_step in enumerate((0, rows // ROWS - 1)):
            if step == last_step:
                place = side * (rows - 1)
                residual[0, place : place + 1, :] += c1[0:1, :] * recv_next[rows + side : rows + side + 1, :]
                for layer in range(split, layers):
                    spot = side * (layers - split) + layer - split
                    residual[layer, place : place + 1, :] += c1[0:1, :] * edge_high[spot : spot + 1, :]
        for which in range(2):
            copy(which, step).start()
    for step in range(rows // ROWS):
        for which in range(2):
            copy(which, step).wait()


SMEM = pl.BlockSpec(memory_space=pltpu.SMEM)
VMEM = pl.BlockSpec(memory_space=pltpu.VMEM)
HBM = pl.BlockSpec(memory_space=pltpu.HBM)


def held(*dims, dtype=F32):
    return pltpu.VMEM(dims, dtype)


def near_core(*arrays):
    return [pltpu.with_memory_space_constraint(array, pltpu.VMEM) for array in arrays]


def in_hbm(*arrays):
    return [pltpu.with_memory_space_constraint(array, pltpu.HBM) for array in arrays]


def cost(flops, size):
    return pl.CostEstimate(flops=int(flops), bytes_accessed=int(size), transcendentals=0)


def params(mib):
    return pltpu.CompilerParams(vmem_limit_bytes=mib * 1024 * 1024)


def shifted(array, axis, by):
    size = lax.axis_size(axis)
    return lax.ppermute(array, axis, [(i, i + by) for i in range(size) if 0 <= i + by < size])


def gather_rows(table, own):
    subs, blks = lax.axis_size("sub"), lax.axis_size("blk")
    steps = [(0, 1)]
    reach = 2
    while reach < blks:
        steps.append((0, reach + 1))
        reach *= 2
    reach = subs // 2
    while reach > 0:
        steps.append((reach, 1))
        reach //= 2
    for place, (by_sub, by_blk) in enumerate(steps):
        pairs = [(s * blks + t, (s ^ by_sub) * blks + (t ^ by_blk)) for s in range(subs) for t in range(blks)]
        other = lax.ppermute(table, ("sub", "blk"), pairs)
        if place == 0:
            (table,) = pl.pallas_call(
                add_kernel,
                in_specs=[VMEM] * 3,
                out_specs=[VMEM],
                out_shape=[held(*table.shape)],
                compiler_params=params(2),
                cost_estimate=cost(table.size, 12 * table.size),
                name="add",
            )(*near_core(own, table, other))
        else:
            table = table + other
    return table


def body(right_side, trans_x, trans_y, trans_z, storage, pair_perm, pair_type, pair_count, proj):
    layers, rows, depth = right_side.shape
    blocks, width, kinds = pair_perm.shape[2], proj.shape[1], proj.shape[0]
    subs, blks = lax.axis_size("sub"), lax.axis_size("blk")
    steps = rows // ROWS
    cells = layers * rows * depth

    (face,) = pl.pallas_call(
        pack_kernel,
        in_specs=[HBM, HBM],
        out_specs=[VMEM],
        out_shape=[held(rows + SUB, depth)],
        scratch_shapes=[pltpu.SemaphoreType.DMA((2,))],
        compiler_params=params(2),
        cost_estimate=cost(0, 4 * rows * depth),
        name="pack",
    )(*in_hbm(right_side, trans_y))
    face_right = shifted(face, "sub", -1)

    b, tx, ty, tz, st, face_next, s_first, s_mid, s_last, first_sums, picks, puts, codes, code_row, proj_t, proj_n = pl.pallas_call(
        first_kernel,
        in_specs=[SMEM] + [VMEM] * 3 + [HBM] * 5,
        out_specs=[VMEM] * 16,
        out_shape=[held(layers, rows, depth)] * 5
        + [
            held(rows, depth), held(rows, depth), held(layers - 2, rows, depth), held(rows, depth), held(SUB, LANES),
            held(blocks, blocks, dtype=BF16), held(blocks, blocks, dtype=BF16), held(blocks, width, dtype=jnp.int32), held(1, blocks),
            held(kinds * width, 2 * width, dtype=BF16), held(kinds * width, 2 * width, dtype=BF16),
        ],
        scratch_shapes=[pltpu.VMEM((2, SUB, LANES), F32), pltpu.SemaphoreType.DMA((5, steps))],
        compiler_params=params(16),
        cost_estimate=cost(20 * cells, 24 * cells),
        name="stencil_first",
    )(
        pair_count, pair_perm, pair_type, proj,
        *in_hbm(right_side, trans_x, trans_y, trans_z, storage),
    )
    face_right_next = shifted(face_next, "sub", -1)

    split = layers // 2
    (image_low,) = pl.pallas_call(
        second_low_kernel,
        in_specs=[VMEM] * 6,
        out_specs=[VMEM],
        out_shape=[held(split, rows, depth)],
        compiler_params=params(8),
        cost_estimate=cost(20 * cells, 15 * cells),
        name="stencil_second_low",
    )(*near_core(s_first, s_mid, tx, ty, tz, st))

    mortar_cost = cost(4 * blocks * blocks * width + 6 * kinds * blocks * width * width, 14 * rows * depth)
    w_last, jump, jump_sums = pl.pallas_call(
        jump_first_kernel,
        in_specs=[VMEM] * 7,
        out_specs=[VMEM] * 3,
        out_shape=[held(rows, depth), held(rows, depth), held(SUB, LANES)],
        compiler_params=params(16),
        cost_estimate=mortar_cost,
        name="jump_first",
    )(*near_core(image_low, b, face_right, s_last, picks, codes, proj_t))
    kinds_by_block, squares = pl.pallas_call(
        kinds_kernel,
        in_specs=[VMEM] * 4,
        out_specs=[VMEM] * 2,
        out_shape=[held(SUB, depth), held(kinds * width, 2 * width, dtype=BF16)],
        compiler_params=params(8),
        cost_estimate=cost(16 * blocks * blocks, 2 * blocks * blocks),
        name="kinds",
    )(*near_core(code_row, picks, proj_t, proj_n))
    (back,) = pl.pallas_call(
        back_first_kernel,
        in_specs=[VMEM] * 5,
        out_specs=[VMEM],
        out_shape=[held(rows + SUB, depth)],
        compiler_params=params(16),
        cost_estimate=mortar_cost,
        name="back_first",
    )(*near_core(jump, kinds_by_block, puts, codes, proj_n))
    recv = shifted(back, "sub", 1)

    split = layers // 2
    image_high, high_sums = pl.pallas_call(
        second_high_kernel,
        in_specs=[VMEM] * 11,
        out_specs=[VMEM] * 2,
        out_shape=[held(layers - split, rows, depth), held(SUB, LANES)],
        scratch_shapes=[pltpu.VMEM((6, SUB, LANES), F32)],
        compiler_params=params(8),
        cost_estimate=cost(20 * cells, 15 * cells),
        name="stencil_second_high",
    )(*near_core(back, first_sums, jump_sums, b, s_mid, s_last, w_last, tx, ty, tz, st))
    up_out, down_out = pl.pallas_call(
        rows_kernel,
        in_specs=[VMEM] * 7,
        out_specs=[VMEM] * 2,
        out_shape=[held(3 * layers + 3, depth), held(2 * layers + 2, depth)],
        compiler_params=params(2),
        cost_estimate=cost(0, 64 * depth),
        name="rows",
    )(*near_core(face_right, b, ty, s_first, s_mid, w_last, back))
    up = shifted(up_out, "blk", 1)
    down = shifted(down_out, "blk", -1)
    s_first, s_mid, s_last, w_last, image_low, edge_sums, image_ends, ends_sums, right_edges, missing, w_up, w_down = pl.pallas_call(
        edge_kernel,
        in_specs=[VMEM] * 15,
        out_specs=[VMEM] * 12,
        out_shape=[held(rows, depth), held(layers - 2, rows, depth), held(rows, depth), held(rows, depth)]
        + [held(split, rows, depth), held(SUB, LANES), held(layers - split, 2 * SUB, depth), held(SUB, LANES)]
        + [held(2, depth), held(2, depth), held(layers, depth), held(layers, depth)],
        input_output_aliases={10: 0, 11: 1, 12: 2, 13: 3, 14: 4},
        compiler_params=params(4),
        cost_estimate=cost(320 * depth, 640 * depth),
        name="edges_first",
    )(
        *near_core(
            first_sums, high_sums, b, face_right, up, down, tx, ty, tz, st, s_first, s_mid, s_last, w_last, image_low,
        )
    )

    jump_next, second_sums = pl.pallas_call(
        jump_second_kernel,
        in_specs=[VMEM] * 11,
        out_specs=[VMEM] * 2,
        out_shape=[held(rows, depth), held(SUB, LANES)],
        scratch_shapes=[pltpu.VMEM((rows, depth), F32)],
        compiler_params=params(16),
        cost_estimate=mortar_cost,
        name="jump_second",
    )(
        *near_core(
            high_sums, w_last, jump, face_right, face_right_next, right_edges, back, missing, picks, codes, proj_t,
        )
    )
    (back_next,) = pl.pallas_call(
        back_second_kernel,
        in_specs=[VMEM] * 5,
        out_specs=[VMEM],
        out_shape=[held(rows + SUB, depth)],
        compiler_params=params(16),
        cost_estimate=mortar_cost,
        name="back_second",
    )(*near_core(w_last, missing, puts, codes, proj_n))

    (back_next,) = pl.pallas_call(
        hold_kernel,
        in_specs=[VMEM] * 2,
        out_specs=[VMEM],
        out_shape=[held(rows + SUB, depth)],
        input_output_aliases={1: 0},
        compiler_params=params(2),
        cost_estimate=cost(0, 8 * depth),
        name="hold",
    )(*near_core(second_sums, back_next))
    recv_next = shifted(back_next, "sub", 1)

    count = subs * blks
    image_low, edge_high, table = pl.pallas_call(
        second_added_kernel,
        in_specs=[VMEM] * 18,
        out_specs=[VMEM] * 3,
        out_shape=[
            held(split, rows, depth), held(2 * (layers - split), depth), held(-(-count * FIELDS // LANES), LANES),
        ],
        input_output_aliases={17: 0},
        scratch_shapes=[pltpu.VMEM((6, SUB, LANES), F32)],
        compiler_params=params(8),
        cost_estimate=cost(20 * cells, 15 * cells),
        name="stencil_second_added",
    )(
        *near_core(
            edge_sums, jump_sums, high_sums, ends_sums, second_sums, b, s_first, s_mid, w_last, recv,
            w_up, w_down, up, tx, ty, tz, st, image_low,
        )
    )
    (own_next,) = pl.pallas_call(
        own_second_kernel,
        in_specs=[VMEM] * 3,
        out_specs=[VMEM],
        out_shape=[held(rows, depth)],
        compiler_params=params(16),
        cost_estimate=mortar_cost,
        name="own_second",
    )(*near_core(s_first, recv, squares))
    tables = gather_rows(table, own_next)

    return pl.pallas_call(
        final_kernel,
        in_specs=[VMEM] * 13,
        out_specs=[HBM] * 2,
        out_shape=[jax.ShapeDtypeStruct((layers, rows, depth), F32)] * 2,
        scratch_shapes=[pltpu.VMEM((layers, rows, depth), F32)] * 2 + [pltpu.SemaphoreType.DMA((2, steps))],
        compiler_params=params(8),
        cost_estimate=cost(8 * cells, 22 * cells),
        name="final_update",
    )(*near_core(tables, b, s_first, s_mid, w_last, recv, image_low, image_high, image_ends, edge_high, jump_next, recv_next, own_next))


def solution(mesh):
    cells = P("sub", "blk", None)
    in_specs = (cells,) * 7 + (P("sub", "blk"), P())
    return jax.shard_map(body, mesh=mesh, in_specs=in_specs, out_specs=(cells, cells), check_vma=False)
```

```python
import jax
import jax.numpy as jnp
from jax import lax
from jax.experimental import pallas as pl
from jax.experimental.pallas import tpu as pltpu
from jax.sharding import PartitionSpec as P

ROWS = 32
FIELDS = 16
SUB = 8
LANES = 128
F32 = jnp.float32
BF16 = jnp.bfloat16
penalty = 4.0


def tile_ids(dim, shape):
    return lax.broadcasted_iota(jnp.int32, shape, dim)


def as_tile(scalars):
    lane = tile_ids(1, (SUB, LANES))
    tile = jnp.zeros((SUB, LANES), F32)
    for place, value in enumerate(scalars):
        tile = jnp.where(lane == place, value, tile)
    return tile


def from_tile(tile, place):
    pick = (tile_ids(1, tile.shape) == place) & (tile_ids(0, tile.shape) == 0)
    return jnp.sum(jnp.where(pick, tile, 0.0))


def fold(array):
    parts = [array[:, place : place + LANES] for place in range(0, array.shape[1], LANES)]
    while len(parts) > 1:
        parts = [one + other for one, other in zip(parts[::2], parts[1::2])]
    return parts[0]


def at(array, layers, start):
    return [array[layer, pl.ds(start, SUB), :] for layer in range(layers)]


def stencil(values, after, tx, ty, tz, st, carry, below=None, above=None):
    shape = values[0].shape
    row = tile_ids(0, shape)
    last_z = tile_ids(1, shape) == shape[1] - 1
    results, carries = [], []
    flux_x = None if below is None else below[1] * (below[0] - values[0])
    for layer, value in enumerate(values):
        follow = value if after is None else pltpu.roll(after[layer], SUB - 1, 0)
        follow = jnp.where(row == SUB - 1, follow, pltpu.roll(value, SUB - 1, 0))
        flux_y = ty[layer] * (value - follow)
        rolled = pltpu.roll(flux_y, 1, 0)
        carries.append(rolled)
        flux_z = jnp.where(last_z, 0.0, tz[layer] * (value - pltpu.roll(value, shape[1] - 1, 1)))
        result = st[layer] * value + (flux_y - jnp.where(row == 0, carry[layer], rolled))
        result = result + (flux_z - pltpu.roll(flux_z, 1, 1))
        if flux_x is not None:
            result = result - flux_x
        next_x = values[layer + 1] if layer < len(values) - 1 else above
        flux_x = None
        if next_x is not None:
            flux_x = tx[layer] * (value - next_x)
            result = result + flux_x
        results.append(result)
    return results, carries


def at_last_block():
    return lax.axis_index("blk") == lax.axis_size("blk") - 1


def edge_terms(before, first, last, beyond, ty_before, ty_last):
    low = ty_before * (first - before)
    high = jnp.where(at_last_block(), 0.0, ty_last * (last - beyond))
    return low, high


def pack_kernel(b_hbm, ty_hbm, face, sems):
    rows = b_hbm.shape[1]
    copies = [
        pltpu.make_async_copy(b_hbm.at[0], face.at[pl.ds(0, rows), :], sems.at[0]),
        pltpu.make_async_copy(ty_hbm.at[0, pl.ds(rows - SUB, SUB), :], face.at[pl.ds(rows, SUB), :], sems.at[1]),
    ]
    for copy in copies:
        copy.start()
    for copy in copies:
        copy.wait()


def two_parts(array):
    high = array.astype(BF16)
    return high, (array - high.astype(F32)).astype(BF16)


def prepare_pairs(perm, kind, count, proj, rows, groups, picks, puts, codes, code_row, proj_t, proj_n):
    kinds, width, _ = proj.shape
    blocks = rows * groups
    lane = tile_ids(1, (1, blocks))
    target = lax.rem(perm, groups) * rows + lax.div(perm, groups)
    shift = kinds.bit_length()
    keys = (target * (1 << shift) + jnp.where(lane < count, kind, kinds)).astype(F32)
    span = LANES // groups
    spread = tile_ids(1, (span, LANES)) - groups * tile_ids(0, (span, LANES))
    lanes = tile_ids(1, (rows, LANES))
    across = []
    for group in range(groups):
        column = jnp.concatenate(
            [
                jnp.sum(jnp.where(spread == group, keys[:, place * LANES : (place + 1) * LANES], 0.0), 1, keepdims=True)
                for place in range(blocks // LANES)
            ],
            axis=0,
        ).astype(jnp.int32)
        column = jnp.broadcast_to(column, (rows, LANES))
        here = pl.ds(group * rows, rows)
        for place in range(rows // LANES):
            turned = jnp.transpose(column[place * LANES : (place + 1) * LANES].astype(F32))
            across.append(turned[0:1, :].astype(jnp.int32))
        codes[here, :] = column & ((1 << shift) - 1)
        column = column >> shift
        for place in range(blocks // LANES):
            picks[here, pl.ds(place * LANES, LANES)] = jnp.where(column == lanes + place * LANES, 1.0, 0.0).astype(BF16)
    across = jnp.concatenate(across, axis=1)
    code_row[...] = (kinds - (across & ((1 << shift) - 1))).astype(F32)
    across = across >> shift
    down = tile_ids(0, (rows, blocks))
    for group in range(groups):
        puts[pl.ds(group * rows, rows), :] = jnp.where(across == down + group * rows, 1.0, 0.0).astype(BF16)
    for kind in range(kinds):
        here = pl.ds(kind * width, width)
        proj_t[here, :] = jnp.concatenate(two_parts(jnp.transpose(proj[kind])), axis=1)
        proj_n[here, :] = jnp.concatenate(two_parts(proj[kind]), axis=1)


def first_kernel(
    count, perm, kind, proj, b_hbm, tx_hbm, ty_hbm, tz_hbm, st_hbm,
    b, tx, ty, tz, st, face_next, s_first, s_mid, s_last, sums, picks, puts, codes, code_row, proj_t, proj_n, total, sems,
):
    layers, rows, depth = b.shape
    steps = rows // ROWS
    sources, targets = (b_hbm, tx_hbm, ty_hbm, tz_hbm, st_hbm), (b, tx, ty, tz, st)

    def copy(which, step):
        part = pl.ds(step * ROWS, ROWS)
        return pltpu.make_async_copy(
            sources[which].at[:, part, :], targets[which].at[:, part, :], sems.at[which, step]
        )

    for step in range(steps):
        for which in range(len(sources)):
            copy(which, step).start()
    width = proj.shape[1]
    prepare_pairs(
        perm[0], kind[0], count[0, 0], proj, rows, depth // width, picks, puts, codes, code_row, proj_t, proj_n
    )
    total[...] = jnp.zeros_like(total)
    copy(0, 0).wait()

    def chunk(start, after, carry):
        values = at(b, layers, start)
        results, carry = stencil(values, after, *[at(array, layers, start) for array in (tx, ty, tz, st)], carry)
        here = pl.ds(start, SUB)
        squares, products = values[0] * values[0], values[0] * results[0]
        for layer in range(1, layers):
            squares = squares + values[layer] * values[layer]
            products = products + values[layer] * results[layer]
        total[0] += fold(squares)
        total[1] += fold(products)
        face_next[here, :] = results[0]
        s_first[here, :] = results[0]
        for layer in range(1, layers - 1):
            s_mid[layer - 1, here, :] = results[layer]
        s_last[here, :] = results[layers - 1]
        return carry

    carry = [jnp.zeros((SUB, depth), F32)] * layers
    for step in range(steps):
        for which in range(1, len(sources)):
            copy(which, step).wait()
        if step < steps - 1:
            copy(0, step + 1).wait()
        for start in range(step * ROWS, (step + 1) * ROWS, SUB):
            carry = chunk(start, None if start == rows - SUB else at(b, layers, start + SUB), carry)
    sums[...] = as_tile([jnp.sum(total[0]), jnp.sum(total[1])])


def up_places(layers):
    return 0, layers, 2 * layers, 3 * layers, 3 * layers + 1, 3 * layers + 2


def edge_kernel(
    sums_in, near_sums, b, right, up, down, tx, ty, tz, st, s_first_in, s_mid_in, s_last_in, w_last_in, image_low_in,
    s_first, s_mid, s_last, w_last, image_low, sums, image_ends, ends_sums, right_edges, missing, w_up, w_down,
):
    layers, rows, depth = b.shape
    at_b, at_ty, at_w, at_back, at_right, at_right_ty = up_places(layers)
    product = 0.0
    for layer in range(layers):
        first, last = b[layer, 0:1, :], b[layer, rows - 1 :, :]
        low, high = edge_terms(
            up[at_b + layer : at_b + layer + 1, :], first, last, down[layer : layer + 1, :],
            up[at_ty + layer : at_ty + layer + 1, :], ty[layer, rows - 1 :, :],
        )
        pairs = [(s_first_in, s_first)] if layer == 0 else [(s_last_in, s_last), (w_last_in, w_last)]
        if 0 < layer < layers - 1:
            pairs = [(s_mid_in.at[layer - 1], s_mid.at[layer - 1])]
        for source, target in pairs:
            target[0:1, :] = source[0:1, :] + low
            target[rows - 1 :, :] = source[rows - 1 :, :] + high
        product = product + first * low + last * high
        w_up[layer : layer + 1, :] = up[at_w + layer : at_w + layer + 1, :] - low
        w_down[layer : layer + 1, :] = down[layers + layer : layers + layer + 1, :] - high
    sums[...] = sums_in[...] + as_tile([0.0, jnp.sum(product)])
    low, high = edge_terms(
        up[at_right : at_right + 1, :], right[0:1, :], right[rows - 1 : rows, :], down[2 * layers + 1 :, :],
        up[at_right_ty : at_right_ty + 1, :], right[rows + SUB - 1 :, :],
    )
    right_edges[0:1, :] = low
    right_edges[1:2, :] = high
    missing[0:1, :] = -up[at_right_ty : at_right_ty + 1, :] * up[at_back : at_back + 1, :]
    missing[1:2, :] = jnp.where(
        at_last_block(), 0.0, -right[rows + SUB - 1 :, :] * down[2 * layers : 2 * layers + 1, :]
    )
    near = from_tile(near_sums[...], 2)
    own, read, plain = high_layers(layers, s_mid, s_last, w_last)
    terms = None
    for place, start in enumerate((0, rows - SUB)):
        values = read(start)
        if place == 0:
            after, carry = read(SUB), [jnp.zeros((SUB, depth), F32)] * len(own)
        else:
            after, carry = None, flux_from(start - SUB, own, read, 1, ty)
        new, _ = chunk_sums(
            start, values, after, carry, own, near, b, plain, tx, ty, tz, st, image_ends, place * SUB
        )
        terms = new if terms is None else [old + more for old, more in zip(terms, new)]
    ends_sums[...] = as_tile([0.0] * 3 + [jnp.sum(term) for term in terms])
    own, read = low_layers(layers, s_first, s_mid)
    zero = [jnp.zeros((SUB, depth), F32)] * len(own)
    low_chunk(0, read(0), read(SUB), zero, own, tx, ty, tz, st, image_low)
    carry = flux_from(rows - 2 * SUB, own, read, 0, ty)
    low_chunk(rows - SUB, read(rows - SUB), None, carry, own, tx, ty, tz, st, image_low)


def high_layers(layers, s_mid, s_last, w_last):
    split = layers // 2

    def read(start):
        here = pl.ds(start, SUB)
        return [s_mid[layer - 1, here, :] for layer in range(split - 1, layers - 1)] + [w_last[here, :]]

    def plain(layer, here):
        return s_last[here, :] if layer == layers - 1 else s_mid[layer - 1, here, :]

    return list(range(split, layers)), read, plain


def flux_from(start, own, read, skip, ty):
    row = None
    carry = []
    for layer, value, after in zip(own, read(start)[skip:], read(start + SUB)[skip:]):
        row = tile_ids(0, value.shape)
        follow = jnp.where(row == SUB - 1, pltpu.roll(after, SUB - 1, 0), pltpu.roll(value, SUB - 1, 0))
        carry.append(pltpu.roll(ty[layer, pl.ds(start, SUB), :] * (value - follow), 1, 0))
    return carry


def chunk_sums(start, values, after, carry, own, near, b, plain, tx, ty, tz, st, image, target, summed=None):
    layers = b.shape[0]
    here = pl.ds(start, SUB)
    below = (values[0], tx[own[0] - 1, here, :]) if own[0] > 0 else None
    above = values[-1] if own[-1] < layers - 1 else None
    skip = 0 if below is None else 1
    mine = values[skip : skip + len(own)]
    results, carry = stencil(
        mine, None if after is None else after[skip : skip + len(own)],
        *[[array[layer, here, :] for layer in own] for array in (tx, ty, tz, st)], carry, below, above,
    )
    terms = None
    for place, layer in enumerate(own):
        w, s = mine[place], results[place]
        image[place, pl.ds(target, SUB), :] = s
        if summed is not None and layer not in summed:
            continue
        u = b[layer, here, :] - near * w
        q = plain(layer, here) - near * s
        new = [fold(term) for term in (u * u, u * w, w * w, u * q, u * s + w * q, w * s)]
        terms = new if terms is None else [old + more for old, more in zip(terms, new)]
    return terms, carry


def mm(left, right):
    return lax.dot_general(left, right, (((1,), (0,)), ((), ())), preferred_element_type=F32)


def by_kind(codes, array, kinds):
    zero = jnp.zeros_like(array)
    return jnp.concatenate([jnp.where(codes == kind, array, zero) for kind in range(kinds)], axis=1)


def apply_proj(codes, high, low, proj, kinds, width):
    both = mm(by_kind(codes, high, kinds), proj[...])
    return both[:, :width] + both[:, width:] + mm(by_kind(codes, low, kinds), proj[:, :width])


def take_jump(group, faces, last, picks, codes_col, proj_t):
    width = proj_t.shape[1] // 2
    kinds = proj_t.shape[0] // width
    here = pl.ds(group * last.shape[0], last.shape[0])
    codes = codes_col[here, :]
    taken = mm(picks[here, :], faces)
    projected = apply_proj(codes, taken[:, :width].astype(BF16), taken[:, width:].astype(BF16), proj_t, kinds, width)
    return jnp.where(codes < kinds, last - projected, 0.0)


def turn_back(group, jump, codes_col, proj_n):
    width = proj_n.shape[1] // 2
    kinds = proj_n.shape[0] // width
    scale = jnp.where(lax.axis_index("sub") < lax.axis_size("sub") - 1, -penalty, 0.0)
    codes = codes_col[pl.ds(group * jump.shape[0], jump.shape[0]), :]
    return jnp.concatenate(two_parts(scale * apply_proj(codes, *two_parts(jump), proj_n, kinds, width)), axis=1)


def put_back(group, backs, puts, rows):
    width = backs.shape[1] // 2
    placed = mm(puts[pl.ds(group * rows, rows), :], backs)
    return placed[:, :width] + placed[:, width:]


def stack_parts(parts):
    return jnp.concatenate(two_parts(jnp.concatenate(parts, axis=0)), axis=1)


def jump_first_kernel(earlier, b, right, s_last, picks, codes, proj_t, w_last, jump_face, sums):
    width = proj_t.shape[1] // 2
    layers, rows, depth = b.shape
    parts = [pl.ds(group * width, width) for group in range(depth // width)]
    faces = stack_parts([right[:rows, part] for part in parts])
    square = jnp.zeros((rows, width), F32)
    for group, part in enumerate(parts):
        jump = take_jump(group, faces, b[layers - 1, :, part], picks, codes, proj_t)
        square = square + jump * jump
        jump_face[:, part] = jump
        w_last[:, part] = s_last[:, part] + penalty * jump
    sums[...] = as_tile([jnp.sum(square)])


def kinds_kernel(code_row, picks, proj_t, proj_n, kinds_by_block, squares):
    width = proj_t.shape[1] // 2
    for kind in range(proj_t.shape[0] // width):
        here = pl.ds(kind * width, width)
        left, right = proj_t[here, :], proj_n[here, :]
        both = mm(left[:, :width], right)
        square = both[:, :width] + both[:, width:] + mm(left[:, width:], right[:, :width])
        squares[here, :] = jnp.concatenate(two_parts(square), axis=1)
    depth = kinds_by_block.shape[1]
    row = mm(jnp.broadcast_to(code_row[...], (2 * SUB, code_row.shape[1])).astype(BF16), picks[...])
    kinds_by_block[...] = jnp.zeros_like(kinds_by_block)
    for place in range(row.shape[1] // depth):
        kinds_by_block[place : place + 1, :] = row[0:1, place * depth : (place + 1) * depth]


def rows_kernel(right, b, ty, s_first, s_mid, w_last, back, up, down):
    layers, rows, _ = b.shape
    at_b, at_ty, at_w, at_back, at_right, at_right_ty = up_places(layers)
    end = pl.ds(rows - 1, 1)
    for layer in range(layers):
        image = s_first if layer == 0 else w_last if layer == layers - 1 else s_mid.at[layer - 1]
        up[at_b + layer : at_b + layer + 1, :] = b[layer, end, :]
        up[at_ty + layer : at_ty + layer + 1, :] = ty[layer, end, :]
        up[at_w + layer : at_w + layer + 1, :] = image[end, :]
        down[layer : layer + 1, :] = b[layer, 0:1, :]
        down[layers + layer : layers + layer + 1, :] = image[0:1, :]
    up[at_back : at_back + 1, :] = back[end, :]
    up[at_right : at_right + 1, :] = right[end, :]
    up[at_right_ty : at_right_ty + 1, :] = right[rows + SUB - 1 :, :]
    down[2 * layers : 2 * layers + 1, :] = back[0:1, :]
    down[2 * layers + 1 : 2 * layers + 2, :] = right[0:1, :]


def jump_second_kernel(
    near_sums, w_last, jump, right_before, right, right_edges, back_before, missing, picks, codes, proj_t,
    jump_next, sums, field,
):
    width = proj_t.shape[1] // 2
    rows, depth = right.shape
    parts = [pl.ds(group * width, width) for group in range(depth // width)]
    near = from_tile(near_sums[...], 2)
    field[...] = right[...] + back_before[:rows, :]
    field[0:1, :] += right_edges[0:1, :]
    field[rows - 1 :, :] += right_edges[1:2, :]
    faces = stack_parts([field[:, part] for part in parts])
    totals = [jnp.zeros((rows, width), F32)] * 3
    for group, part in enumerate(parts):
        later = take_jump(group, faces, w_last[:, part], picks, codes, proj_t)
        jump_next[:, part] = later
        close = jump[:, part] - near * later
        totals = [total + new for total, new in zip(totals, (close * close, close * later, later * later))]
    found = [jnp.sum(total) for total in totals]
    found = [penalty * found[0], 2.0 * penalty * found[1], penalty * found[2]]
    extra = [0.0] * 3
    for side, place in enumerate((0, rows - 1)):
        s = missing[side : side + 1, :]
        w = field[place : place + 1, :]
        u = right_before[place : place + 1, :] - near * w
        extra = [old + more for old, more in zip(extra, [-near * u * s, u * s - near * w * s, w * s])]
    sums[...] = as_tile([0.0] * 6 + [old + jnp.sum(more) for old, more in zip(found, extra)])


def back_first_kernel(jump, kinds_by_block, puts, codes, proj_n, back):
    rows = jump.shape[0]
    back_kernel(jump, puts, codes, proj_n, back)
    back[rows:, :] = kinds_by_block[...]


def back_second_kernel(w_last, missing, puts, codes, proj_n, back):
    rows = w_last.shape[0]
    back_kernel(w_last, puts, codes, proj_n, back)
    back[rows : rows + 2, :] = missing[...]


def own_second_kernel(s_first, recv, squares, own):
    rows, depth = own.shape
    width = squares.shape[1] // 2
    kinds = squares.shape[0] // width
    for group in range(depth // width):
        part = pl.ds(group * width, width)
        codes = []
        for place in range(rows // LANES):
            start = group * rows + place * LANES
            row = recv[rows + start // depth : rows + start // depth + 1, start % depth : start % depth + LANES]
            codes.append(jnp.transpose(jnp.broadcast_to(row, (LANES, LANES))))
        codes = kinds - jnp.concatenate(codes, axis=0).astype(jnp.int32)
        field = s_first[:, part] + recv[:rows, part]
        own[:, part] = penalty * apply_proj(codes, *two_parts(field), squares, kinds, width)


def hold_kernel(later, much_later, back_in, back):
    back[back.shape[0] - SUB + 2 :, :] = jnp.zeros((SUB - 2, back.shape[1]), F32)


def back_kernel(jump_next, puts, codes, proj_n, back):
    width = proj_n.shape[1] // 2
    rows, depth = jump_next.shape
    parts = [pl.ds(group * width, width) for group in range(depth // width)]
    backs = [turn_back(group, jump_next[:, part], codes, proj_n) for group, part in enumerate(parts)]
    backs = jnp.concatenate(backs, axis=0)
    for group, part in enumerate(parts):
        back[:rows, part] = put_back(group, backs, puts, rows)


def stencil_sums(read, own, near, b, plain, tx, ty, tz, st, image, total, inner, summed=None):
    layers, rows, depth = b.shape
    total[...] = jnp.zeros_like(total)
    skip = 1 if own[0] > 0 else 0

    def several(start, count, carry, at_end=False):
        starts = [pl.multiple_of(start + SUB * place, SUB) for place in range(count + 1)]
        values = [read(place) for place in starts[:-1]] + [None if at_end else read(starts[-1])]
        terms = None
        for place in range(count):
            new, carry = chunk_sums(
                starts[place], values[place], values[place + 1], carry, own, near, b, plain, tx, ty, tz, st, image,
                starts[place], summed,
            )
            terms = new if terms is None else [old + more for old, more in zip(terms, new)]
        for place, term in enumerate(terms):
            total[place] += term
        return carry

    group = 2
    if inner:
        begin, count, carry = SUB, (rows // SUB - 2) // group, flux_from(0, own, read, skip, ty)
    else:
        begin, count, carry = 0, rows // (group * SUB) - 1, [jnp.zeros((SUB, depth), F32)] * len(own)
    carry = lax.fori_loop(
        0, count,
        lambda index, carry: tuple(
            several(pl.multiple_of(begin + index * group * SUB, SUB), group, list(carry))
        ),
        tuple(carry),
    )
    if not inner:
        several(rows - group * SUB, group, list(carry), True)
    return [jnp.sum(total[place]) for place in range(total.shape[0])]


def second_high_kernel(later, first_sums, jump_sums, b, s_mid, s_last, w_last, tx, ty, tz, st, image, sums, total):
    norm = from_tile(first_sums[...], 0)
    energy = from_tile(first_sums[...], 1) + penalty * from_tile(jump_sums[...], 0)
    safe = energy > 0.01 * norm
    ratio = jnp.full((SUB, LANES), norm, F32) / jnp.full((SUB, LANES), jnp.where(safe, energy, 1.0), F32)
    near = jnp.where(safe, jnp.max(ratio), 0.0)
    own, read, plain = high_layers(b.shape[0], s_mid, s_last, w_last)
    found = stencil_sums(read, own, near, b, plain, tx, ty, tz, st, image, total, True)
    sums[...] = as_tile([0.0, 0.0, near] + found)


def low_layers(layers, s_first, s_mid):
    split = layers // 2

    def read(start):
        here = pl.ds(start, SUB)
        return [s_first[here, :]] + [s_mid[layer - 1, here, :] for layer in range(1, split + 1)]

    return list(range(split)), read


def low_chunk(start, values, after, carry, own, tx, ty, tz, st, image):
    here = pl.ds(start, SUB)
    results, carry = stencil(
        values[:-1], None if after is None else after[:-1],
        *[[array[layer, here, :] for layer in own] for array in (tx, ty, tz, st)], carry, None, values[-1],
    )
    for layer in own:
        image[layer, here, :] = results[layer]
    return carry


def second_low_kernel(s_first, s_mid, tx, ty, tz, st, image):
    layers, rows = tx.shape[:2]
    own, read = low_layers(layers, s_first, s_mid)
    group = 3

    def several(index, carry):
        start = pl.multiple_of(SUB + index * group * SUB, SUB)
        starts = [pl.multiple_of(start + SUB * place, SUB) for place in range(group + 1)]
        values = [read(place) for place in starts]
        carry = list(carry)
        for place in range(group):
            carry = low_chunk(starts[place], values[place], values[place + 1], carry, own, tx, ty, tz, st, image)
        return tuple(carry)

    lax.fori_loop(0, (rows // SUB - 2) // group, several, tuple(flux_from(0, own, read, 0, ty)))


def second_added_kernel(
    first_sums, jump_sums, high_sums, ends_sums, second_sums, b, s_first, s_mid, w_last, recv,
    w_up, w_down, up, tx, ty, tz, st, image_in, image, edge_high, table, total,
):
    layers, rows, depth = b.shape
    split = layers // 2
    near = from_tile(high_sums[...], 2)
    total[...] = jnp.zeros_like(total)
    first, second = 0, 1

    def several(start, count, carry, at_end=False):
        starts = [pl.multiple_of(start + SUB * place, SUB) for place in range(count + 1)]
        added = [recv[pl.ds(place, SUB), :] for place in starts[:-1]]
        added.append(None if at_end else recv[pl.ds(starts[-1], SUB), :])
        terms = None
        for place in range(count):
            here = pl.ds(starts[place], SUB)
            e, t_x = added[place], tx[first, here, :]
            (s,), carry = stencil(
                [e], None if added[place + 1] is None else [added[place + 1]], [t_x], [ty[first, here, :]],
                [tz[first, here, :]], [st[first, here, :] + t_x], carry,
            )
            s = image_in[first, here, :] + s
            image[first, here, :] = s
            plain = s_first[here, :]
            w = plain + e
            u = b[first, here, :] - near * w
            q = plain - near * s
            new = [u * u, u * w, w * w, u * q, u * s + w * q, w * s]
            s = image_in[second, here, :] - t_x * e
            image[second, here, :] = s
            w = s_mid[second - 1, here, :]
            u = b[second, here, :] - near * w
            q = w - near * s
            more = [u * u, u * w, w * w, u * q, u * s + w * q, w * s]
            new = [fold(one + other) for one, other in zip(new, more)]
            terms = new if terms is None else [old + more for old, more in zip(terms, new)]
        for place, term in enumerate(terms):
            total[place] += term
        return carry

    group = 4
    carry = lax.fori_loop(
        0, rows // (group * SUB) - 1,
        lambda index, carry: several(pl.multiple_of(index * group * SUB, SUB), group, [carry])[0],
        jnp.zeros((SUB, depth), F32),
    )
    several(rows - group * SUB, group, [carry], True)
    found = [jnp.sum(total[place]) for place in range(total.shape[0])]

    def row(layer, place):
        here = pl.ds(place, 1)
        if layer == 0:
            return s_first[here, :] + recv[here, :]
        return w_last[here, :] if layer == layers - 1 else s_mid[layer - 1, here, :]

    extra = [jnp.zeros((1, depth), F32)] * 3
    for layer in range(layers):
        ends = row(layer, 0), row(layer, rows - 1)
        added = edge_terms(
            w_up[layer : layer + 1, :], *ends, w_down[layer : layer + 1, :],
            up[layers + layer : layers + layer + 1, :], ty[layer, rows - 1 :, :],
        )
        for side, (place, w, s) in enumerate(zip((0, rows - 1), ends, added)):
            u = b[layer, place : place + 1, :] - near * w
            extra = [old + more for old, more in zip(extra, [-near * u * s, u * s - near * w * s, w * s])]
            if layer < split:
                image[layer, place : place + 1, :] += s
            else:
                spot = side * (layers - split) + layer - split
                edge_high[spot : spot + 1, :] = s
    found[3:] = [old + jnp.sum(more) for old, more in zip(found[3:], extra)]
    norm = from_tile(first_sums[...], 0)
    energy = from_tile(first_sums[...], 1) + penalty * from_tile(jump_sums[...], 0)
    sums = high_sums[...] + ends_sums[...] + second_sums[...]
    sums = sums + as_tile([norm, energy, 0.0] + found)
    mine = lax.axis_index("sub") * lax.axis_size("blk") + lax.axis_index("blk")
    device = tile_ids(0, table.shape) * (LANES // FIELDS) + lax.div(tile_ids(1, table.shape), FIELDS)
    field = lax.rem(tile_ids(1, table.shape), FIELDS)
    filled = jnp.zeros(table.shape, F32)
    for place in range(9):
        filled = jnp.where((device == mine) & (field == place), jnp.sum(sums[0:1, place : place + 1]), filled)
    table[...] = filled


def add_kernel(earlier, one, other, both):
    both[...] = one[...] + other[...]


def final_kernel(
    tables, b, s_first, s_mid, w_last, recv, image_low, image_high, image_ends, edge_high, jump_next, recv_next, own_next, solution_hbm, residual_hbm,
    solution, residual, sems,
):
    layers, rows, depth = b.shape
    split = image_low.shape[0]
    flat = tables[...]
    norm, energy, near, uu, uw, ww, uq, cross, wq = [
        flat if place == 0 else pltpu.roll(flat, LANES - place, 1) for place in range(9)
    ]
    own = lax.rem(tile_ids(1, flat.shape), FIELDS) == 0

    def whole(array):
        array = jnp.sum(jnp.where(own, array, 0.0), axis=0, keepdims=True)
        return jnp.sum(array, axis=1, keepdims=True)

    norm, energy = whole(norm), whole(energy)
    alpha = norm / energy
    away = alpha - near
    norm_next = whole(uu - away * (2.0 * uw - away * ww))
    energy_next = whole(uq - away * (cross - away * wq))
    beta = norm_next / norm
    step_size = norm_next / (energy_next - beta * norm_next / alpha)
    c0 = jnp.broadcast_to(alpha + step_size * beta + step_size, (SUB, depth))
    c1 = jnp.broadcast_to(step_size * alpha, (SUB, depth))
    c2 = jnp.broadcast_to(alpha + step_size * (1.0 + beta), (SUB, depth))

    def copy(which, step):
        part = pl.ds(step * ROWS, ROWS)
        source, target = ((solution, solution_hbm), (residual, residual_hbm))[which]
        return pltpu.make_async_copy(source.at[:, part, :], target.at[:, part, :], sems.at[which, step])

    for step in range(rows // ROWS):
        for start in range(step * ROWS, (step + 1) * ROWS, SUB):
            here = pl.ds(start, SUB)
            for layer in range(layers):
                v = b[layer, here, :]
                if layer < split:
                    s = image_low[layer, here, :]
                elif start == 0:
                    s = image_ends[layer - split, :SUB, :]
                elif start == rows - SUB:
                    s = image_ends[layer - split, SUB:, :]
                else:
                    s = image_high[layer - split, here, :]
                if layer == 0:
                    w = s_first[here, :] + recv[here, :]
                    s = s + (recv_next[here, :] + own_next[here, :])
                elif layer < layers - 1:
                    w = s_mid[layer - 1, here, :]
                else:
                    w = w_last[here, :]
                    s = s + penalty * jump_next[here, :]
                solution[layer, here, :] = c0 * v - c1 * w
                residual[layer, here, :] = v - c2 * w + c1 * s
        for side, last_step in enumerate((0, rows // ROWS - 1)):
            if step == last_step:
                place = side * (rows - 1)
                residual[0, place : place + 1, :] += c1[0:1, :] * recv_next[rows + side : rows + side + 1, :]
                for layer in range(split, layers):
                    spot = side * (layers - split) + layer - split
                    residual[layer, place : place + 1, :] += c1[0:1, :] * edge_high[spot : spot + 1, :]
        for which in range(2):
            copy(which, step).start()
    for step in range(rows // ROWS):
        for which in range(2):
            copy(which, step).wait()


SMEM = pl.BlockSpec(memory_space=pltpu.SMEM)
VMEM = pl.BlockSpec(memory_space=pltpu.VMEM)
HBM = pl.BlockSpec(memory_space=pltpu.HBM)


def held(*dims, dtype=F32):
    return pltpu.VMEM(dims, dtype)


def near_core(*arrays):
    return [pltpu.with_memory_space_constraint(array, pltpu.VMEM) for array in arrays]


def in_hbm(*arrays):
    return [pltpu.with_memory_space_constraint(array, pltpu.HBM) for array in arrays]


def cost(flops, size):
    return pl.CostEstimate(flops=int(flops), bytes_accessed=int(size), transcendentals=0)


def scaled(estimate, by):
    return pl.CostEstimate(
        flops=int(estimate.flops * by) + 1, bytes_accessed=int(estimate.bytes_accessed * by) + 1, transcendentals=0
    )


def params(mib):
    return pltpu.CompilerParams(vmem_limit_bytes=mib * 1024 * 1024)


def shifted(array, axis, by):
    size = lax.axis_size(axis)
    return lax.ppermute(array, axis, [(i, i + by) for i in range(size) if 0 <= i + by < size])


def gather_rows(table, own):
    subs, blks = lax.axis_size("sub"), lax.axis_size("blk")
    steps = [(0, 1)]
    reach = 2
    while reach < blks:
        steps.append((0, reach + 1))
        reach *= 2
    reach = subs // 2
    while reach > 0:
        steps.append((reach, 1))
        reach //= 2
    for place, (by_sub, by_blk) in enumerate(steps):
        pairs = [(s * blks + t, (s ^ by_sub) * blks + (t ^ by_blk)) for s in range(subs) for t in range(blks)]
        other = lax.ppermute(table, ("sub", "blk"), pairs)
        if place == 0:
            (table,) = pl.pallas_call(
                add_kernel,
                in_specs=[VMEM] * 3,
                out_specs=[VMEM],
                out_shape=[held(*table.shape)],
                compiler_params=params(2),
                cost_estimate=scaled(cost(table.size, 12 * table.size), 0.03),
                name="add",
            )(*near_core(own, table, other))
        else:
            table = table + other
    return table


def body(right_side, trans_x, trans_y, trans_z, storage, pair_perm, pair_type, pair_count, proj):
    layers, rows, depth = right_side.shape
    blocks, width, kinds = pair_perm.shape[2], proj.shape[1], proj.shape[0]
    subs, blks = lax.axis_size("sub"), lax.axis_size("blk")
    steps = rows // ROWS
    cells = layers * rows * depth

    (face,) = pl.pallas_call(
        pack_kernel,
        in_specs=[HBM, HBM],
        out_specs=[VMEM],
        out_shape=[held(rows + SUB, depth)],
        scratch_shapes=[pltpu.SemaphoreType.DMA((2,))],
        compiler_params=params(2),
        cost_estimate=scaled(cost(0, 4 * rows * depth), 100),
        name="pack",
    )(*in_hbm(right_side, trans_y))
    face_right = shifted(face, "sub", -1)

    b, tx, ty, tz, st, face_next, s_first, s_mid, s_last, first_sums, picks, puts, codes, code_row, proj_t, proj_n = pl.pallas_call(
        first_kernel,
        in_specs=[SMEM] + [VMEM] * 3 + [HBM] * 5,
        out_specs=[VMEM] * 16,
        out_shape=[held(layers, rows, depth)] * 5
        + [
            held(rows, depth), held(rows, depth), held(layers - 2, rows, depth), held(rows, depth), held(SUB, LANES),
            held(blocks, blocks, dtype=BF16), held(blocks, blocks, dtype=BF16), held(blocks, width, dtype=jnp.int32), held(1, blocks),
            held(kinds * width, 2 * width, dtype=BF16), held(kinds * width, 2 * width, dtype=BF16),
        ],
        scratch_shapes=[pltpu.VMEM((2, SUB, LANES), F32), pltpu.SemaphoreType.DMA((5, steps))],
        compiler_params=params(16),
        cost_estimate=scaled(cost(20 * cells, 24 * cells), 4),
        name="stencil_first",
    )(
        pair_count, pair_perm, pair_type, proj,
        *in_hbm(right_side, trans_x, trans_y, trans_z, storage),
    )
    face_right_next = shifted(face_next, "sub", -1)

    split = layers // 2
    (image_low,) = pl.pallas_call(
        second_low_kernel,
        in_specs=[VMEM] * 6,
        out_specs=[VMEM],
        out_shape=[held(split, rows, depth)],
        compiler_params=params(8),
        cost_estimate=scaled(cost(20 * cells, 15 * cells), 20),
        name="stencil_second_low",
    )(*near_core(s_first, s_mid, tx, ty, tz, st))

    mortar_cost = cost(4 * blocks * blocks * width + 6 * kinds * blocks * width * width, 14 * rows * depth)
    w_last, jump, jump_sums = pl.pallas_call(
        jump_first_kernel,
        in_specs=[VMEM] * 7,
        out_specs=[VMEM] * 3,
        out_shape=[held(rows, depth), held(rows, depth), held(SUB, LANES)],
        compiler_params=params(16),
        cost_estimate=scaled(mortar_cost, 0.3),
        name="jump_first",
    )(*near_core(image_low, b, face_right, s_last, picks, codes, proj_t))
    kinds_by_block, squares = pl.pallas_call(
        kinds_kernel,
        in_specs=[VMEM] * 4,
        out_specs=[VMEM] * 2,
        out_shape=[held(SUB, depth), held(kinds * width, 2 * width, dtype=BF16)],
        compiler_params=params(8),
        cost_estimate=scaled(cost(16 * blocks * blocks, 2 * blocks * blocks), 20),
        name="kinds",
    )(*near_core(code_row, picks, proj_t, proj_n))
    (back,) = pl.pallas_call(
        back_first_kernel,
        in_specs=[VMEM] * 5,
        out_specs=[VMEM],
        out_shape=[held(rows + SUB, depth)],
        compiler_params=params(16),
        cost_estimate=scaled(mortar_cost, 20),
        name="back_first",
    )(*near_core(jump, kinds_by_block, puts, codes, proj_n))
    recv = shifted(back, "sub", 1)

    split = layers // 2
    image_high, high_sums = pl.pallas_call(
        second_high_kernel,
        in_specs=[VMEM] * 11,
        out_specs=[VMEM] * 2,
        out_shape=[held(layers - split, rows, depth), held(SUB, LANES)],
        scratch_shapes=[pltpu.VMEM((6, SUB, LANES), F32)],
        compiler_params=params(8),
        cost_estimate=scaled(cost(20 * cells, 15 * cells), 1),
        name="stencil_second_high",
    )(*near_core(back, first_sums, jump_sums, b, s_mid, s_last, w_last, tx, ty, tz, st))
    up_out, down_out = pl.pallas_call(
        rows_kernel,
        in_specs=[VMEM] * 7,
        out_specs=[VMEM] * 2,
        out_shape=[held(3 * layers + 3, depth), held(2 * layers + 2, depth)],
        compiler_params=params(2),
        cost_estimate=scaled(cost(0, 64 * depth), 4),
        name="rows",
    )(*near_core(face_right, b, ty, s_first, s_mid, w_last, back))
    up = shifted(up_out, "blk", 1)
    down = shifted(down_out, "blk", -1)
    s_first, s_mid, s_last, w_last, image_low, edge_sums, image_ends, ends_sums, right_edges, missing, w_up, w_down = pl.pallas_call(
        edge_kernel,
        in_specs=[VMEM] * 15,
        out_specs=[VMEM] * 12,
        out_shape=[held(rows, depth), held(layers - 2, rows, depth), held(rows, depth), held(rows, depth)]
        + [held(split, rows, depth), held(SUB, LANES), held(layers - split, 2 * SUB, depth), held(SUB, LANES)]
        + [held(2, depth), held(2, depth), held(layers, depth), held(layers, depth)],
        input_output_aliases={10: 0, 11: 1, 12: 2, 13: 3, 14: 4},
        compiler_params=params(4),
        cost_estimate=scaled(cost(320 * depth, 640 * depth), 1),
        name="edges_first",
    )(
        *near_core(
            first_sums, high_sums, b, face_right, up, down, tx, ty, tz, st, s_first, s_mid, s_last, w_last, image_low,
        )
    )

    jump_next, second_sums = pl.pallas_call(
        jump_second_kernel,
        in_specs=[VMEM] * 11,
        out_specs=[VMEM] * 2,
        out_shape=[held(rows, depth), held(SUB, LANES)],
        scratch_shapes=[pltpu.VMEM((rows, depth), F32)],
        compiler_params=params(16),
        cost_estimate=scaled(mortar_cost, 100),
        name="jump_second",
    )(
        *near_core(
            high_sums, w_last, jump, face_right, face_right_next, right_edges, back, missing, picks, codes, proj_t,
        )
    )
    (back_next,) = pl.pallas_call(
        back_second_kernel,
        in_specs=[VMEM] * 5,
        out_specs=[VMEM],
        out_shape=[held(rows + SUB, depth)],
        compiler_params=params(16),
        cost_estimate=scaled(mortar_cost, 20),
        name="back_second",
    )(*near_core(w_last, missing, puts, codes, proj_n))

    (back_next,) = pl.pallas_call(
        hold_kernel,
        in_specs=[VMEM] * 3,
        out_specs=[VMEM],
        out_shape=[held(rows + SUB, depth)],
        input_output_aliases={2: 0},
        compiler_params=params(2),
        cost_estimate=scaled(cost(0, 8 * depth), 20),
        name="hold",
    )(*near_core(second_sums, recv, back_next))
    recv_next = shifted(back_next, "sub", 1)

    count = subs * blks
    image_low, edge_high, table = pl.pallas_call(
        second_added_kernel,
        in_specs=[VMEM] * 18,
        out_specs=[VMEM] * 3,
        out_shape=[
            held(split, rows, depth), held(2 * (layers - split), depth), held(-(-count * FIELDS // LANES), LANES),
        ],
        input_output_aliases={17: 0},
        scratch_shapes=[pltpu.VMEM((6, SUB, LANES), F32)],
        compiler_params=params(8),
        cost_estimate=scaled(cost(20 * cells, 15 * cells), 0.3),
        name="stencil_second_added",
    )(
        *near_core(
            edge_sums, jump_sums, high_sums, ends_sums, second_sums, b, s_first, s_mid, w_last, recv,
            w_up, w_down, up, tx, ty, tz, st, image_low,
        )
    )
    (own_next,) = pl.pallas_call(
        own_second_kernel,
        in_specs=[VMEM] * 3,
        out_specs=[VMEM],
        out_shape=[held(rows, depth)],
        compiler_params=params(16),
        cost_estimate=scaled(mortar_cost, 0.3),
        name="own_second",
    )(*near_core(s_first, recv, squares))
    tables = gather_rows(table, own_next)

    return pl.pallas_call(
        final_kernel,
        in_specs=[VMEM] * 13,
        out_specs=[HBM] * 2,
        out_shape=[jax.ShapeDtypeStruct((layers, rows, depth), F32)] * 2,
        scratch_shapes=[pltpu.VMEM((layers, rows, depth), F32)] * 2 + [pltpu.SemaphoreType.DMA((2, steps))],
        compiler_params=params(8),
        cost_estimate=scaled(cost(8 * cells, 22 * cells), 0),
        name="final_update",
    )(*near_core(tables, b, s_first, s_mid, w_last, recv, image_low, image_high, image_ends, edge_high, jump_next, recv_next, own_next))


def solution(mesh):
    cells = P("sub", "blk", None)
    in_specs = (cells,) * 7 + (P("sub", "blk"), P())
    return jax.shard_map(body, mesh=mesh, in_specs=in_specs, out_specs=(cells, cells), check_vma=False)
```
